32 devices in a mesh: dp: 4 (over z), seq: 2 (over y), tensor: 4 (over x, core).
Axes of the slice: x: 2, y: 2, z: 4, core: 2. Of those that a mesh axis runs over, the one named last changes fastest.
Arguments:
- hidden_in: bfloat16 [8192, 2048], P(('dp', 'seq', 'tensor')), may hold values from -6 to 6
- norm1_gain: bfloat16 [2048], replicated, may hold values from 0.5 to 1.5
- norm1_bias: bfloat16 [2048], replicated, may hold values from -3 to 3
- query_weight: bfloat16 [2048, 2048], P(None, 'tensor'), may hold values from -0.125 to 0.125
- query_bias: bfloat16 [2048], P('tensor'), may hold values from -3 to 3
- key_weight: bfloat16 [2048, 2048], P(None, 'tensor'), may hold values from -0.125 to 0.125
- value_weight: bfloat16 [2048, 2048], P(None, 'tensor'), may hold values from -0.125 to 0.125
- value_bias: bfloat16 [2048], P('tensor'), may hold values from -3 to 3
- out_weight: bfloat16 [2048, 2048], P('tensor'), may hold values from -0.375 to 0.375
- out_bias: bfloat16 [2048], replicated, may hold values from -3 to 3
- norm2_gain: bfloat16 [2048], replicated, may hold values from 0.5 to 1.5
- norm2_bias: bfloat16 [2048], replicated, may hold values from -3 to 3
- up_weight: bfloat16 [2048, 8192], P(None, 'tensor'), may hold values from -0.125 to 0.125
- up_bias: bfloat16 [8192], P('tensor'), may hold values from -3 to 3
- down_weight: bfloat16 [8192, 2048], P('tensor'), may hold values from -0.09375 to 0.09375
- down_bias: bfloat16 [2048], replicated, may hold values from -3 to 3
- seg_lengths: int32 [4, 13], P('dp'), may hold values from 64 to 576, as said below
- parents: int32 [4, 13], P('dp'), may hold values from 0 to 4, as said below
- out_grad: bfloat16 [8192, 2048], P(('dp', 'seq', 'tensor')), may hold values from -6 to 6
Outputs:
- layer_out: bfloat16 [8192, 2048], P(('dp', 'seq', 'tensor'))
- grad_in: bfloat16 [8192, 2048], P(('dp', 'seq', 'tensor'))
- grad_norm1_gain: float32 [2048], replicated
- grad_norm1_bias: float32 [2048], replicated
- grad_query_weight: float32 [2048, 2048], P(None, 'tensor')
- grad_query_bias: float32 [2048], P('tensor')
- grad_key_weight: float32 [2048, 2048], P(None, 'tensor')
- grad_value_weight: float32 [2048, 2048], P(None, 'tensor')
- grad_value_bias: float32 [2048], P('tensor')
- grad_out_weight: float32 [2048, 2048], P('tensor')
- grad_out_bias: float32 [2048], replicated
- grad_norm2_gain: float32 [2048], replicated
- grad_norm2_bias: float32 [2048], replicated
- grad_up_weight: float32 [2048, 8192], P(None, 'tensor')
- grad_up_bias: float32 [8192], P('tensor')
- grad_down_weight: float32 [8192, 2048], P('tensor')
- grad_down_bias: float32 [2048], replicated
The draws below stay inside these ranges and needn't reach their ends.
Inputs may be any that keep to these rules, and one draw needn't show every extreme that they name: `seg_lengths`: in every slot the 13 lengths sum to 2048; segment 0 (the trunk) comes first and is the longest, then the 4 branches, then the leaves. `parents`: entry 0 is 0 and unused; segments 1 to 4 have parent 0; every later segment has a parent among 1 to 4.
All inputs are finite; a program needn't handle non-finite values.
Results may differ from the reference program's by a relative error of at most 0.02.
Values may be sent and summed in bfloat16 or wider, within the bound.
No kernel may reach another device: no remote copies, remote signals or barrier semaphores. Data moves between devices by JAX's collectives and lax.ppermute only.
A program may use at most 384 MiB of HBM per device.

```python
import jax
import jax.numpy as jnp
from jax import lax

D = 2048
HEADS = 32
HD = 64
FF = 8192
SEG = 128
BRANCHES = 4
NSEG = 13
SLOT = 2048
SLOTS = 4
TOKENS = 8192


def draw_seg_lengths(key, part):
    key = jax.random.fold_in(key, 11)
    slot_keys = jax.random.split(key, SLOTS)
    half = SEG // 2

    def one_slot(slot_key):
        pair_key, last_key = jax.random.split(slot_key)
        trunk = jnp.full((1,), 4 * SEG + half, jnp.int32)
        shifts = jax.random.randint(pair_key, (NSEG // 2 - 1,), -half, half + 1).astype(jnp.int32)
        paired = jnp.stack([SEG + shifts, SEG - shifts], axis=1).reshape(-1)
        tail_shift = jax.random.randint(last_key, (), 0, half + 1).astype(jnp.int32)
        tail = jnp.stack([SEG - half + tail_shift, SEG - tail_shift])
        return jnp.concatenate([trunk, paired, tail]).astype(jnp.int32)
    return jax.vmap(one_slot)(slot_keys)


def draw_parents(key, part):
    key = jax.random.fold_in(key, 12)
    leaves = jax.random.randint(key, (SLOTS, NSEG - 1 - BRANCHES), 1, BRANCHES + 1)
    heads = jnp.zeros((SLOTS, 1 + BRANCHES), jnp.int32)
    return jnp.concatenate([heads, leaves.astype(jnp.int32)], axis=1)


def block_scale(stream_key, dims, cuts, least, largest):
    factor_of = 1.0
    for dim, shards_of in cuts:
        draws = jax.random.uniform(jax.random.fold_in(jax.random.fold_in(stream_key, 6), dim), (shards_of,), jnp.float32, least / len(cuts), largest / len(cuts))
        factor_of = factor_of * jnp.repeat(jnp.exp(draws), dims[dim] // shards_of).reshape((-1,) + (1,) * (len(dims) - 1 - dim))
    return factor_of


def noise(own_key, shape, deviation, bound, cuts=(), kind=jnp.bfloat16):
    factor_of = block_scale(own_key, shape, cuts, -0.22, 0.18) if cuts else 1.0
    values = jax.random.normal(own_key, shape, jnp.float32) * deviation * factor_of
    return jnp.minimum(jnp.maximum(values, -bound), bound).astype(kind)


def setup_inputs(seed: int = 0) -> dict:
    seeds = jax.random.split(jax.random.key(seed), 20)
    return {
        "hidden_in": noise(seeds[0], (TOKENS, D), 1.0, 6.0, ((0, 32),)),
        "norm1_gain": jnp.clip(1.0 + 0.1 * jax.random.normal(seeds[1], (D,), jnp.float32), 0.5, 1.5).astype(jnp.bfloat16),
        "norm1_bias": noise(seeds[2], (D,), 0.5, 3.0),
        "query_weight": noise(seeds[3], (D, D), D ** -0.5, 0.125, ((1, 4),)),
        "query_bias": noise(seeds[4], (D,), 0.5, 3.0, ((0, 4),)),
        "key_weight": noise(seeds[5], (D, D), D ** -0.5, 0.125, ((1, 4),)),
        "value_weight": noise(seeds[6], (D, D), D ** -0.5, 0.125, ((1, 4),)),
        "value_bias": noise(seeds[7], (D,), 0.5, 3.0, ((0, 4),)),
        "out_weight": noise(seeds[8], (D, D), (D // 8) ** -0.5, 0.375, ((0, 4),)),
        "out_bias": noise(seeds[9], (D,), 0.5, 3.0),
        "norm2_gain": jnp.clip(1.0 + 0.1 * jax.random.normal(seeds[10], (D,), jnp.float32), 0.5, 1.5).astype(jnp.bfloat16),
        "norm2_bias": noise(seeds[11], (D,), 0.5, 3.0),
        "up_weight": noise(seeds[12], (D, FF), D ** -0.5, 0.125, ((1, 4),)),
        "up_bias": noise(seeds[13], (FF,), 0.5, 3.0, ((0, 4),)),
        "down_weight": noise(seeds[14], (FF, D), (FF // 2) ** -0.5, 0.09375, ((0, 4),)),
        "down_bias": noise(seeds[15], (D,), 0.5, 3.0),
        "seg_lengths": draw_seg_lengths(jax.random.fold_in(seeds[19], 71), 0),
        "parents": draw_parents(jax.random.fold_in(seeds[19], 71), 0),
        "out_grad": noise(seeds[18], (TOKENS, D), 1.0, 6.0, ((0, 32),)),
    }


EPS = 1e-05
NEG = -1e+30
HIGH = lax.Precision.HIGHEST

@jax.custom_vjp
def low(v):
    return lax.optimization_barrier(v.astype(jnp.bfloat16)).astype(jnp.float32)

@jax.custom_vjp
def low_back(v):
    return v

def low_keep(v):
    return (low(v), None)

def low_pass(kept, grad):
    return (grad,)

def back_keep(v):
    return (v, None)

def back_low(kept, grad):
    return (low(grad),)
low.defvjp(low_keep, low_pass)
low_back.defvjp(back_keep, back_low)

def tree_tables(lengths, parent_ids, whole):
    nseg = lengths.shape[0]
    seg_ids = jnp.arange(nseg, dtype=jnp.int32)
    ends = jnp.cumsum(lengths, dtype=jnp.int32)
    starts = ends - lengths
    token = jnp.arange(whole, dtype=jnp.int32)
    segment = lax.optimization_barrier(jnp.sum((token[:, None] >= ends[None, :]).astype(jnp.int32), axis=1, dtype=jnp.int32))
    link = ((parent_ids[:, None] == seg_ids[None, :]) & (seg_ids[:, None] > 0)).astype(jnp.int32)
    identity = (seg_ids[:, None] == seg_ids[None, :]).astype(jnp.int32)
    ancestor = identity
    for _ in range(nseg):
        ancestor = jnp.minimum(identity + lax.optimization_barrier(jnp.sum(link[:, :, None] * ancestor[None, :, :], axis=1, dtype=jnp.int32)), 1)
    path_start = lax.optimization_barrier(jnp.sum((ancestor - identity) * lengths[None, :], axis=1, dtype=jnp.int32))
    onehot = (segment[:, None] == seg_ids[None, :]).astype(jnp.int32)
    depth = token + lax.optimization_barrier(jnp.sum(onehot * (path_start - starts)[None, :], axis=1, dtype=jnp.int32))
    return (onehot.astype(jnp.float32), ancestor.astype(jnp.float32), depth.astype(jnp.float32))

def norm_rows(values, gain, shift):
    center = values - lax.optimization_barrier(jnp.mean(values, axis=-1, keepdims=True))
    variance = lax.optimization_barrier(jnp.mean(center * center, axis=-1, keepdims=True))
    return center * lax.rsqrt(variance + EPS) * gain + shift

def matmul(left, right):
    return jnp.dot(left, right, precision=HIGH, preferred_element_type=jnp.float32)

def layer(params, inputs, onehot, ancestor, depth):
    gain_one, shift_one, query_weight, query_bias, key_weight, value_weight, value_bias, out_weight, out_bias, gain_two, shift_two, up_weight, up_bias, down_weight, down_bias = params
    whole = inputs.shape[0]
    normed = low(norm_rows(inputs, gain_one, shift_one))
    queries = low(low_back(matmul(normed, query_weight) + query_bias)).reshape(whole, HEADS, HD)
    keys = low(low_back(matmul(normed, key_weight))).reshape(whole, HEADS, HD)
    values = low(low_back(matmul(normed, value_weight) + value_bias)).reshape(whole, HEADS, HD)
    head_ids = jnp.arange(HEADS, dtype=jnp.float32)
    slopes = jnp.exp2(-8.0 * (head_ids + 1.0) / HEADS)
    block = min(512, whole)
    count = whole // block
    key_index = jnp.arange(whole, dtype=jnp.int32)
    reach = matmul(ancestor, onehot.T)

    def attend(index):
        start = index * block
        query_block = lax.dynamic_slice_in_dim(queries, start, block, 0)
        query_hot = lax.dynamic_slice_in_dim(onehot, start, block, 0)
        query_depth = lax.dynamic_slice_in_dim(depth, start, block, 0)
        rows_index = start + jnp.arange(block, dtype=jnp.int32)
        allowed = (matmul(query_hot, reach) > 0.5) & (key_index[None, :] <= rows_index[:, None])
        raw = jnp.einsum('bhd,khd->hbk', query_block, keys, precision=HIGH) * HD ** (-0.5)
        raw = raw - slopes[:, None, None] * (query_depth[:, None] - depth[None, :])[None]
        scores = jnp.where(allowed[None], low_back(raw), NEG)
        log_total = jax.nn.logsumexp(scores, axis=-1, keepdims=True)
        weights = low(jnp.exp(scores - log_total))
        mixed = jnp.einsum('hbk,khd->bhd', weights, values, precision=HIGH)
        return mixed.reshape(block, HEADS * HD)
    attended = lax.map(jax.checkpoint(attend), jnp.arange(count, dtype=jnp.int32)).reshape(whole, HEADS * HD)
    heads_out = low(low_back(attended))
    branch = low_back(matmul(heads_out, out_weight) + out_bias)
    middle = inputs + branch
    normed_two = low(norm_rows(middle, gain_two, shift_two))
    pre_act = low_back(matmul(normed_two, up_weight) + up_bias)
    activated = low(jax.nn.gelu(pre_act, approximate=False))
    return middle + matmul(activated, down_weight) + down_bias

def reference(hidden_in, norm1_gain, norm1_bias, query_weight, query_bias, key_weight, value_weight, value_bias, out_weight, out_bias, norm2_gain, norm2_bias, up_weight, up_bias, down_weight, down_bias, seg_lengths, parents, out_grad):
    params = tuple((w.astype(jnp.float32) for w in (norm1_gain, norm1_bias, query_weight, query_bias, key_weight, value_weight, value_bias, out_weight, out_bias, norm2_gain, norm2_bias, up_weight, up_bias, down_weight, down_bias)))
    inputs = hidden_in.astype(jnp.float32).reshape(SLOTS, SLOT, D)
    cotangent = out_grad.astype(jnp.float32).reshape(SLOTS, SLOT, D)

    def slot_step(totals, pieces):
        slot_in, slot_grad, lengths, parent_ids = pieces
        onehot, ancestor, depth = tree_tables(lengths, parent_ids, SLOT)
        result, pull = jax.vjp(lambda p, v: layer(p, v, onehot, ancestor, depth), params, slot_in)
        grads, input_grad = pull(slot_grad)
        totals = tuple((a + b for a, b in zip(totals, grads)))
        return (totals, (result.astype(jnp.bfloat16), input_grad.astype(jnp.bfloat16)))
    zeros = tuple((jnp.zeros(p.shape, jnp.float32) for p in params))
    totals, (outputs, input_grads) = lax.scan(slot_step, zeros, (inputs, cotangent, seg_lengths, parents))
    g_gain_one, g_shift_one, g_query_w, g_query_b, g_key_w, g_value_w, g_value_b, g_out_w, g_out_b, g_gain_two, g_shift_two, g_up_w, g_up_b, g_down_w, g_down_b = totals
    return (outputs.reshape(TOKENS, D), input_grads.reshape(TOKENS, D), g_gain_one, g_shift_one, g_query_w, g_query_b, g_key_w, g_value_w, g_value_b, g_out_w, g_out_b, g_gain_two, g_shift_two, g_up_w, g_up_b, g_down_w, g_down_b)
```

```python
from functools import partial

import jax
import jax.numpy as jnp
from jax import lax
from jax.experimental import pallas as pl
from jax.experimental.pallas import tpu as pltpu
from jax.sharding import PartitionSpec as P

HEADS = 32
EPS = 1e-05
HD = 64
LANES = 128
BIG = 2.0 ** 100
SLOPE_COL = 16
LSE_COL = 24
VMEM_LIMIT = 60 * 1024 * 1024


def dot_nt(left, right):
    return lax.dot_general(left, right, (((1,), (1,)), ((), ())), preferred_element_type=jnp.float32)


def dot_tn(left, right):
    return lax.dot_general(left, right, (((0,), (0,)), ((), ())), preferred_element_type=jnp.float32)


def dot_nn(left, right):
    return lax.dot_general(left, right, (((1,), (0,)), ((), ())), preferred_element_type=jnp.float32)


def three_parts(value):
    high = value.astype(jnp.bfloat16).astype(jnp.float32)
    rest = value - high
    middle = rest.astype(jnp.bfloat16).astype(jnp.float32)
    return high, middle, rest - middle


def tree_features(lengths, parent_ids, first_head, heads, block, whole):
    nseg = lengths.shape[0]
    seg_ids = jnp.arange(nseg, dtype=jnp.int32)
    ends = jnp.cumsum(lengths, dtype=jnp.int32)
    starts = ends - lengths
    parents = jnp.where(seg_ids > 0, parent_ids, 0)
    own = seg_ids[:, None] == seg_ids[None, :]
    ancestor = own | (parents[:, None] == seg_ids[None, :]) | (seg_ids[None, :] == 0)
    above = (ancestor & ~own).astype(jnp.int32)
    path_start = jnp.sum(above * lengths[None, :], axis=1, dtype=jnp.int32)
    token = jnp.arange(whole, dtype=jnp.int32)[:, None]
    hot = (token >= starts[None, :]) & (token < ends[None, :])
    depth = token + jnp.sum(jnp.where(hot, (path_start - starts)[None, :], 0), axis=1, keepdims=True)
    reach = jnp.sum(jnp.where(hot[:, None, :] & ancestor[None, :, :], 1, 0), axis=2)
    lane = jnp.arange(LANES, dtype=jnp.int32)[None, :]
    pad = ((0, 0), (0, LANES - nseg))
    query_side = jnp.pad(hot.astype(jnp.float32), pad)
    key_side = jnp.pad(jnp.where(reach > 0, 0.0, -BIG), pad)
    digit = lane - SLOPE_COL
    coarse = (depth // 256) * 256
    fine = depth - coarse
    in_slope = (digit >= 0) & (digit < 6)
    key_side = jnp.where(in_slope, jnp.where(digit % 2 == 0, coarse, fine).astype(jnp.float32), key_side)
    key_side = jnp.where((lane >= LSE_COL) & (lane < LSE_COL + 3), 1.0, key_side)
    head_ids = (first_head + jnp.arange(heads, dtype=jnp.int32)).astype(jnp.float32)
    slopes = jnp.exp2(-8.0 * (head_ids + 1.0) / 32)
    parts = jnp.stack(three_parts(slopes), axis=1)
    slope_rows = jnp.pad(jnp.repeat(parts, 2, axis=1), ((0, 0), (SLOPE_COL, LANES - SLOPE_COL - 6)))
    count = whole // block
    held = jnp.max(hot.reshape(count, block, nseg).astype(jnp.float32), axis=1)
    reached = jnp.max(reach.reshape(count, block, nseg).astype(jnp.float32), axis=1)
    ids = jnp.arange(count, dtype=jnp.int32)
    active = (jnp.sum(held[:, None, :] * reached[None, :, :], axis=2) > 0.5) & (ids[None, :] < ids[:, None])

    def packed(flags):
        rank = jnp.cumsum(flags.astype(jnp.int32), axis=1) - 1
        slot = flags[:, :, None] & (rank[:, :, None] == ids[None, None, :])
        listed = jnp.sum(jnp.where(slot, ids[None, :, None], 0), axis=1, dtype=jnp.int32)
        total = jnp.sum(flags.astype(jnp.int32), axis=1, keepdims=True, dtype=jnp.int32)
        return jnp.concatenate([total, listed], axis=1)

    return (
        query_side.astype(jnp.bfloat16),
        key_side.astype(jnp.bfloat16),
        slope_rows.astype(jnp.bfloat16),
        packed(active),
        packed(active.T),
    )


def _masks(block):
    lane = lax.broadcasted_iota(jnp.int32, (block, LANES), 1)
    return [lane < HD, lane >= HD], lane


def forward_kernel(place, lists, qkv, fq, fk, srow, o, lse, qa, vt, top, acc, *, block, pairs):
    count = qkv.shape[0] // block
    width = pairs * LANES
    heads = 2 * pairs
    halves, lane = _masks(block)
    zero = jnp.zeros((block, LANES), jnp.bfloat16)
    ones = jnp.ones((16, block), jnp.bfloat16)
    row = lax.broadcasted_iota(jnp.int32, (block, block), 0)
    col = lax.broadcasted_iota(jnp.int32, (block, block), 1)
    diagonal = row <= col

    def spot(index):
        return pl.ds(pl.multiple_of(place[index] * block, block), block)

    def canon(index):
        return pl.ds(pl.multiple_of(index * block, block), block)

    def turn(j, _):
        for pair in range(pairs):
            cols = slice(pair * LANES, (pair + 1) * LANES)
            turned = qkv[spot(j), 2 * width + pair * LANES : 2 * width + (pair + 1) * LANES].astype(jnp.float32).T.astype(jnp.bfloat16)
            for side in range(2):
                vt[j, 2 * pair + side] = jnp.concatenate([turned[side * HD : (side + 1) * HD], ones], axis=0)
        return 0

    lax.fori_loop(0, count, turn, 0)

    def step(j, first):
        key_features = fk[canon(j), :]
        keys = [
            jnp.concatenate([qkv[spot(j), width + pair * LANES : width + (pair + 1) * LANES], key_features], axis=1) for pair in range(pairs)
        ]
        scores = [dot_nt(keys[h // 2], qa[h]) for h in range(heads)]
        if first:
            scores = [jnp.where(diagonal, score, -BIG) for score in scores]
        bests = [jnp.max(score, axis=0, keepdims=True) for score in scores]
        if not first:
            olds = [top[h : h + 1, :] for h in range(heads)]
            bests = [jnp.maximum(old, best) for old, best in zip(olds, bests)]
            scales = [jnp.exp(old - best) for old, best in zip(olds, bests)]
        weights = [jnp.exp(score - best).astype(jnp.bfloat16) for score, best in zip(scores, bests)]
        mixed = [dot_nn(vt[j, h], weights[h]) for h in range(heads)]
        for h in range(heads):
            acc[h] = mixed[h] if first else acc[h] * scales[h] + mixed[h]
            top[h : h + 1, :] = bests[h]

    def rows(i, _):
        query_features = fq[canon(i), :]
        for pair in range(pairs):
            cols = slice(pair * LANES, (pair + 1) * LANES)
            queries = qkv[spot(i), cols] * jnp.bfloat16(HD ** -0.5)
            for side in range(2):
                h = 2 * pair + side
                qa[h] = jnp.concatenate(
                    [jnp.where(halves[side], queries, zero), query_features + srow[h : h + 1, :]], axis=1
                )
        step(i, True)

        def other(n, _):
            step(lists[i, n + 1], False)
            return 0

        lax.fori_loop(0, lists[i, 0], other, 0)
        logs = []
        for pair in range(pairs):
            cols = slice(pair * LANES, (pair + 1) * LANES)
            mixed = []
            for h in (2 * pair, 2 * pair + 1):
                total = acc[h, HD : HD + 1, :]
                mixed.append(acc[h, :HD, :] / total)
                logs.append(top[h : h + 1, :] + jnp.log(total))
            o[spot(i), cols] = jnp.concatenate(mixed, axis=0).T.astype(o.dtype)
        logs.append(jnp.zeros((LANES - heads, block), jnp.float32))
        lse[canon(i), :] = jnp.concatenate(logs, axis=0).T
        return 0

    lax.fori_loop(0, count, rows, 0)


def backward_kernel(place, lists, qkv, do, o, fq, fk, srow, lse, dqkv, qa, da, dqa, dka, dva, *, block, pairs):
    count = qkv.shape[0] // block
    width = pairs * LANES
    heads = 2 * pairs
    halves, lane = _masks(block)
    zero = jnp.zeros((block, LANES), jnp.bfloat16)
    row = lax.broadcasted_iota(jnp.int32, (block, block), 0)
    col = lax.broadcasted_iota(jnp.int32, (block, block), 1)
    diagonal = row <= col
    ones = jnp.where(lane < 3, 1.0, 0.0).astype(jnp.bfloat16)

    def spot(index):
        return pl.ds(pl.multiple_of(place[index] * block, block), block)

    def canon(index):
        return pl.ds(pl.multiple_of(index * block, block), block)

    def spread(value, first):
        high, middle, low = three_parts(value)
        spread_out = jnp.where(lane == first, high, 0.0)
        spread_out = jnp.where(lane == first + 1, middle, spread_out)
        return jnp.where(lane == first + 2, low, spread_out).astype(jnp.bfloat16)

    def prepare(i, _):
        query_features = fq[canon(i), :]
        logs = lse[canon(i), :]
        for pair in range(pairs):
            cols = slice(pair * LANES, (pair + 1) * LANES)
            queries = qkv[spot(i), cols] * jnp.bfloat16(HD ** -0.5)
            grads = do[spot(i), cols]
            product = grads.astype(jnp.float32) * o[spot(i), cols].astype(jnp.float32)
            for side in range(2):
                h = 2 * pair + side
                delta = jnp.sum(jnp.where(halves[side], product, 0.0), axis=1, keepdims=True)
                log_total = jnp.sum(jnp.where(lane == h, logs, 0.0), axis=1, keepdims=True)
                features = query_features + srow[h : h + 1, :] + spread(-log_total, LSE_COL)
                qa[h, canon(i), :] = jnp.concatenate([jnp.where(halves[side], queries, zero), features], axis=1)
                da[h, canon(i), :] = jnp.concatenate([jnp.where(halves[side], grads, zero), spread(-delta, 0)], axis=1)
        dqa[i] = jnp.zeros((pairs * LANES, block), jnp.float32)
        return 0

    lax.fori_loop(0, count, prepare, 0)

    def columns(j, _):
        key_features = fk[canon(j), :]
        key_blocks = [qkv[spot(j), width + pair * LANES : width + (pair + 1) * LANES] for pair in range(pairs)]
        keys = [jnp.concatenate([key_block, key_features], axis=1) for key_block in key_blocks]
        values = [
            jnp.concatenate([qkv[spot(j), 2 * width + pair * LANES : 2 * width + (pair + 1) * LANES], ones], axis=1) for pair in range(pairs)
        ]
        turned = [key_block.astype(jnp.float32).T.astype(jnp.bfloat16) for key_block in key_blocks]

        def step(i, first):
            query_rows = [qa[h, canon(i), :] for h in range(heads)]
            grad_rows = [da[h, canon(i), :] for h in range(heads)]
            scores = [dot_nt(keys[h // 2], query_rows[h]) for h in range(heads)]
            slopes = [dot_nt(values[h // 2], grad_rows[h]) for h in range(heads)]
            if first:
                scores = [jnp.where(diagonal, score, -BIG) for score in scores]
            probs = [jnp.exp(score) for score in scores]
            changes = [(prob * slope).astype(jnp.bfloat16) for prob, slope in zip(probs, slopes)]
            probs = [prob.astype(jnp.bfloat16) for prob in probs]
            for pair in range(pairs):
                cols = slice(pair * LANES, (pair + 1) * LANES)
                a, b = 2 * pair, 2 * pair + 1
                value_part = dot_nn(probs[a], grad_rows[a][:, :LANES]) + dot_nn(probs[b], grad_rows[b][:, :LANES])
                key_part = dot_nn(changes[a], query_rows[a][:, :LANES]) + dot_nn(changes[b], query_rows[b][:, :LANES])
                if first:
                    dva[:, cols] = value_part
                    dka[:, cols] = key_part
                else:
                    dva[:, cols] += value_part
                    dka[:, cols] += key_part
                for side in range(2):
                    h = 2 * pair + side
                    part = slice(h * HD, (h + 1) * HD)
                    dqa[i, part, :] += dot_nn(turned[pair][side * HD : (side + 1) * HD], changes[h])

        step(j, True)

        def other(n, _):
            step(lists[j, n + 1], False)
            return 0

        lax.fori_loop(0, lists[j, 0], other, 0)
        dqkv[spot(j), width : 2 * width] = dka[...].astype(dqkv.dtype)
        dqkv[spot(j), 2 * width :] = dva[...].astype(dqkv.dtype)
        return 0

    lax.fori_loop(0, count, columns, 0)

    def finish(i, _):
        dqkv[spot(i), :width] = (dqa[i] * HD ** -0.5).T.astype(dqkv.dtype)
        return 0

    lax.fori_loop(0, count, finish, 0)


def _specs(number):
    return [pl.BlockSpec(memory_space=pltpu.SMEM)] * 2 + [pl.BlockSpec(memory_space=pltpu.VMEM)] * number


def attention_forward(place, lists, qkv, fq, fk, srow, block):
    whole, width = qkv.shape[0], qkv.shape[1] // 3
    pairs = width // LANES
    return pl.pallas_call(
        partial(forward_kernel, block=block, pairs=pairs),
        out_shape=(jax.ShapeDtypeStruct((whole, width), jnp.bfloat16), jax.ShapeDtypeStruct((whole, LANES), jnp.float32)),
        in_specs=_specs(4),
        out_specs=(pl.BlockSpec(memory_space=pltpu.VMEM),) * 2,
        scratch_shapes=[
            pltpu.VMEM((2 * pairs, block, 2 * LANES), jnp.bfloat16),
            pltpu.VMEM((whole // block, 2 * pairs, HD + 16, block), jnp.bfloat16),
            pltpu.VMEM((8, block), jnp.float32),
            pltpu.VMEM((2 * pairs, HD + 16, block), jnp.float32),
        ],
        compiler_params=pltpu.CompilerParams(vmem_limit_bytes=VMEM_LIMIT),
        name="attention_forward",
    )(place, lists, qkv, fq, fk, srow)


def attention_backward(place, lists, qkv, do, o, fq, fk, srow, lse, block):
    whole, width = do.shape
    pairs = width // LANES
    return pl.pallas_call(
        partial(backward_kernel, block=block, pairs=pairs),
        out_shape=jax.ShapeDtypeStruct((whole, 3 * width), jnp.bfloat16),
        in_specs=_specs(7),
        out_specs=pl.BlockSpec(memory_space=pltpu.VMEM),
        scratch_shapes=[
            pltpu.VMEM((2 * pairs, whole, 2 * LANES), jnp.bfloat16),
            pltpu.VMEM((2 * pairs, whole, 2 * LANES), jnp.bfloat16),
            pltpu.VMEM((whole // block, width, block), jnp.float32),
            pltpu.VMEM((block, width), jnp.float32),
            pltpu.VMEM((block, width), jnp.float32),
        ],
        compiler_params=pltpu.CompilerParams(vmem_limit_bytes=VMEM_LIMIT),
        name="attention_backward",
    )(place, lists, qkv, do, o, fq, fk, srow, lse)


CORE = [(0, 1), (1, 0), (2, 3), (3, 2)]
ACROSS = [(0, 2), (2, 0), (1, 3), (3, 1)]
SWAP = [(0, 1), (1, 0)]
INWARD = [(0, 1), (3, 2)]
MIDDLE = [(1, 2), (2, 1)]
OUTWARD = [(1, 0), (2, 3)]


def low(value):
    return lax.optimization_barrier(value.astype(jnp.bfloat16))


def wide(value):
    return value.astype(jnp.float32)


def core(value):
    return lax.ppermute(value, "tensor", CORE)


def across(value):
    return lax.ppermute(value, "tensor", ACROSS)


def over(value):
    return lax.ppermute(value, "seq", SWAP)


def norm_forward(values, gain, shift):
    center = values - jnp.mean(values, axis=-1, keepdims=True)
    variance = jnp.mean(center * center, axis=-1, keepdims=True)
    inverse = lax.rsqrt(variance + EPS)
    normed = center * inverse
    return (normed * gain + shift, normed, inverse)


def norm_backward(incoming, normed, inverse, gain):
    scaled = incoming * gain
    inner = (
        scaled
        - jnp.mean(scaled, axis=-1, keepdims=True)
        - normed * jnp.mean(scaled * normed, axis=-1, keepdims=True)
    )
    return (inner * inverse, jnp.sum(incoming * normed, axis=0), jnp.sum(incoming, axis=0))


def halves_of(value, axis, which):
    size = value.shape[axis] // 2
    return (
        lax.dynamic_slice_in_dim(value, which * size, size, axis),
        lax.dynamic_slice_in_dim(value, (1 - which) * size, size, axis),
    )


def in_order(own, other, axis, which):
    first = which == 0
    return jnp.concatenate([jnp.where(first, own, other), jnp.where(first, other, own)], axis=axis)


def gather_group(value):
    if lax.axis_size("tensor") == 4:
        beside = core(value)
        far = across(value)
        return (jnp.concatenate([value, beside]), jnp.concatenate([far, core(far)]))
    rows = lax.all_gather(value, "tensor", axis=0, tiled=True)
    return tuple(jnp.split(rows, 2))


def scatter_group(far, near):
    if lax.axis_size("tensor") == 4:
        away = far()
        size = away.shape[0] // 2
        sent = across(low(wide(away[:size]) + wide(core(away[size:]))))
        here = near()
        return wide(here[:size]) + wide(core(here[size:])) + wide(sent)
    away = far()
    here = near()
    return wide(lax.psum_scatter(jnp.concatenate([here, away]), "tensor", scatter_dimension=0, tiled=True))


def gather_slot(value):
    if lax.axis_size("tensor") == 4:
        half = value.shape[0] // 2
        beside = core(value)
        far = across(value)
        past = over(value)
        both = jnp.concatenate([over(far[:half]), across(past[half:])])
        return [jnp.concatenate([piece, other]) for piece, other in
                ((value, beside), (far, core(far)), (past, core(past)), (both, core(both)))]
    own = lax.all_gather(value, "tensor", axis=0, tiled=True)
    return jnp.split(own, 2) + jnp.split(over(own), 2)


def scatter_slot(parts):
    if lax.axis_size("tensor") == 4:
        def chip(part):
            rows = part()
            size = rows.shape[0] // 2
            return wide(rows[:size]) + wide(core(rows[size:]))

        both = low(chip(parts[3]))
        half = both.shape[0] // 2
        both_far = across(both[:half])
        both_past = over(both[half:])
        far = chip(parts[1])
        far_first = across(low(far[:half]))
        past = chip(parts[2])
        past_last = over(low(past[half:]))
        far_last = across(low(far[half:] + wide(both_past)))
        past_first = over(low(past[:half] + wide(both_far)))
        here = chip(parts[0])
        return here + wide(jnp.concatenate([far_first, far_last])) + wide(jnp.concatenate([past_first, past_last]))
    own = lax.psum_scatter(jnp.concatenate([parts[0](), parts[1]()]), "tensor", scatter_dimension=0, tiled=True)
    other = lax.psum_scatter(jnp.concatenate([parts[2](), parts[3]()]), "tensor", scatter_dimension=0, tiled=True)
    return wide(own) + wide(over(other))


def tie(values, after):
    count = len(values)
    return pl.pallas_call(
        lambda *refs: None,
        out_shape=[jax.ShapeDtypeStruct(v.shape, v.dtype) for v in values],
        in_specs=[pl.BlockSpec(memory_space=pl.ANY)] * (count + len(after)),
        out_specs=[pl.BlockSpec(memory_space=pl.ANY)] * count,
        input_output_aliases={i: i for i in range(count)},
        name="tie",
    )(*values, *after)


class Hops:
    def __init__(self, steps):
        self.steps = steps
        self.pending, self.sent = next(steps)
        self.result = None

    def arrived(self, values):
        try:
            self.pending, self.sent = self.steps.send(values)
        except StopIteration as stop:
            self.pending, self.sent, self.result = [], [], stop.value


class Order:
    def __init__(self, after):
        self.after = [after]

    def enter(self, *values):
        out = tie(list(values), self.after)
        self.after = [out[0]]
        return out

    def done(self, *values):
        self.after.extend(values)

    def wait(self, *hops):
        values = [v for h in hops for v in h.pending]
        out = self.enter(*values)
        self.after = []
        for h in hops:
            count = len(h.pending)
            h.arrived(out[:count])
            self.after.extend(h.sent if h.sent else h.result)
            out = out[count:]


def on_line(value, pairs):
    return lax.ppermute(value, "dp", pairs)


def at_end():
    place = lax.axis_index("dp")
    return (place == 0) | (place == 3)


def line_hops(mine):
    (arrived,) = yield [on_line(mine, INWARD)], [mine]
    inner = low(wide(mine) + wide(arrived))
    (arrived,) = yield [on_line(inner, MIDDLE)], [inner]
    total = low(wide(inner) + wide(arrived))
    (arrived,) = yield [on_line(total, OUTWARD)], [total]
    total = low(jnp.where(at_end(), arrived, total))
    (arrived,) = yield [over(total)], [total]
    return [total, arrived]


def pair_hops(own, other):
    (arrived,) = yield [over(other)], [other, own]
    return (yield from line_hops(low(wide(own) + wide(arrived))))


def middle_hops(both):
    (arrived,) = yield [on_line(both, INWARD)], [both]
    inner = low(wide(both) + wide(arrived))
    size = both.shape[1] // 2
    upper = lax.axis_index("dp") // 2
    keep = lax.dynamic_slice_in_dim(inner, upper * size, size, 1)
    give = low(lax.dynamic_slice_in_dim(inner, (1 - upper) * size, size, 1))
    (arrived,) = yield [on_line(give, MIDDLE)], [give]
    kept = low(wide(keep) + wide(arrived))
    (arrived,) = yield [over(kept)], [kept]
    total = low(wide(kept) + wide(jnp.concatenate([arrived[1:], arrived[:1]])))
    first, second = yield [on_line(total, MIDDLE), on_line(total, OUTWARD)], [total]
    total = low(jnp.where(at_end(), second, total))
    (arrived,) = yield [on_line(first, OUTWARD)], [first, total]
    return [total, low(jnp.where(at_end(), arrived, first))]


def vector_sum(group, pair):
    if lax.axis_size("tensor") == 4 and lax.axis_size("dp") == 4:
        group = group + core(group)
        group = group + across(group)
        rows = jnp.concatenate([group, pair])
        rows = rows + over(rows)
        rows = rows + lax.ppermute(rows, "dp", CORE)
        rows = rows + lax.ppermute(rows, "dp", ACROSS)
        return rows[: group.shape[0]], rows[group.shape[0] :]
    return lax.psum(group, ("dp", "seq", "tensor")), lax.psum(pair, ("dp", "seq"))


def local(
    hidden_in, norm1_gain, norm1_bias, query_weight, query_bias, key_weight, value_weight, value_bias, out_weight,
    out_bias, norm2_gain, norm2_bias, up_weight, up_bias, down_weight, down_bias, seg_lengths, parents, out_grad,
):
    local_rows, model = hidden_in.shape
    tensor_count = lax.axis_size("tensor")
    group = local_rows * tensor_count
    whole = 2 * group
    columns = query_weight.shape[1]
    width = columns // 2
    heads = width // HD
    units = up_weight.shape[1]
    seq = lax.axis_index("seq")
    tensor = lax.axis_index("tensor")
    block = 256
    f32 = jnp.float32
    gain_one, gain_two = wide(norm1_gain), wide(norm2_gain)

    quick = tensor_count == 4 and lax.axis_size("dp") == 4

    inputs = wide(hidden_in)
    first, normed_one, inverse_one = norm_forward(inputs, gain_one, wide(norm1_bias))
    chunks_one = gather_slot(low(first))

    qkv_weight = jnp.concatenate([halves_of(w, 1, seq)[0] for w in (query_weight, key_weight, value_weight)], axis=1)
    qkv_bias = jnp.concatenate(
        [halves_of(query_bias, 0, seq)[0], jnp.zeros((width,), jnp.bfloat16), halves_of(value_bias, 0, seq)[0]]
    )
    out_rel = jnp.concatenate(halves_of(out_weight, 0, seq))
    up_rel = jnp.concatenate(halves_of(up_weight, 1, seq), axis=1)
    up_bias_rel = wide(jnp.concatenate(halves_of(up_bias, 0, seq)))
    down_rel = jnp.concatenate(halves_of(down_weight, 0, seq))

    blocks = jnp.arange(whole // block, dtype=jnp.int32)
    if tensor_count == 4:
        place = blocks ^ (seq * 4 + tensor)
    else:
        side = group // block
        place = ((blocks // side) ^ seq) * side + blocks % side
    fq, fk, slope_rows, key_lists, query_lists = tree_features(
        seg_lengths[0], parents[0], tensor * (columns // HD) + seq * heads, heads, block, whole
    )

    qkv = jnp.concatenate(
        [(jnp.dot(rows, qkv_weight, preferred_element_type=f32) + wide(qkv_bias)).astype(jnp.bfloat16) for rows in chunks_one]
    )
    order = Order(qkv)
    (out_grad_late,) = order.enter(out_grad)
    grad_near, grad_far = gather_group(out_grad_late)
    mixed, log_totals = attention_forward(place, key_lists, qkv, fq, fk, slope_rows, block)
    heads_out = jnp.concatenate([mixed[:group], over(mixed[group:])], axis=1)
    half = group // 2

    def product(left, right):
        return lambda: jnp.dot(left, right, preferred_element_type=f32).astype(jnp.bfloat16)

    def product_nt(left, right):
        return lambda: dot_nt(left, right).astype(jnp.bfloat16)

    def low_dot(left, right):
        return dot_tn(left, right).astype(jnp.bfloat16)

    branch = scatter_group(product(heads_out[half:], out_rel), product(heads_out[:half], out_rel)) + wide(out_bias)
    act_grad_near = low(dot_nt(grad_near, down_rel))
    order = Order(act_grad_near)
    (branch,) = order.enter(branch)
    middle = inputs + branch
    second, normed_two, inverse_two = norm_forward(middle, gain_two, wide(norm2_bias))
    two_near, two_far = gather_group(low(second))
    act_grad_far = low(dot_nt(grad_far, down_rel))
    order = Order(act_grad_far)
    (two_far,) = order.enter(two_far)
    activated, up_grad = [], []
    for rows, grads in ((two_near, act_grad_near), (two_far, act_grad_far)):
        pre = jnp.dot(rows, up_rel, preferred_element_type=f32) + up_bias_rel
        cdf = 0.5 * (1.0 + lax.erf(pre * (0.5 ** 0.5)))
        activated.append((pre * cdf).astype(jnp.bfloat16))
        slope = cdf + pre * (jnp.exp(-0.5 * pre * pre) * 0.3989422804014327)
        up_grad.append((wide(grads) * slope).astype(jnp.bfloat16))
    act_all = jnp.concatenate(activated)
    up_grad_all = jnp.concatenate(up_grad)
    rows_two = jnp.concatenate([two_near, two_far])
    grad_rows = jnp.concatenate([grad_near, grad_far])
    rows_one = jnp.concatenate(chunks_one)
    part = units // 2
    cotangent = wide(out_grad)

    def down_parts(index):
        cols = slice(index * (model // 2), (index + 1) * (model // 2))
        return low_dot(act_all[:, :part], grad_rows[:, cols]), low_dot(act_all[:, part:], grad_rows[:, cols])

    quarter = model // 4

    def up_parts(index):
        rows = rows_two[:, index * quarter : (index + 1) * quarter]
        return jnp.stack([low_dot(rows, up_grad_all[:, :part]), low_dot(rows, up_grad_all[:, part:])])

    def ffn_sum():
        return scatter_group(product(act_all[half:], down_rel), product(act_all[:half], down_rel)) + wide(down_bias)

    def norm_two(second_grad):
        middle_part, gain_grad, bias_grad = norm_backward(second_grad, normed_two, inverse_two, gain_two)
        return cotangent + middle_part, gain_grad, bias_grad

    def heads_grads(rows):
        return dot_nt(rows, out_rel).astype(jnp.bfloat16)

    def attention_grads(arrived, near_grads):
        return attention_backward(
            place, query_lists, qkv, jnp.concatenate([near_grads, arrived]), mixed, fq, fk, slope_rows, log_totals, block
        )

    def first_grads(grads):
        return scatter_slot([product_nt(grads[i * half : (i + 1) * half], qkv_weight) for i in range(4)])

    def qkv_part(grads, index):
        return low_dot(rows_one, grads[:, index * width : (index + 1) * width])

    if quick:
        order = Order(up_grad_all)
        (act_all,) = order.enter(act_all)
        down0 = Hops(pair_hops(*down_parts(0)))
        order.done(*down0.sent)
        (up_grad_all,) = order.enter(up_grad_all)
        up0 = Hops(middle_hops(up_parts(0)))
        order.done(*up0.sent)
        (up_grad_all,) = order.enter(up_grad_all)
        second_far = product_nt(up_grad_all[half:], up_rel)()
        second_size = half // 2
        second_sent = low(wide(second_far[:second_size]) + wide(core(second_far[second_size:])))
        second_back = across(second_sent)
        order.done(second_sent)
        (act_all,) = order.enter(act_all)
        down1 = Hops(pair_hops(*down_parts(1)))
        order.done(*down1.sent)
        (up_grad_all,) = order.enter(up_grad_all)
        second_near = product_nt(up_grad_all[:half], up_rel)()
        second_own = wide(second_near[:second_size]) + wide(core(second_near[second_size:]))
        order.done(second_own)
        (second_back,) = order.enter(second_back)
        middle_grad, grad_norm2_gain, grad_norm2_bias = norm_two(second_own + wide(second_back))
        branch_grad = low(middle_grad)
        branch_near, branch_far = gather_group(branch_grad)
        order.done(branch_grad)
        (act_all,) = order.enter(act_all)
        ffn_out = ffn_sum()
        grad_up_bias = jnp.sum(wide(up_grad_all), axis=0)
        order.wait(down0)
        order.wait(up0)
        (branch_far,) = order.enter(branch_far)
        heads_grad = jnp.concatenate([heads_grads(branch_near), heads_grads(branch_far)])
        heads_grad_sent = low(heads_grad[:, width:])
        heads_grad_back = over(heads_grad_sent)
        order.done(heads_grad, heads_grad_sent)
        (up_grad_all,) = order.enter(up_grad_all)
        up1 = Hops(middle_hops(up_parts(1)))
        order.done(*up1.sent)
        order.wait(up0)
        branch_rows = jnp.concatenate([branch_near, branch_far])
        order.wait(down1)
        order.wait(down0)
        (heads_grad_back,) = order.enter(heads_grad_back)
        grads = attention_grads(heads_grad_back, heads_grad[:, :width])
        order.done(grads)
        (up_grad_all,) = order.enter(up_grad_all)
        up2 = Hops(middle_hops(up_parts(2)))
        order.done(*up2.sent)
        order.wait(up0)
        order.wait(up1)
        order.wait(down0)
        (grads,) = order.enter(grads)
        first_grad = first_grads(grads)
        out0 = Hops(pair_hops(low_dot(heads_out[:, :width], branch_rows), low_dot(heads_out[:, width:], branch_rows)))
        order.done(*out0.sent)
        order.wait(up1)
        (up_grad_all,) = order.enter(up_grad_all)
        up3 = Hops(middle_hops(up_parts(3)))
        order.done(*up3.sent)
        qkv0 = Hops(line_hops(qkv_part(grads, 0)))
        order.wait(down0)
        order.wait(down1)
        order.wait(up0)
        order.wait(up2)
        order.wait(out0)
        order.wait(up1)
        qkv1 = Hops(line_hops(qkv_part(grads, 1)))
        qkv2 = Hops(line_hops(qkv_part(grads, 2)))
        order.wait(down0)
        order.wait(up2)
        order.wait(down1)
        order.wait(up1)
        order.wait(up3)
        order.wait(up2)
        order.wait(qkv0)
        order.wait(out0)
        order.wait(up0)
        order.wait(up3)
        order.wait(down1)
        order.wait(qkv0, qkv1)
        order.wait(out0)
        order.wait(up2)
        order.wait(up3)
        order.wait(qkv0, qkv1, qkv2)
        order.wait(out0)
        order.wait(up1)
        order.wait(qkv1, qkv2)
        order.wait(up3)
        order.wait(down1)
        order.wait(out0)
        order.wait(up2)
        order.wait(qkv0, qkv2)
        order.wait(up3)
        order.wait(qkv1)
        order.wait(qkv2)
        for h in (down0, down1, up0, up1, up2, up3, out0, qkv0, qkv1, qkv2):
            assert h.result is not None
    else:
        second_grad = scatter_group(product_nt(up_grad[1], up_rel), product_nt(up_grad[0], up_rel))
        middle_grad, grad_norm2_gain, grad_norm2_bias = norm_two(second_grad)
        branch_grad = low(middle_grad)
        branch_near, branch_far = gather_group(branch_grad)
        ffn_out = ffn_sum()
        grad_up_bias = jnp.sum(wide(up_grad_all), axis=0)
        heads_grad = jnp.concatenate([heads_grads(branch_near), heads_grads(branch_far)])
        grads = attention_grads(over(heads_grad[:, width:]), heads_grad[:, :width])
        branch_rows = jnp.concatenate([branch_near, branch_far])
        first_grad = first_grads(grads)
        sums = [[*down_parts(0)], [*down_parts(1)], *[[up[0], up[1]] for up in map(up_parts, range(4))]]
        sums.append([low_dot(heads_out[:, :width], branch_rows), low_dot(heads_out[:, width:], branch_rows)])
        axes = [0, 0, 1, 1, 1, 1, 0, 1, 1, 1]
        for i in range(3):
            sums.append([qkv_part(grads, i), jnp.zeros((model, width), jnp.bfloat16)])
        sums = [lax.psum(in_order(own, other, axis, seq), ("dp", "seq")) for (own, other), axis in zip(sums, axes)]

    layer_out = (middle + ffn_out).astype(jnp.bfloat16)
    grad_down_bias = jnp.sum(cotangent, axis=0)
    grad_out_bias = jnp.sum(wide(branch_grad), axis=0)
    bias_sum = jnp.sum(wide(grads), axis=0)
    input_part, grad_norm1_gain, grad_norm1_bias = norm_backward(first_grad, normed_one, inverse_one, gain_one)
    grad_in = (middle_grad + input_part).astype(jnp.bfloat16)

    nothing = jnp.zeros((width,), f32)
    query_bias_row = in_order(bias_sum[:width], nothing, 0, seq)
    value_bias_row = in_order(bias_sum[2 * width :], nothing, 0, seq)
    up_bias_row = in_order(grad_up_bias[:part], grad_up_bias[part:], 0, seq)
    pairs = jnp.concatenate([query_bias_row, value_bias_row, up_bias_row])
    group_rows, pair_rows = vector_sum(
        jnp.stack([grad_norm1_gain, grad_norm1_bias, grad_out_bias, grad_norm2_gain, grad_norm2_bias, grad_down_bias]),
        jnp.pad(pairs, (0, -pairs.shape[0] % model)).reshape(-1, model),
    )
    pair_rows = pair_rows.reshape(-1)

    def put(out, value, row, column):
        return lax.dynamic_update_slice(out, wide(value), (row, column))

    if quick:
        down = jnp.zeros((units, model), f32)
        for i, (own, other) in enumerate((down0.result, down1.result)):
            down = put(down, own, seq * part, i * (model // 2))
            down = put(down, other, (1 - seq) * part, i * (model // 2))
        up = jnp.zeros((model, units), f32)
        upper = lax.axis_index("dp") // 2
        for i, h in enumerate((up0, up1, up2, up3)):
            for value, side in zip(h.result, (upper, 1 - upper)):
                row = i * quarter + side * (quarter // 2)
                up = put(up, value[0], row, seq * part)
                up = put(up, value[1], row, (1 - seq) * part)
        out = jnp.zeros((columns, model), f32)
        out = put(put(out, out0.result[0], seq * width, 0), out0.result[1], (1 - seq) * width, 0)
        qkv_out = []
        for h in (qkv0, qkv1, qkv2):
            empty = jnp.zeros((model, columns), f32)
            qkv_out.append(put(put(empty, h.result[0], 0, seq * width), h.result[1], 0, (1 - seq) * width))
    else:
        down = wide(jnp.concatenate(sums[:2], axis=1))
        up = wide(jnp.concatenate(sums[2:6], axis=0))
        out = wide(sums[6])
        qkv_out = [wide(v) for v in sums[7:]]

    return (
        layer_out,
        grad_in,
        group_rows[0],
        group_rows[1],
        qkv_out[0],
        pair_rows[:columns],
        qkv_out[1],
        qkv_out[2],
        pair_rows[columns : 2 * columns],
        out,
        group_rows[2],
        group_rows[3],
        group_rows[4],
        up,
        pair_rows[2 * columns : 2 * columns + units],
        down,
        group_rows[5],
    )


def solution(mesh):
    placed = (
        P(("dp", "seq", "tensor"), None),
        P(),
        P(),
        P(None, "tensor"),
        P("tensor"),
        P(None, "tensor"),
        P(None, "tensor"),
        P("tensor"),
        P("tensor", None),
        P(),
        P(),
        P(),
        P(None, "tensor"),
        P("tensor"),
        P("tensor", None),
        P(),
        P("dp", None),
        P("dp", None),
        P(("dp", "seq", "tensor"), None),
    )
    return jax.shard_map(
        local,
        mesh=mesh,
        in_specs=placed,
        out_specs=(
            P(("dp", "seq", "tensor"), None),
            P(("dp", "seq", "tensor"), None),
            P(),
            P(),
            P(None, "tensor"),
            P("tensor"),
            P(None, "tensor"),
            P(None, "tensor"),
            P("tensor"),
            P("tensor", None),
            P(),
            P(),
            P(),
            P(None, "tensor"),
            P("tensor"),
            P("tensor", None),
            P(),
        ),
        check_vma=False,
    )
```

```python
from functools import partial

import jax
import jax.numpy as jnp
from jax import lax
from jax.experimental import pallas as pl
from jax.experimental.pallas import tpu as pltpu
from jax.sharding import PartitionSpec as P

HEADS = 32
EPS = 1e-05
HD = 64
LANES = 128
BIG = 2.0 ** 100
SLOPE_COL = 16
LSE_COL = 24
VMEM_LIMIT = 36 * 1024 * 1024
MATMUL_LIMIT = 26 * 1024 * 1024


def dot_nt(left, right):
    return lax.dot_general(left, right, (((1,), (1,)), ((), ())), preferred_element_type=jnp.float32)


def dot_tn(left, right):
    return lax.dot_general(left, right, (((0,), (0,)), ((), ())), preferred_element_type=jnp.float32)


def dot_nn(left, right):
    return lax.dot_general(left, right, (((1,), (0,)), ((), ())), preferred_element_type=jnp.float32)


def three_parts(value):
    high = value.astype(jnp.bfloat16).astype(jnp.float32)
    rest = value - high
    middle = rest.astype(jnp.bfloat16).astype(jnp.float32)
    return high, middle, rest - middle


def tree_features(lengths, parent_ids, first_head, heads, block, whole):
    nseg = lengths.shape[0]
    seg_ids = jnp.arange(nseg, dtype=jnp.int32)
    ends = jnp.cumsum(lengths, dtype=jnp.int32)
    starts = ends - lengths
    parents = jnp.where(seg_ids > 0, parent_ids, 0)
    own = seg_ids[:, None] == seg_ids[None, :]
    ancestor = own | (parents[:, None] == seg_ids[None, :]) | (seg_ids[None, :] == 0)
    above = (ancestor & ~own).astype(jnp.int32)
    path_start = jnp.sum(above * lengths[None, :], axis=1, dtype=jnp.int32)
    token = jnp.arange(whole, dtype=jnp.int32)[:, None]
    hot = (token >= starts[None, :]) & (token < ends[None, :])
    depth = token + jnp.sum(jnp.where(hot, (path_start - starts)[None, :], 0), axis=1, keepdims=True)
    reach = jnp.sum(jnp.where(hot[:, None, :] & ancestor[None, :, :], 1, 0), axis=2)
    lane = jnp.arange(LANES, dtype=jnp.int32)[None, :]
    pad = ((0, 0), (0, LANES - nseg))
    query_side = jnp.pad(hot.astype(jnp.float32), pad)
    key_side = jnp.pad(jnp.where(reach > 0, 0.0, -BIG), pad)
    digit = lane - SLOPE_COL
    coarse = (depth // 256) * 256
    fine = depth - coarse
    in_slope = (digit >= 0) & (digit < 6)
    key_side = jnp.where(in_slope, jnp.where(digit % 2 == 0, coarse, fine).astype(jnp.float32), key_side)
    key_side = jnp.where((lane >= LSE_COL) & (lane < LSE_COL + 3), 1.0, key_side)
    head_ids = (first_head + jnp.arange(heads, dtype=jnp.int32)).astype(jnp.float32)
    slopes = jnp.exp2(-8.0 * (head_ids + 1.0) / 32)
    parts = jnp.stack(three_parts(slopes), axis=1)
    slope_rows = jnp.pad(jnp.repeat(parts, 2, axis=1), ((0, 0), (SLOPE_COL, LANES - SLOPE_COL - 6)))
    count = whole // block
    held = jnp.max(hot.reshape(count, block, nseg).astype(jnp.float32), axis=1)
    reached = jnp.max(reach.reshape(count, block, nseg).astype(jnp.float32), axis=1)
    ids = jnp.arange(count, dtype=jnp.int32)
    active = (jnp.sum(held[:, None, :] * reached[None, :, :], axis=2) > 0.5) & (ids[None, :] < ids[:, None])

    def packed(flags):
        rank = jnp.cumsum(flags.astype(jnp.int32), axis=1) - 1
        slot = flags[:, :, None] & (rank[:, :, None] == ids[None, None, :])
        listed = jnp.sum(jnp.where(slot, ids[None, :, None], 0), axis=1, dtype=jnp.int32)
        total = jnp.sum(flags.astype(jnp.int32), axis=1, keepdims=True, dtype=jnp.int32)
        return jnp.concatenate([total, listed], axis=1)

    return (
        query_side.astype(jnp.bfloat16),
        key_side.astype(jnp.bfloat16),
        slope_rows.astype(jnp.bfloat16),
        packed(active),
        packed(active.T),
    )


def _masks(block):
    lane = lax.broadcasted_iota(jnp.int32, (block, LANES), 1)
    return [lane < HD, lane >= HD], lane


def forward_kernel(first_block, place, lists, qkv, fq, fk, srow, o, lse, qa, vt, top, acc, *, block, pairs):
    count = qkv.shape[0] // block
    width = pairs * LANES
    heads = 2 * pairs
    halves, lane = _masks(block)
    zero = jnp.zeros((block, LANES), jnp.bfloat16)
    ones = jnp.ones((16, block), jnp.bfloat16)
    row = lax.broadcasted_iota(jnp.int32, (block, block), 0)
    col = lax.broadcasted_iota(jnp.int32, (block, block), 1)
    diagonal = row <= col
    side_blocks = count // 2

    def spot(index):
        return pl.ds(pl.multiple_of(place[index] * block, block), block)

    def canon(index):
        return pl.ds(pl.multiple_of(index * block, block), block)

    def turn(j, _):
        for pair in range(pairs):
            cols = slice(pair * LANES, (pair + 1) * LANES)
            turned = qkv[spot(j), 2 * width + pair * LANES : 2 * width + (pair + 1) * LANES].astype(jnp.float32).T.astype(jnp.bfloat16)
            for side in range(2):
                vt[j, 2 * pair + side] = jnp.concatenate([turned[side * HD : (side + 1) * HD], ones], axis=0)
        return 0

    lax.fori_loop(0, count, turn, 0)

    def step(j, first):
        key_features = fk[canon(j), :]
        keys = [
            jnp.concatenate([qkv[spot(j), width + pair * LANES : width + (pair + 1) * LANES], key_features], axis=1) for pair in range(pairs)
        ]
        scores = [dot_nt(keys[h // 2], qa[h]) for h in range(heads)]
        if first:
            scores = [jnp.where(diagonal, score, -BIG) for score in scores]
        bests = [jnp.max(score, axis=0, keepdims=True) for score in scores]
        if not first:
            olds = [top[h : h + 1, :] for h in range(heads)]
            bests = [jnp.maximum(old, best) for old, best in zip(olds, bests)]
            scales = [jnp.exp(old - best) for old, best in zip(olds, bests)]
        weights = [jnp.exp(score - best).astype(jnp.bfloat16) for score, best in zip(scores, bests)]
        mixed = [dot_nn(vt[j, h], weights[h]) for h in range(heads)]
        for h in range(heads):
            acc[h] = mixed[h] if first else acc[h] * scales[h] + mixed[h]
            top[h : h + 1, :] = bests[h]

    def rows(n, _):
        i = place[first_block[0] + n]
        query_features = fq[canon(i), :]
        for pair in range(pairs):
            cols = slice(pair * LANES, (pair + 1) * LANES)
            queries = qkv[spot(i), cols] * jnp.bfloat16(HD ** -0.5)
            for side in range(2):
                h = 2 * pair + side
                qa[h] = jnp.concatenate(
                    [jnp.where(halves[side], queries, zero), query_features + srow[h : h + 1, :]], axis=1
                )
        step(i, True)

        def other(m, _):
            step(lists[i, m + 1], False)
            return 0

        lax.fori_loop(0, lists[i, 0], other, 0)
        logs = []
        for pair in range(pairs):
            cols = slice(pair * LANES, (pair + 1) * LANES)
            mixed = []
            for h in (2 * pair, 2 * pair + 1):
                total = acc[h, HD : HD + 1, :]
                mixed.append(acc[h, :HD, :] / total)
                logs.append(top[h : h + 1, :] + jnp.log(total))
            o[canon(n), cols] = jnp.concatenate(mixed, axis=0).T.astype(o.dtype)
        logs.append(jnp.zeros((LANES - heads, block), jnp.float32))
        lse[canon(n), :] = jnp.concatenate(logs, axis=0).T
        return 0

    lax.fori_loop(0, o.shape[0] // block, rows, 0)


def backward_kernel(
    place, lists, qkv, do, o_own, o_other, fq, fk, srow, lse_own, lse_other, dqkv, qa, da, dqa, dka, dva, *, block, pairs
):
    count = qkv.shape[0] // block
    width = pairs * LANES
    heads = 2 * pairs
    halves, lane = _masks(block)
    zero = jnp.zeros((block, LANES), jnp.bfloat16)
    row = lax.broadcasted_iota(jnp.int32, (block, block), 0)
    col = lax.broadcasted_iota(jnp.int32, (block, block), 1)
    diagonal = row <= col
    ones = jnp.where(lane < 3, 1.0, 0.0).astype(jnp.bfloat16)
    side_blocks = count // 2

    def spot(index):
        return pl.ds(pl.multiple_of(place[index] * block, block), block)

    def canon(index):
        return pl.ds(pl.multiple_of(index * block, block), block)

    def spread(value, first):
        high, middle, low = three_parts(value)
        spread_out = jnp.where(lane == first, high, 0.0)
        spread_out = jnp.where(lane == first + 1, middle, spread_out)
        return jnp.where(lane == first + 2, low, spread_out).astype(jnp.bfloat16)

    def prepare(i, _):
        query_features = fq[canon(i), :]
        own = place[i] < side_blocks
        mixed_rows = canon(place[i] % side_blocks)
        logs = jnp.where(own, lse_own[mixed_rows, :], lse_other[mixed_rows, :])
        for pair in range(pairs):
            cols = slice(pair * LANES, (pair + 1) * LANES)
            queries = qkv[spot(i), cols] * jnp.bfloat16(HD ** -0.5)
            grads = do[spot(i), cols]
            mixed = jnp.where(own, o_own[mixed_rows, cols], o_other[mixed_rows, cols])
            product = grads.astype(jnp.float32) * mixed.astype(jnp.float32)
            for side in range(2):
                h = 2 * pair + side
                delta = jnp.sum(jnp.where(halves[side], product, 0.0), axis=1, keepdims=True)
                log_total = jnp.sum(jnp.where(lane == h, logs, 0.0), axis=1, keepdims=True)
                features = query_features + srow[h : h + 1, :] + spread(-log_total, LSE_COL)
                qa[h, canon(i), :] = jnp.concatenate([jnp.where(halves[side], queries, zero), features], axis=1)
                da[h, canon(i), :] = jnp.concatenate([jnp.where(halves[side], grads, zero), spread(-delta, 0)], axis=1)
        dqa[i] = jnp.zeros((pairs * LANES, block), jnp.float32)
        return 0

    lax.fori_loop(0, count, prepare, 0)

    def columns(j, _):
        key_features = fk[canon(j), :]
        key_blocks = [qkv[spot(j), width + pair * LANES : width + (pair + 1) * LANES] for pair in range(pairs)]
        keys = [jnp.concatenate([key_block, key_features], axis=1) for key_block in key_blocks]
        values = [
            jnp.concatenate([qkv[spot(j), 2 * width + pair * LANES : 2 * width + (pair + 1) * LANES], ones], axis=1) for pair in range(pairs)
        ]
        turned = [key_block.astype(jnp.float32).T.astype(jnp.bfloat16) for key_block in key_blocks]

        def step(i, first):
            query_rows = [qa[h, canon(i), :] for h in range(heads)]
            grad_rows = [da[h, canon(i), :] for h in range(heads)]
            scores = [dot_nt(keys[h // 2], query_rows[h]) for h in range(heads)]
            slopes = [dot_nt(values[h // 2], grad_rows[h]) for h in range(heads)]
            if first:
                scores = [jnp.where(diagonal, score, -BIG) for score in scores]
            probs = [jnp.exp(score) for score in scores]
            changes = [(prob * slope).astype(jnp.bfloat16) for prob, slope in zip(probs, slopes)]
            probs = [prob.astype(jnp.bfloat16) for prob in probs]
            for pair in range(pairs):
                cols = slice(pair * LANES, (pair + 1) * LANES)
                a, b = 2 * pair, 2 * pair + 1
                value_part = dot_nn(probs[a], grad_rows[a][:, :LANES]) + dot_nn(probs[b], grad_rows[b][:, :LANES])
                key_part = dot_nn(changes[a], query_rows[a][:, :LANES]) + dot_nn(changes[b], query_rows[b][:, :LANES])
                if first:
                    dva[:, cols] = value_part
                    dka[:, cols] = key_part
                else:
                    dva[:, cols] += value_part
                    dka[:, cols] += key_part
                for side in range(2):
                    h = 2 * pair + side
                    part = slice(h * HD, (h + 1) * HD)
                    dqa[i, part, :] += dot_nn(turned[pair][side * HD : (side + 1) * HD], changes[h])

        step(j, True)

        def other(n, _):
            step(lists[j, n + 1], False)
            return 0

        lax.fori_loop(0, lists[j, 0], other, 0)
        dqkv[spot(j), width : 2 * width] = dka[...].astype(dqkv.dtype)
        dqkv[spot(j), 2 * width :] = dva[...].astype(dqkv.dtype)
        return 0

    lax.fori_loop(0, count, columns, 0)

    def finish(i, _):
        dqkv[spot(i), :width] = (dqa[i] * HD ** -0.5).T.astype(dqkv.dtype)
        return 0

    lax.fori_loop(0, count, finish, 0)


def cost(microseconds):
    return pl.CostEstimate(flops=int(microseconds * 1.15e9), bytes_accessed=0, transcendentals=0)


def _attention_call(name, kernel, scalars, arrays, outs, scratch, microseconds):
    vmem = pl.BlockSpec(memory_space=pltpu.VMEM)
    return pl.pallas_call(
        kernel,
        out_shape=outs,
        in_specs=[pl.BlockSpec(memory_space=pltpu.SMEM)] * len(scalars) + [vmem] * len(arrays),
        out_specs=[vmem] * len(outs),
        scratch_shapes=scratch,
        compiler_params=pltpu.CompilerParams(vmem_limit_bytes=VMEM_LIMIT),
        cost_estimate=cost(microseconds),
        name=name,
    )(*scalars, *arrays)


def attention_forward(first_block, count, place, lists, qkv, fq, fk, srow, block):
    whole, width = qkv.shape[0], qkv.shape[1] // 3
    pairs = width // LANES
    return _attention_call(
        "attention_forward",
        partial(forward_kernel, block=block, pairs=pairs),
        (first_block.reshape(1), place, lists),
        (qkv, fq, fk, srow),
        [jax.ShapeDtypeStruct((count * block, width), jnp.bfloat16), jax.ShapeDtypeStruct((count * block, LANES), jnp.float32)],
        [
            pltpu.VMEM((2 * pairs, block, 2 * LANES), jnp.bfloat16),
            pltpu.VMEM((whole // block, 2 * pairs, HD + 16, block), jnp.bfloat16),
            pltpu.VMEM((8, block), jnp.float32),
            pltpu.VMEM((2 * pairs, HD + 16, block), jnp.float32),
        ],
        0,
    )


def attention_backward(place, lists, qkv, do, o, fq, fk, srow, lse, block):
    whole, width = do.shape
    pairs = width // LANES
    return _attention_call(
        "attention_backward",
        partial(backward_kernel, block=block, pairs=pairs),
        (place, lists),
        (qkv, do, *o, fq, fk, srow, *lse),
        [jax.ShapeDtypeStruct((whole, 3 * width), jnp.bfloat16)],
        [
            pltpu.VMEM((2 * pairs, whole, 2 * LANES), jnp.bfloat16),
            pltpu.VMEM((2 * pairs, whole, 2 * LANES), jnp.bfloat16),
            pltpu.VMEM((whole // block, width, block), jnp.float32),
            pltpu.VMEM((block, width), jnp.float32),
            pltpu.VMEM((block, width), jnp.float32),
        ],
        0,
    )[0]


CORE = [(0, 1), (1, 0), (2, 3), (3, 2)]
ACROSS = [(0, 2), (2, 0), (1, 3), (3, 1)]
SWAP = [(0, 1), (1, 0)]
INWARD = [(0, 1), (3, 2)]
MIDDLE = [(1, 2), (2, 1)]
OUTWARD = [(1, 0), (2, 3)]


def low(value):
    return lax.optimization_barrier(value.astype(jnp.bfloat16))


def wide(value):
    return value.astype(jnp.float32)


def core(value):
    return lax.ppermute(value, "tensor", CORE)


def across(value):
    return lax.ppermute(value, "tensor", ACROSS)


def over(value):
    return lax.ppermute(value, "seq", SWAP)


def norm_forward(values, gain, shift):
    center = values - jnp.mean(values, axis=-1, keepdims=True)
    variance = jnp.mean(center * center, axis=-1, keepdims=True)
    inverse = lax.rsqrt(variance + EPS)
    normed = center * inverse
    return (normed * gain + shift, normed, inverse)


def norm_backward(incoming, normed, inverse, gain):
    scaled = incoming * gain
    inner = (
        scaled
        - jnp.mean(scaled, axis=-1, keepdims=True)
        - normed * jnp.mean(scaled * normed, axis=-1, keepdims=True)
    )
    return (inner * inverse, jnp.sum(incoming * normed, axis=0), jnp.sum(incoming, axis=0))


def halves_of(value, axis, which):
    size = value.shape[axis] // 2
    return (
        lax.dynamic_slice_in_dim(value, which * size, size, axis),
        lax.dynamic_slice_in_dim(value, (1 - which) * size, size, axis),
    )


def in_order(own, other, axis, which):
    first = which == 0
    return jnp.concatenate([jnp.where(first, own, other), jnp.where(first, other, own)], axis=axis)


def gather_group(value):
    if lax.axis_size("tensor") == 4:
        beside = core(value)
        far = across(value)
        return (jnp.concatenate([value, beside]), jnp.concatenate([far, core(far)]))
    rows = lax.all_gather(value, "tensor", axis=0, tiled=True)
    return tuple(jnp.split(rows, 2))


def scatter_group(far, near):
    if lax.axis_size("tensor") == 4:
        away = far()
        size = away.shape[0] // 2
        sent = across(low(wide(away[:size]) + wide(core(away[size:]))))
        here = near()
        return wide(here[:size]) + wide(core(here[size:])) + wide(sent)
    away = far()
    here = near()
    return wide(lax.psum_scatter(jnp.concatenate([here, away]), "tensor", scatter_dimension=0, tiled=True))


def gather_slot(value):
    if lax.axis_size("tensor") == 4:
        half = value.shape[0] // 2
        beside = core(value)
        far = across(value)
        past = over(value)
        both = jnp.concatenate([over(far[:half]), across(past[half:])])
        return [jnp.concatenate([piece, other]) for piece, other in
                ((value, beside), (far, core(far)), (past, core(past)), (both, core(both)))]
    own = lax.all_gather(value, "tensor", axis=0, tiled=True)
    return jnp.split(own, 2) + jnp.split(over(own), 2)


def scatter_slot(parts):
    if lax.axis_size("tensor") == 4:
        def chip(part):
            rows = part()
            size = rows.shape[0] // 2
            return wide(rows[:size]) + wide(core(rows[size:]))

        both = low(chip(parts[3]))
        half = both.shape[0] // 2
        both_far = across(both[:half])
        both_past = over(both[half:])
        far = chip(parts[1])
        far_first = across(low(far[:half]))
        past = chip(parts[2])
        past_last = over(low(past[half:]))
        far_last = across(low(far[half:] + wide(both_past)))
        past_first = over(low(past[:half] + wide(both_far)))
        here = chip(parts[0])
        return here + wide(jnp.concatenate([far_first, far_last])) + wide(jnp.concatenate([past_first, past_last]))
    own = lax.psum_scatter(jnp.concatenate([parts[0](), parts[1]()]), "tensor", scatter_dimension=0, tiled=True)
    other = lax.psum_scatter(jnp.concatenate([parts[2](), parts[3]()]), "tensor", scatter_dimension=0, tiled=True)
    return wide(own) + wide(over(other))


def on_line(value, pairs):
    return lax.ppermute(value, "dp", pairs)


def vector_sum(group, pair):
    if lax.axis_size("tensor") == 4 and lax.axis_size("dp") == 4:
        group = group + core(group)
        group = group + across(group)
        rows = jnp.concatenate([group, pair])
        rows = rows + over(rows)
        rows = rows + lax.ppermute(rows, "dp", CORE)
        rows = rows + lax.ppermute(rows, "dp", ACROSS)
        return rows[: group.shape[0]], rows[group.shape[0] :]
    return lax.psum(group, ("dp", "seq", "tensor")), lax.psum(pair, ("dp", "seq"))


def tie(values, after, name):
    count = len(values)
    return pl.pallas_call(
        lambda *refs: None,
        out_shape=[jax.ShapeDtypeStruct(v.shape, v.dtype) for v in values],
        in_specs=[pl.BlockSpec(memory_space=pl.ANY)] * (count + len(after)),
        out_specs=[pl.BlockSpec(memory_space=pl.ANY)] * count,
        input_output_aliases={i: i for i in range(count)},
        compiler_params=pltpu.CompilerParams(vmem_limit_bytes=1 << 16),
        cost_estimate=cost(0),
        name="tie_" + name,
    )(*values, *after)


class Order:
    def __init__(self):
        self.after, self.label = [], "front"

    def enter(self, *values):
        out = tie(list(values), self.after, self.label)
        self.after = [out[0]]
        return out if len(out) > 1 else out[0]

    def done(self, *values):
        self.after.extend(values)


def feed_forward(pieces, weight, bias, grads, act, up_grad, chunk, tile=512):
    half, model, units = 2 * pieces[0].shape[0], weight.shape[0], weight.shape[1]

    def kernel(first, second, weight_ref, bias_ref, grads_ref, *refs):
        act_ref, up_ref, sums_ref = refs[-3:]
        rows = jnp.concatenate([first[...], second[...]], axis=0)
        pre = dot_nn(rows, weight_ref[...]) + wide(bias_ref[...])
        cdf = 0.5 * (1.0 + lax.erf(pre * (0.5**0.5)))
        act_ref[...] = (pre * cdf).astype(jnp.bfloat16)
        slope = cdf + pre * (jnp.exp(-0.5 * pre * pre) * 0.3989422804014327)
        low_grad = (wide(grads_ref[...]) * slope).astype(jnp.bfloat16)
        up_ref[...] = low_grad
        sums_ref[...] = jnp.broadcast_to(jnp.sum(wide(low_grad), axis=0, keepdims=True), sums_ref.shape)

    there = pl.BlockSpec(memory_space=pl.ANY)
    whole = pl.BlockSpec(pieces[0].shape, lambda n: (0, 0))
    filled = pl.BlockSpec((half, tile), lambda n: (chunk, n))
    held = [] if act is None else [act, up_grad]
    return pl.pallas_call(
        kernel,
        grid=(units // tile,),
        out_shape=[jax.ShapeDtypeStruct((2 * half, units), jnp.bfloat16)] * 2 + [jax.ShapeDtypeStruct((8, units), jnp.float32)],
        in_specs=[
            whole,
            whole,
            pl.BlockSpec((model, tile), lambda n: (0, n)),
            pl.BlockSpec((1, tile), lambda n: (0, n)),
            pl.BlockSpec((half, tile), lambda n: (0, n)),
            *[there] * len(held),
        ],
        out_specs=[filled, filled, pl.BlockSpec((8, tile), lambda n: (0, n))],
        input_output_aliases={5: 0, 6: 1} if held else {},
        compiler_params=pltpu.CompilerParams(vmem_limit_bytes=MATMUL_LIMIT),
        cost_estimate=cost(0),
        name="feed_forward",
    )(*pieces, weight, bias.reshape(1, -1), grads, *held)


def blank(shape):
    return pl.pallas_call(
        lambda out: None,
        out_shape=jax.ShapeDtypeStruct(shape, jnp.float32),
        out_specs=pl.BlockSpec(memory_space=pl.ANY),
        compiler_params=pltpu.CompilerParams(vmem_limit_bytes=1 << 16),
        cost_estimate=cost(0),
        name="blank",
    )()


DOTS = {"nn": dot_nn, "nt": dot_nt, "tn": dot_tn}


def matmul(name, kind, where, grid, left, right, outs, axis=0):
    def kernel(where_ref, left_ref, right_ref, *out_refs):
        total = DOTS[kind](left_ref[...], right_ref[...])
        start = 0
        for out in out_refs:
            size = out.shape[axis]
            piece = total[start : start + size] if axis == 0 else total[:, start : start + size]
            out[...] = piece.astype(jnp.bfloat16)
            start += size

    return pl.pallas_call(
        kernel,
        grid_spec=pltpu.PrefetchScalarGridSpec(
            num_scalar_prefetch=1,
            grid=grid,
            in_specs=[pl.BlockSpec(block, index) for _, block, index in (left, right)],
            out_specs=[pl.BlockSpec(block, index) for _, block, index in outs],
        ),
        out_shape=[jax.ShapeDtypeStruct(shape, jnp.bfloat16) for shape, _, _ in outs],
        compiler_params=pltpu.CompilerParams(vmem_limit_bytes=MATMUL_LIMIT),
        cost_estimate=cost(0),
        name=name,
    )(where, left[0], right[0])


def plain_local(
    hidden_in, norm1_gain, norm1_bias, query_weight, query_bias, key_weight, value_weight, value_bias, out_weight,
    out_bias, norm2_gain, norm2_bias, up_weight, up_bias, down_weight, down_bias, seg_lengths, parents, out_grad,
):
    local_rows, model = hidden_in.shape
    tensor_count = lax.axis_size("tensor")
    group = local_rows * tensor_count
    whole = 2 * group
    columns = query_weight.shape[1]
    width = columns // 2
    heads = width // HD
    units = up_weight.shape[1]
    seq = lax.axis_index("seq")
    tensor = lax.axis_index("tensor")
    block = 256
    f32 = jnp.float32
    gain_one, gain_two = wide(norm1_gain), wide(norm2_gain)

    inputs = wide(hidden_in)
    first, normed_one, inverse_one = norm_forward(inputs, gain_one, wide(norm1_bias))
    chunks_one = gather_slot(low(first))

    qkv_weight = jnp.concatenate([halves_of(w, 1, seq)[0] for w in (query_weight, key_weight, value_weight)], axis=1)
    qkv_bias = jnp.concatenate(
        [halves_of(query_bias, 0, seq)[0], jnp.zeros((width,), jnp.bfloat16), halves_of(value_bias, 0, seq)[0]]
    )
    out_rel = jnp.concatenate(halves_of(out_weight, 0, seq))
    up_rel = jnp.concatenate(halves_of(up_weight, 1, seq), axis=1)
    up_bias_rel = wide(jnp.concatenate(halves_of(up_bias, 0, seq)))
    down_rel = jnp.concatenate(halves_of(down_weight, 0, seq))

    blocks = jnp.arange(whole // block, dtype=jnp.int32)
    if tensor_count == 4:
        place = blocks ^ (seq * 4 + tensor)
    else:
        side = group // block
        place = ((blocks // side) ^ seq) * side + blocks % side
    fq, fk, slope_rows, key_lists, query_lists = tree_features(
        seg_lengths[0], parents[0], tensor * (columns // HD) + seq * heads, heads, block, whole
    )

    qkv = jnp.concatenate(
        [(jnp.dot(rows, qkv_weight, preferred_element_type=f32) + wide(qkv_bias)).astype(jnp.bfloat16) for rows in chunks_one]
    )
    grad_near, grad_far = gather_group(out_grad)
    side = whole // block // 2
    mixed_other, logs_other = attention_forward(jnp.int32(side), side, place, key_lists, qkv, fq, fk, slope_rows, block)
    mixed_own, logs_own = attention_forward(jnp.int32(0), side, place, key_lists, qkv, fq, fk, slope_rows, block)
    heads_out = jnp.concatenate([mixed_own, over(mixed_other)], axis=1)
    half = group // 2

    def product(left, right):
        return lambda: jnp.dot(left, right, preferred_element_type=f32).astype(jnp.bfloat16)

    def product_nt(left, right):
        return lambda: dot_nt(left, right).astype(jnp.bfloat16)

    def low_dot(left, right):
        return dot_tn(left, right).astype(jnp.bfloat16)

    branch = scatter_group(product(heads_out[half:], out_rel), product(heads_out[:half], out_rel)) + wide(out_bias)
    act_grad_near = low(dot_nt(grad_near, down_rel))
    middle = inputs + branch
    second, normed_two, inverse_two = norm_forward(middle, gain_two, wide(norm2_bias))
    two_near, two_far = gather_group(low(second))
    act_grad_far = low(dot_nt(grad_far, down_rel))
    activated, up_grad = [], []
    for rows, grads in ((two_near, act_grad_near), (two_far, act_grad_far)):
        pre = jnp.dot(rows, up_rel, preferred_element_type=f32) + up_bias_rel
        cdf = 0.5 * (1.0 + lax.erf(pre * (0.5 ** 0.5)))
        activated.append((pre * cdf).astype(jnp.bfloat16))
        slope = cdf + pre * (jnp.exp(-0.5 * pre * pre) * 0.3989422804014327)
        up_grad.append((wide(grads) * slope).astype(jnp.bfloat16))
    act_all = jnp.concatenate(activated)
    up_grad_all = jnp.concatenate(up_grad)
    rows_two = jnp.concatenate([two_near, two_far])
    grad_rows = jnp.concatenate([grad_near, grad_far])
    rows_one = jnp.concatenate(chunks_one)
    part = units // 2
    cotangent = wide(out_grad)

    def down_parts(index):
        cols = slice(index * (model // 2), (index + 1) * (model // 2))
        return low_dot(act_all[:, :part], grad_rows[:, cols]), low_dot(act_all[:, part:], grad_rows[:, cols])

    quarter = model // 4

    def up_parts(index):
        rows = rows_two[:, index * quarter : (index + 1) * quarter]
        return jnp.stack([low_dot(rows, up_grad_all[:, :part]), low_dot(rows, up_grad_all[:, part:])])

    def ffn_sum():
        return scatter_group(product(act_all[half:], down_rel), product(act_all[:half], down_rel)) + wide(down_bias)

    def norm_two(second_grad):
        middle_part, gain_grad, bias_grad = norm_backward(second_grad, normed_two, inverse_two, gain_two)
        return cotangent + middle_part, gain_grad, bias_grad

    def heads_grads(rows):
        return dot_nt(rows, out_rel).astype(jnp.bfloat16)

    def attention_grads(arrived, near_grads):
        return attention_backward(
            place, query_lists, qkv, jnp.concatenate([near_grads, arrived]), (mixed_own, mixed_other),
            fq, fk, slope_rows, (logs_own, logs_other), block,
        )

    def first_grads(grads):
        return scatter_slot([product_nt(grads[i * half : (i + 1) * half], qkv_weight) for i in range(4)])

    def qkv_part(grads, index):
        return low_dot(rows_one, grads[:, index * width : (index + 1) * width])

    second_grad = scatter_group(product_nt(up_grad[1], up_rel), product_nt(up_grad[0], up_rel))
    middle_grad, grad_norm2_gain, grad_norm2_bias = norm_two(second_grad)
    branch_grad = low(middle_grad)
    branch_near, branch_far = gather_group(branch_grad)
    ffn_out = ffn_sum()
    grad_up_bias = jnp.sum(wide(up_grad_all), axis=0)
    heads_grad = jnp.concatenate([heads_grads(branch_near), heads_grads(branch_far)])
    grads = attention_grads(over(heads_grad[:, width:]), heads_grad[:, :width])
    branch_rows = jnp.concatenate([branch_near, branch_far])
    first_grad = first_grads(grads)
    sums = [[*down_parts(0)], [*down_parts(1)], *[[up[0], up[1]] for up in map(up_parts, range(4))]]
    sums.append([low_dot(heads_out[:, :width], branch_rows), low_dot(heads_out[:, width:], branch_rows)])
    axes = [0, 0, 1, 1, 1, 1, 0, 1, 1, 1]
    for i in range(3):
        sums.append([qkv_part(grads, i), jnp.zeros((model, width), jnp.bfloat16)])
    sums = [lax.psum(in_order(own, other, axis, seq), ("dp", "seq")) for (own, other), axis in zip(sums, axes)]

    layer_out = (middle + ffn_out).astype(jnp.bfloat16)
    grad_down_bias = jnp.sum(cotangent, axis=0)
    grad_out_bias = jnp.sum(wide(branch_grad), axis=0)
    bias_sum = jnp.sum(wide(grads), axis=0)
    input_part, grad_norm1_gain, grad_norm1_bias = norm_backward(first_grad, normed_one, inverse_one, gain_one)
    grad_in = (middle_grad + input_part).astype(jnp.bfloat16)

    nothing = jnp.zeros((width,), f32)
    query_bias_row = in_order(bias_sum[:width], nothing, 0, seq)
    value_bias_row = in_order(bias_sum[2 * width :], nothing, 0, seq)
    up_bias_row = in_order(grad_up_bias[:part], grad_up_bias[part:], 0, seq)
    pairs = jnp.concatenate([query_bias_row, value_bias_row, up_bias_row])
    group_rows, pair_rows = vector_sum(
        jnp.stack([grad_norm1_gain, grad_norm1_bias, grad_out_bias, grad_norm2_gain, grad_norm2_bias, grad_down_bias]),
        jnp.pad(pairs, (0, -pairs.shape[0] % model)).reshape(-1, model),
    )
    pair_rows = pair_rows.reshape(-1)

    down = wide(jnp.concatenate(sums[:2], axis=1))
    up = wide(jnp.concatenate(sums[2:6], axis=0))
    out = wide(sums[6])
    qkv_out = [wide(v) for v in sums[7:]]

    return (
        layer_out,
        grad_in,
        group_rows[0],
        group_rows[1],
        qkv_out[0],
        pair_rows[:columns],
        qkv_out[1],
        qkv_out[2],
        pair_rows[columns : 2 * columns],
        out,
        group_rows[2],
        group_rows[3],
        group_rows[4],
        up,
        pair_rows[2 * columns : 2 * columns + units],
        down,
        group_rows[5],
    )


ORDER = " ".join((
    "U0 SF SFa D0", "SN U2 S u0", "BN d0 BF u0", "D1 u2 ATT u0", "d0 u2 d1 u0", "F3 u2 Q0 u0",
    "FB F1 d0 F2", "d1 U3 O u2", "FE FL q0 F0", "d0 o d1 u3", "u2 FN Q1 q0", "o u3 d0 d1",
    "U1 q1 o u3", "q0 o q1 u1", "GF V d1 u3", "q0 u1 GFa q1", "v o u3 u1", "GN u1 v v",
    "v v q1 u1",
)).split()


def line_steps(mine):
    arrived = yield [on_line(mine, INWARD)], [mine]
    inner = low(wide(mine) + wide(arrived))
    arrived = yield [on_line(inner, MIDDLE)], [inner]
    total = low(wide(inner) + wide(arrived))
    arrived = yield [on_line(total, OUTWARD)], [total]
    line = lax.axis_index("dp")
    total = low(jnp.where((line == 0) | (line == 3), arrived, total))
    arrived = yield [over(total)], [total]
    return total, arrived


def pair_steps(own, other):
    arrived = yield [over(other)], [other, own]
    return (yield from line_steps(low(wide(own) + wide(arrived))))


def middle_steps(value):
    arrived = yield [on_line(value, INWARD)], [value]
    inner = wide(value) + wide(arrived)
    size = value.shape[0] // 2
    line = lax.axis_index("dp")
    upper, end = line // 2, (line == 0) | (line == 3)
    keep = lax.dynamic_slice_in_dim(inner, upper * size, size, 0)
    give = low(lax.dynamic_slice_in_dim(inner, (1 - upper) * size, size, 0))
    arrived = yield [on_line(give, MIDDLE)], [give]
    kept = low(keep + wide(arrived))
    arrived = yield [over(kept)], [kept]
    total = low(wide(kept) + wide(arrived))
    arrived, outer = yield [on_line(total, MIDDLE), on_line(total, OUTWARD)], [total]
    total = low(jnp.where(end, outer, total))
    last = yield [on_line(arrived, OUTWARD)], [arrived, total]
    return total, low(jnp.where(end, last, arrived))


def vector_steps(group, pair):
    arrived = yield [core(group)], [group]
    group = group + arrived
    arrived = yield [across(group)], [group]
    rows = jnp.concatenate([group + arrived, pair])
    arrived = yield [over(rows)], [rows]
    rows = rows + arrived
    arrived = yield [on_line(rows, CORE)], [rows]
    rows = rows + arrived
    arrived = yield [on_line(rows, ACROSS)], [rows]
    rows = rows + arrived
    return rows[: group.shape[0]], rows[group.shape[0] :]


class Sums:
    def __init__(self, order):
        self.order, self.steps, self.pending, self.results = order, {}, {}, {}

    def start(self, name, steps):
        self.steps[name] = steps
        self.pending[name], sent = next(steps)
        self.order.done(*sent)

    def wait(self, name):
        arrived = self.order.enter(*self.pending[name])
        try:
            self.pending[name], sent = self.steps[name].send(arrived)
            self.order.done(*sent)
        except StopIteration as stop:
            self.results[name] = stop.value


def quick_local(
    hidden_in, norm1_gain, norm1_bias, query_weight, query_bias, key_weight, value_weight, value_bias, out_weight,
    out_bias, norm2_gain, norm2_bias, up_weight, up_bias, down_weight, down_bias, seg_lengths, parents, out_grad,
):
    size, model = hidden_in.shape
    half, group, whole = 2 * size, 4 * size, 8 * size
    columns = query_weight.shape[1]
    width = columns // 2
    heads = width // HD
    units = up_weight.shape[1]
    part = units // 2
    seq, tensor = lax.axis_index("seq"), lax.axis_index("tensor")
    block = size
    f32, bf16 = jnp.float32, jnp.bfloat16
    gain_one, gain_two = wide(norm1_gain), wide(norm2_gain)

    def product(left, right):
        return jnp.dot(left, right, preferred_element_type=f32).astype(bf16)

    def product_nt(left, right):
        return dot_nt(left, right).astype(bf16)

    def product_tn(left, right):
        return dot_tn(left, right).astype(bf16)

    order = Order()
    inputs = wide(hidden_in)
    first, normed_one, inverse_one = norm_forward(inputs, gain_one, wide(norm1_bias))
    first = low(first)
    far, past = across(first), over(first)
    order.done(first)
    lengths, parent_ids = order.enter(seg_lengths, parents)
    qkv_weight = jnp.concatenate([halves_of(w, 1, seq)[0] for w in (query_weight, key_weight, value_weight)], axis=1)
    qkv_bias = jnp.concatenate(
        [halves_of(query_bias, 0, seq)[0], jnp.zeros((width,), bf16), halves_of(value_bias, 0, seq)[0]]
    )

    def projected(rows):
        return (jnp.dot(rows, qkv_weight, preferred_element_type=f32) + wide(qkv_bias)).astype(bf16)

    blocks = jnp.arange(whole // block, dtype=jnp.int32)
    place = blocks ^ (seq * 4 + tensor)
    fq, fk, slope_rows, key_lists, query_lists = tree_features(
        lengths[0], parent_ids[0], tensor * (columns // HD) + seq * heads, heads, block, whole
    )
    chunks_one = [jnp.concatenate([first, core(first)])]
    qkv_parts = [projected(chunks_one[0])]
    out_rel = jnp.concatenate(halves_of(out_weight, 0, seq))
    order.done(qkv_parts[0], fk, fq, out_rel)
    far, past = order.enter(far, past)
    both = [over(low(far[: size // 2])), across(low(past[size // 2 :]))]
    for piece in (far, past):
        chunks_one.append(jnp.concatenate([piece, core(piece)]))
        qkv_parts.append(projected(chunks_one[-1]))
        order.done(qkv_parts[-1])
    both = jnp.concatenate(order.enter(*both))
    chunks_one.append(jnp.concatenate([both, core(both)]))
    qkv_parts.append(projected(chunks_one[-1]))
    qkv = jnp.concatenate(qkv_parts)

    order.done(qkv)
    grad_piece = order.enter(out_grad)
    grad_back = across(grad_piece)
    side = whole // block // 2

    def attend(first_block, count):
        place_now = order.enter(place)
        mixed, logs = attention_forward(jnp.int32(first_block), count, place_now, key_lists, qkv, fq, fk, slope_rows, block)
        order.done(mixed)
        return mixed, logs

    mixed_other, logs_other = attend(side, side)
    far_part = attend(side // 2, side - side // 2)
    mixed_past = over(mixed_other)
    near_part = attend(0, side // 2)
    mixed_own, logs_own = (jnp.concatenate(pair) for pair in zip(near_part, far_part))
    mixed_past, grad_back = order.enter(mixed_past, grad_back)
    heads_out = jnp.concatenate([mixed_own, mixed_past], axis=1)
    branch_far = product(heads_out[half:], out_rel)
    branch_sent = low(wide(branch_far[:size]) + wide(core(branch_far[size:])))
    branch_back = across(branch_sent)
    branch_near = product(heads_out[:half], out_rel)
    grad_near = jnp.concatenate([grad_piece, core(grad_piece)])
    grad_far = jnp.concatenate([grad_back, core(grad_back)])
    order.done(branch_near, branch_sent)
    grad_near = order.enter(grad_near)
    act_grad_near = product_nt(grad_near, down_weight)
    order.done(act_grad_near)
    branch_back = order.enter(branch_back)
    branch = wide(branch_near[:size]) + wide(core(branch_near[size:])) + wide(branch_back)
    middle = inputs + branch + wide(out_bias)
    second, normed_two, inverse_two = norm_forward(middle, gain_two, wide(norm2_bias))
    second = low(second)
    second_core, second_back = core(second), across(second)
    order.done(second)
    grad_far = order.enter(grad_far)
    act_grad_far = product_nt(grad_far, down_weight)
    order.done(act_grad_far)
    second_core = order.enter(second_core)
    act, up_grad, up_sums_near = feed_forward((second, second_core), up_weight, up_bias, act_grad_near, None, None, 0)
    order.done(act, up_grad)
    second_back = order.enter(second_back)
    second_last = core(second_back)
    act, up_grad, up_sums_far = feed_forward(
        (second_back, second_last), up_weight, up_bias, act_grad_far, act, up_grad, 1
    )
    order.done(act, up_grad)
    grad_near, grad_far = order.enter(grad_near, grad_far)
    grad_rows = jnp.concatenate([grad_near, grad_far])
    rows_two = jnp.concatenate([second, second_core, second_back, second_last])
    rows_one = jnp.concatenate(chunks_one)
    cotangent = wide(out_grad)

    sums = Sums(order)
    state = {}
    order.done(act, up_grad)

    down_parts, up_parts = 2, sum(name.startswith("U") for name in ORDER)
    where = seq.reshape(1)
    tile = 512

    def start_down(index):
        cols = model // down_parts
        steps = part // tile
        rows = order.enter(grad_rows)
        halves = [
            matmul(
                "down_part", "tn", where, (steps,),
                (act, (group, tile), lambda m, w, s=s: (0, (w[0] ^ s) * steps + m)),
                (rows, (group, cols), lambda m, w: (0, index)),
                [((part, cols), (tile, cols), lambda m, w: (m, 0))],
            )[0]
            for s in range(2)
        ]
        sums.start("d%d" % index, pair_steps(*halves))

    def start_up(index):
        rows = model // up_parts
        (value,) = matmul(
            "up_part", "tn", where, (units // 1024,),
            (order.enter(rows_two), (group, rows), lambda n, w: (0, index)),
            (up_grad, (group, 1024), lambda n, w: (0, n)),
            [((rows, units), (rows, 1024), lambda n, w: (0, n))],
        )
        sums.start("u%d" % index, middle_steps(value))

    def chunk_rows(name, kind, left, chunk, right, tile):
        depth = left.shape[1]
        cols = right.shape[0] if kind == "nt" else right.shape[1]
        block, index = ((tile, depth), lambda n, w: (n, 0)) if kind == "nt" else ((depth, tile), lambda n, w: (0, n))
        return matmul(
            name, kind, where, (cols // tile,),
            (left, (half, depth), lambda n, w: (chunk, 0)), (right, block, index),
            [((size, cols), (size, tile), lambda n, w: (0, n))] * 2,
        )

    def second_far():
        own, other = chunk_rows("second_gradient", "nt", order.enter(up_grad), 1, up_weight, 512)
        state["second_far"] = own, core(other)
        order.done(own)

    def second_send():
        own, other = state["second_far"]
        sent = low(wide(own) + wide(order.enter(other)))
        state["second_back"] = across(sent)
        order.done(sent)

    def second_near():
        own, other = chunk_rows("second_gradient", "nt", order.enter(up_grad), 0, up_weight, 512)
        state["second_own"] = wide(own) + wide(core(other))
        order.done(own)

    def second_norm():
        incoming = state["second_own"] + wide(order.enter(state["second_back"]))
        inner, gain_grad, bias_grad = norm_backward(incoming, normed_two, inverse_two, gain_two)
        middle_grad = cotangent + inner
        branch_grad = low(middle_grad)
        state["middle_grad"], state["norm2"] = middle_grad, (gain_grad, bias_grad)
        state["dy"] = [branch_grad, core(branch_grad)]
        state["dy_back"] = across(branch_grad)
        order.done(branch_grad)

    def heads_rows(pieces):
        rows = jnp.concatenate(pieces)
        return matmul(
            "heads_gradient", "nt", where, (1,),
            (rows, rows.shape, lambda n, w: (0, 0)), (out_rel, out_rel.shape, lambda n, w: (0, 0)),
            [((half, width), (half, width), lambda n, w: (0, 0))] * 2, 1,
        )

    def heads_near():
        state["dy"] = [order.enter(state["dy"][0]), state["dy"][1]]
        state["do_near"] = heads_rows(state["dy"])
        order.done(state["do_near"][0])

    def heads_far():
        back = order.enter(state["dy_back"])
        state["dy"] += [back, core(back)]
        far = heads_rows(state["dy"][2:])
        state["do_own"], sent = (low(jnp.concatenate(pair)) for pair in zip(state["do_near"], far))
        state["do_past"] = over(sent)
        order.done(state["do_own"], sent)

    def attention():
        rows = jnp.concatenate([state["do_own"], order.enter(state["do_past"])])
        state["grads"] = attention_backward(
            place, query_lists, qkv, rows, (mixed_own, mixed_other), fq, fk, slope_rows, (logs_own, logs_other), block
        )
        order.done(state["grads"])

    def ffn_far():
        own, other = chunk_rows("feed_back", "nn", order.enter(act), 1, down_weight, 512)
        state["ffn_far"] = own, core(other)
        order.done(own)

    def ffn_send():
        own, other = state["ffn_far"]
        sent = low(wide(own) + wide(order.enter(other)))
        state["ffn_back"] = across(sent)
        order.done(sent)

    def ffn_near():
        own, other = chunk_rows("feed_back", "nn", order.enter(act), 0, down_weight, 512)
        state["ffn_own"] = wide(own) + wide(core(other))
        order.done(own)

    def start_out():
        rows = order.enter(jnp.concatenate(state["dy"]))
        halves = [
            matmul(
                "out_part", "tn", where, (2,),
                (v, (group, width), lambda n, w: (0, 0)), (rows, (group, model // 2), lambda n, w: (0, n)),
                [((width, model), (width, model // 2), lambda n, w: (0, n))],
            )[0]
            for v in (mixed_own, mixed_past)
        ]
        sums.start("o", pair_steps(*halves))

    def first_rows(chunk):
        grads = state["grads"] = order.enter(state["grads"])
        own, other = chunk_rows("first_gradient", "nt", grads, chunk, qkv_weight, 1024)
        state["F%d" % chunk] = wide(own) + wide(core(other))
        order.done(own)

    def first_both():
        both = low(state["F3"])
        state["both"] = across(both)
        order.done(both)

    def first_far():
        far = low(state["F1"])
        state["far"] = across(far)
        order.done(far)

    def first_past():
        past = low(state["F2"] + wide(order.enter(state["both"])))
        state["past"] = over(past)
        order.done(past)

    def first_norm():
        far, past = order.enter(state["far"], state["past"])
        incoming = state["F0"] + wide(far) + wide(past)
        inner, gain_grad, bias_grad = norm_backward(incoming, normed_one, inverse_one, gain_one)
        state["grad_in"] = (state["middle_grad"] + inner).astype(bf16)
        state["norm1"] = gain_grad, bias_grad
        order.done(state["grad_in"])

    def start_qkv(index):
        grads = state["grads"] = order.enter(state["grads"])
        size_of = 3 * width // projection_parts
        (value,) = matmul(
            "projection_part", "tn", where, (4,),
            (rows_one, (whole, model // 4), lambda m, w: (0, m)), (grads, (whole, size_of), lambda m, w: (0, index)),
            [((model, size_of), (model // 4, size_of), lambda m, w: (m, 0))],
        )
        sums.start("q%d" % index, line_steps(value))

    projection_parts = sum(name.startswith("Q") for name in ORDER)
    steps = {
        "SF": second_far, "SFa": second_send,
        "SN": second_near, "S": second_norm, "BN": heads_near, "BF": heads_far, "ATT": attention, "GF": ffn_far, "GFa": ffn_send,
        "GN": ffn_near, "O": start_out, "F0": partial(first_rows, 0), "F1": partial(first_rows, 1),
        "F2": partial(first_rows, 2), "F3": partial(first_rows, 3), "FB": first_both, "FE": first_far, "FL": first_past,
        "FN": first_norm, }
    for i in range(4):
        steps["D%d" % i], steps["U%d" % i], steps["Q%d" % i] = partial(start_down, i), partial(start_up, i), partial(start_qkv, i)
    def start_vectors():
        bias_sum = jnp.sum(wide(state["grads"]), axis=0)
        nothing = jnp.zeros((width,), f32)
        pairs = jnp.concatenate(
            [
                in_order(bias_sum[:width], nothing, 0, seq),
                in_order(bias_sum[2 * width :], nothing, 0, seq),
                up_sums_near[0] + up_sums_far[0],
            ]
        )
        grad_out_bias = jnp.sum(wide(state["dy"][0]), axis=0)
        grad_down_bias = jnp.sum(cotangent, axis=0)
        group_rows = jnp.stack([*state["norm1"], grad_out_bias, *state["norm2"], grad_down_bias])
        sums.start("v", vector_steps(group_rows, jnp.pad(pairs, (0, -pairs.shape[0] % model)).reshape(-1, model)))

    steps["V"] = start_vectors
    for name in ORDER:
        order.label = name
        if name in steps:
            steps[name]()
        else:
            sums.wait(name)

    layer_out = (middle + state["ffn_own"] + wide(state["ffn_back"]) + wide(down_bias)).astype(bf16)
    group_rows, pair_rows = sums.results["v"]
    pair_rows = pair_rows.reshape(-1)

    def put(out, value, row, column):
        return lax.dynamic_update_slice(out, wide(value), (row, column))

    up = blank((model, units))
    upper = lax.axis_index("dp") // 2
    cols = model // up_parts
    for i in range(up_parts):
        kept, other = sums.results["u%d" % i]
        up = put(put(up, kept, i * cols + upper * (cols // 2), 0), other, i * cols + (1 - upper) * (cols // 2), 0)
    down = blank((units, model))
    cols = model // down_parts
    for i in range(down_parts):
        own, other = sums.results["d%d" % i]
        down = put(put(down, own, seq * part, i * cols), other, (1 - seq) * part, i * cols)
    out = blank((columns, model))
    own, other = sums.results["o"]
    out = put(put(out, own, seq * width, 0), other, (1 - seq) * width, 0)
    own, other = (
        jnp.concatenate([sums.results["q%d" % i][j] for i in range(projection_parts)], axis=1) for j in range(2)
    )
    projections = []
    for i in range(3):
        cols = slice(i * width, (i + 1) * width)
        projection = put(blank((model, columns)), own[:, cols], 0, seq * width)
        projections.append(put(projection, other[:, cols], 0, (1 - seq) * width))
    return (
        layer_out,
        state["grad_in"],
        group_rows[0],
        group_rows[1],
        projections[0],
        pair_rows[:columns],
        projections[1],
        projections[2],
        pair_rows[columns : 2 * columns],
        out,
        group_rows[2],
        group_rows[3],
        group_rows[4],
        up,
        pair_rows[2 * columns : 2 * columns + units],
        down,
        group_rows[5],
    )


def local(*args):
    quick = lax.axis_size("tensor") == 4 and lax.axis_size("dp") == 4 and args[0].shape[0] == 256
    return quick_local(*args) if quick else plain_local(*args)


def solution(mesh):
    placed = (
        P(("dp", "seq", "tensor"), None),
        P(),
        P(),
        P(None, "tensor"),
        P("tensor"),
        P(None, "tensor"),
        P(None, "tensor"),
        P("tensor"),
        P("tensor", None),
        P(),
        P(),
        P(),
        P(None, "tensor"),
        P("tensor"),
        P("tensor", None),
        P(),
        P("dp", None),
        P("dp", None),
        P(("dp", "seq", "tensor"), None),
    )
    return jax.shard_map(
        local,
        mesh=mesh,
        in_specs=placed,
        out_specs=(
            P(("dp", "seq", "tensor"), None),
            P(("dp", "seq", "tensor"), None),
            P(),
            P(),
            P(None, "tensor"),
            P("tensor"),
            P(None, "tensor"),
            P(None, "tensor"),
            P("tensor"),
            P("tensor", None),
            P(),
            P(),
            P(),
            P(None, "tensor"),
            P("tensor"),
            P("tensor", None),
            P(),
        ),
        check_vma=False,
    )
```

```python
from functools import partial

import jax
import jax.numpy as jnp
from jax import lax
from jax.experimental import pallas as pl
from jax.experimental.pallas import tpu as pltpu
from jax.sharding import PartitionSpec as P

HEADS = 32
EPS = 1e-05
HD = 64
LANES = 128
BIG = 2.0 ** 100
SLOPE_COL = 16
LSE_COL = 24
VMEM_LIMIT = 36 * 1024 * 1024
MATMUL_LIMIT = 26 * 1024 * 1024


def dot_nt(left, right):
    return lax.dot_general(left, right, (((1,), (1,)), ((), ())), preferred_element_type=jnp.float32)


def dot_tn(left, right):
    return lax.dot_general(left, right, (((0,), (0,)), ((), ())), preferred_element_type=jnp.float32)


def dot_nn(left, right):
    return lax.dot_general(left, right, (((1,), (0,)), ((), ())), preferred_element_type=jnp.float32)


def three_parts(value):
    high = value.astype(jnp.bfloat16).astype(jnp.float32)
    rest = value - high
    middle = rest.astype(jnp.bfloat16).astype(jnp.float32)
    return high, middle, rest - middle


def tree_features(lengths, parent_ids, first_head, heads, block, whole):
    nseg = lengths.shape[0]
    seg_ids = jnp.arange(nseg, dtype=jnp.int32)
    ends = jnp.cumsum(lengths, dtype=jnp.int32)
    starts = ends - lengths
    parents = jnp.where(seg_ids > 0, parent_ids, 0)
    own = seg_ids[:, None] == seg_ids[None, :]
    ancestor = own | (parents[:, None] == seg_ids[None, :]) | (seg_ids[None, :] == 0)
    above = (ancestor & ~own).astype(jnp.int32)
    path_start = jnp.sum(above * lengths[None, :], axis=1, dtype=jnp.int32)
    token = jnp.arange(whole, dtype=jnp.int32)[:, None]
    hot = (token >= starts[None, :]) & (token < ends[None, :])
    depth = token + jnp.sum(jnp.where(hot, (path_start - starts)[None, :], 0), axis=1, keepdims=True)
    reach = jnp.sum(jnp.where(hot[:, None, :] & ancestor[None, :, :], 1, 0), axis=2)
    lane = jnp.arange(LANES, dtype=jnp.int32)[None, :]
    pad = ((0, 0), (0, LANES - nseg))
    query_side = jnp.pad(hot.astype(jnp.float32), pad)
    key_side = jnp.pad(jnp.where(reach > 0, 0.0, -BIG), pad)
    digit = lane - SLOPE_COL
    coarse = (depth // 256) * 256
    fine = depth - coarse
    in_slope = (digit >= 0) & (digit < 6)
    key_side = jnp.where(in_slope, jnp.where(digit % 2 == 0, coarse, fine).astype(jnp.float32), key_side)
    key_side = jnp.where((lane >= LSE_COL) & (lane < LSE_COL + 3), 1.0, key_side)
    head_ids = (first_head + jnp.arange(heads, dtype=jnp.int32)).astype(jnp.float32)
    slopes = jnp.exp2(-8.0 * (head_ids + 1.0) / 32)
    parts = jnp.stack(three_parts(slopes), axis=1)
    slope_rows = jnp.pad(jnp.repeat(parts, 2, axis=1), ((0, 0), (SLOPE_COL, LANES - SLOPE_COL - 6)))
    count = whole // block
    held = jnp.max(hot.reshape(count, block, nseg).astype(jnp.float32), axis=1)
    reached = jnp.max(reach.reshape(count, block, nseg).astype(jnp.float32), axis=1)
    ids = jnp.arange(count, dtype=jnp.int32)
    active = (jnp.sum(held[:, None, :] * reached[None, :, :], axis=2) > 0.5) & (ids[None, :] < ids[:, None])

    def packed(flags):
        rank = jnp.cumsum(flags.astype(jnp.int32), axis=1) - 1
        slot = flags[:, :, None] & (rank[:, :, None] == ids[None, None, :])
        listed = jnp.sum(jnp.where(slot, ids[None, :, None], 0), axis=1, dtype=jnp.int32)
        total = jnp.sum(flags.astype(jnp.int32), axis=1, keepdims=True, dtype=jnp.int32)
        return jnp.concatenate([total, listed], axis=1)

    return (
        query_side.astype(jnp.bfloat16),
        key_side.astype(jnp.bfloat16),
        slope_rows.astype(jnp.bfloat16),
        packed(active),
        packed(active.T),
    )


def _masks(block):
    lane = lax.broadcasted_iota(jnp.int32, (block, LANES), 1)
    return [lane < HD, lane >= HD], lane


def forward_kernel(first_block, place, lists, qkv, fq, fk, srow, o, lse, qa, vt, top, acc, *, block, pairs):
    count = qkv.shape[0] // block
    width = pairs * LANES
    heads = 2 * pairs
    halves, lane = _masks(block)
    zero = jnp.zeros((block, LANES), jnp.bfloat16)
    ones = jnp.ones((16, block), jnp.bfloat16)
    row = lax.broadcasted_iota(jnp.int32, (block, block), 0)
    col = lax.broadcasted_iota(jnp.int32, (block, block), 1)
    diagonal = row <= col
    side_blocks = count // 2

    def spot(index):
        return pl.ds(pl.multiple_of(place[index] * block, block), block)

    def canon(index):
        return pl.ds(pl.multiple_of(index * block, block), block)

    def turn(j, _):
        for pair in range(pairs):
            cols = slice(pair * LANES, (pair + 1) * LANES)
            turned = qkv[spot(j), 2 * width + pair * LANES : 2 * width + (pair + 1) * LANES].astype(jnp.float32).T.astype(jnp.bfloat16)
            for side in range(2):
                vt[j, 2 * pair + side] = jnp.concatenate([turned[side * HD : (side + 1) * HD], ones], axis=0)
        return 0

    lax.fori_loop(0, count, turn, 0)

    def step(j, first):
        key_features = fk[canon(j), :]
        keys = [
            jnp.concatenate([qkv[spot(j), width + pair * LANES : width + (pair + 1) * LANES], key_features], axis=1) for pair in range(pairs)
        ]
        scores = [dot_nt(keys[h // 2], qa[h]) for h in range(heads)]
        if first:
            scores = [jnp.where(diagonal, score, -BIG) for score in scores]
        bests = [jnp.max(score, axis=0, keepdims=True) for score in scores]
        if not first:
            olds = [top[h : h + 1, :] for h in range(heads)]
            bests = [jnp.maximum(old, best) for old, best in zip(olds, bests)]
            scales = [jnp.exp(old - best) for old, best in zip(olds, bests)]
        weights = [jnp.exp(score - best).astype(jnp.bfloat16) for score, best in zip(scores, bests)]
        mixed = [dot_nn(vt[j, h], weights[h]) for h in range(heads)]
        for h in range(heads):
            acc[h] = mixed[h] if first else acc[h] * scales[h] + mixed[h]
            top[h : h + 1, :] = bests[h]

    def rows(n, _):
        i = place[first_block[0] + n]
        query_features = fq[canon(i), :]
        for pair in range(pairs):
            cols = slice(pair * LANES, (pair + 1) * LANES)
            queries = qkv[spot(i), cols] * jnp.bfloat16(HD ** -0.5)
            for side in range(2):
                h = 2 * pair + side
                qa[h] = jnp.concatenate(
                    [jnp.where(halves[side], queries, zero), query_features + srow[h : h + 1, :]], axis=1
                )
        step(i, True)

        def other(m, _):
            step(lists[i, m + 1], False)
            return 0

        lax.fori_loop(0, lists[i, 0], other, 0)
        logs = []
        for pair in range(pairs):
            cols = slice(pair * LANES, (pair + 1) * LANES)
            mixed = []
            for h in (2 * pair, 2 * pair + 1):
                total = acc[h, HD : HD + 1, :]
                mixed.append(acc[h, :HD, :] / total)
                logs.append(top[h : h + 1, :] + jnp.log(total))
            o[canon(n), cols] = jnp.concatenate(mixed, axis=0).T.astype(o.dtype)
        logs.append(jnp.zeros((LANES - heads, block), jnp.float32))
        lse[canon(n), :] = jnp.concatenate(logs, axis=0).T
        return 0

    lax.fori_loop(0, o.shape[0] // block, rows, 0)


def backward_kernel(
    place, lists, qkv, do, o_own, o_other, fq, fk, srow, lse_own, lse_other, dqkv, qa, da, dqa, dka, dva, *, block, pairs
):
    count = qkv.shape[0] // block
    width = pairs * LANES
    heads = 2 * pairs
    halves, lane = _masks(block)
    zero = jnp.zeros((block, LANES), jnp.bfloat16)
    row = lax.broadcasted_iota(jnp.int32, (block, block), 0)
    col = lax.broadcasted_iota(jnp.int32, (block, block), 1)
    diagonal = row <= col
    ones = jnp.where(lane < 3, 1.0, 0.0).astype(jnp.bfloat16)
    side_blocks = count // 2

    def spot(index):
        return pl.ds(pl.multiple_of(place[index] * block, block), block)

    def canon(index):
        return pl.ds(pl.multiple_of(index * block, block), block)

    def spread(value, first):
        high, middle, low = three_parts(value)
        spread_out = jnp.where(lane == first, high, 0.0)
        spread_out = jnp.where(lane == first + 1, middle, spread_out)
        return jnp.where(lane == first + 2, low, spread_out).astype(jnp.bfloat16)

    def prepare(i, _):
        query_features = fq[canon(i), :]
        own = place[i] < side_blocks
        mixed_rows = canon(place[i] % side_blocks)
        logs = jnp.where(own, lse_own[mixed_rows, :], lse_other[mixed_rows, :])
        for pair in range(pairs):
            cols = slice(pair * LANES, (pair + 1) * LANES)
            queries = qkv[spot(i), cols] * jnp.bfloat16(HD ** -0.5)
            grads = do[spot(i), cols]
            mixed = jnp.where(own, o_own[mixed_rows, cols], o_other[mixed_rows, cols])
            product = grads.astype(jnp.float32) * mixed.astype(jnp.float32)
            for side in range(2):
                h = 2 * pair + side
                delta = jnp.sum(jnp.where(halves[side], product, 0.0), axis=1, keepdims=True)
                log_total = jnp.sum(jnp.where(lane == h, logs, 0.0), axis=1, keepdims=True)
                features = query_features + srow[h : h + 1, :] + spread(-log_total, LSE_COL)
                qa[h, canon(i), :] = jnp.concatenate([jnp.where(halves[side], queries, zero), features], axis=1)
                da[h, canon(i), :] = jnp.concatenate([jnp.where(halves[side], grads, zero), spread(-delta, 0)], axis=1)
        dqa[i] = jnp.zeros((pairs * LANES, block), jnp.float32)
        return 0

    lax.fori_loop(0, count, prepare, 0)

    def columns(j, _):
        key_features = fk[canon(j), :]
        key_blocks = [qkv[spot(j), width + pair * LANES : width + (pair + 1) * LANES] for pair in range(pairs)]
        keys = [jnp.concatenate([key_block, key_features], axis=1) for key_block in key_blocks]
        values = [
            jnp.concatenate([qkv[spot(j), 2 * width + pair * LANES : 2 * width + (pair + 1) * LANES], ones], axis=1) for pair in range(pairs)
        ]
        turned = [key_block.astype(jnp.float32).T.astype(jnp.bfloat16) for key_block in key_blocks]

        def step(i, first):
            query_rows = [qa[h, canon(i), :] for h in range(heads)]
            grad_rows = [da[h, canon(i), :] for h in range(heads)]
            scores = [dot_nt(keys[h // 2], query_rows[h]) for h in range(heads)]
            slopes = [dot_nt(values[h // 2], grad_rows[h]) for h in range(heads)]
            if first:
                scores = [jnp.where(diagonal, score, -BIG) for score in scores]
            probs = [jnp.exp(score) for score in scores]
            changes = [(prob * slope).astype(jnp.bfloat16) for prob, slope in zip(probs, slopes)]
            probs = [prob.astype(jnp.bfloat16) for prob in probs]
            for pair in range(pairs):
                cols = slice(pair * LANES, (pair + 1) * LANES)
                a, b = 2 * pair, 2 * pair + 1
                value_part = dot_nn(probs[a], grad_rows[a][:, :LANES]) + dot_nn(probs[b], grad_rows[b][:, :LANES])
                key_part = dot_nn(changes[a], query_rows[a][:, :LANES]) + dot_nn(changes[b], query_rows[b][:, :LANES])
                if first:
                    dva[:, cols] = value_part
                    dka[:, cols] = key_part
                else:
                    dva[:, cols] += value_part
                    dka[:, cols] += key_part
                for side in range(2):
                    h = 2 * pair + side
                    part = slice(h * HD, (h + 1) * HD)
                    dqa[i, part, :] += dot_nn(turned[pair][side * HD : (side + 1) * HD], changes[h])

        step(j, True)

        def other(n, _):
            step(lists[j, n + 1], False)
            return 0

        lax.fori_loop(0, lists[j, 0], other, 0)
        dqkv[spot(j), width : 2 * width] = dka[...].astype(dqkv.dtype)
        dqkv[spot(j), 2 * width :] = dva[...].astype(dqkv.dtype)
        return 0

    lax.fori_loop(0, count, columns, 0)

    def finish(i, _):
        dqkv[spot(i), :width] = (dqa[i] * HD ** -0.5).T.astype(dqkv.dtype)
        return 0

    lax.fori_loop(0, count, finish, 0)


def cost(microseconds):
    return pl.CostEstimate(flops=int(microseconds * 1.15e9), bytes_accessed=0, transcendentals=0)


def _attention_call(name, kernel, scalars, arrays, outs, scratch, microseconds):
    vmem = pl.BlockSpec(memory_space=pltpu.VMEM)
    return pl.pallas_call(
        kernel,
        out_shape=outs,
        in_specs=[pl.BlockSpec(memory_space=pltpu.SMEM)] * len(scalars) + [vmem] * len(arrays),
        out_specs=[vmem] * len(outs),
        scratch_shapes=scratch,
        compiler_params=pltpu.CompilerParams(vmem_limit_bytes=VMEM_LIMIT),
        cost_estimate=cost(microseconds),
        name=name,
    )(*scalars, *arrays)


def attention_forward(first_block, count, place, lists, qkv, fq, fk, srow, block):
    whole, width = qkv.shape[0], qkv.shape[1] // 3
    pairs = width // LANES
    return _attention_call(
        "attention_forward",
        partial(forward_kernel, block=block, pairs=pairs),
        (first_block.reshape(1), place, lists),
        (qkv, fq, fk, srow),
        [jax.ShapeDtypeStruct((count * block, width), jnp.bfloat16), jax.ShapeDtypeStruct((count * block, LANES), jnp.float32)],
        [
            pltpu.VMEM((2 * pairs, block, 2 * LANES), jnp.bfloat16),
            pltpu.VMEM((whole // block, 2 * pairs, HD + 16, block), jnp.bfloat16),
            pltpu.VMEM((8, block), jnp.float32),
            pltpu.VMEM((2 * pairs, HD + 16, block), jnp.float32),
        ],
        0,
    )


def attention_backward(place, lists, qkv, do, o, fq, fk, srow, lse, block):
    whole, width = do.shape
    pairs = width // LANES
    return _attention_call(
        "attention_backward",
        partial(backward_kernel, block=block, pairs=pairs),
        (place, lists),
        (qkv, do, *o, fq, fk, srow, *lse),
        [jax.ShapeDtypeStruct((whole, 3 * width), jnp.bfloat16)],
        [
            pltpu.VMEM((2 * pairs, whole, 2 * LANES), jnp.bfloat16),
            pltpu.VMEM((2 * pairs, whole, 2 * LANES), jnp.bfloat16),
            pltpu.VMEM((whole // block, width, block), jnp.float32),
            pltpu.VMEM((block, width), jnp.float32),
            pltpu.VMEM((block, width), jnp.float32),
        ],
        0,
    )[0]


CORE = [(0, 1), (1, 0), (2, 3), (3, 2)]
ACROSS = [(0, 2), (2, 0), (1, 3), (3, 1)]
SWAP = [(0, 1), (1, 0)]
INWARD = [(0, 1), (3, 2)]
MIDDLE = [(1, 2), (2, 1)]
OUTWARD = [(1, 0), (2, 3)]


def low(value):
    return lax.optimization_barrier(value.astype(jnp.bfloat16))


def wide(value):
    return value.astype(jnp.float32)


def core(value):
    return lax.ppermute(value, "tensor", CORE)


def across(value):
    return lax.ppermute(value, "tensor", ACROSS)


def over(value):
    return lax.ppermute(value, "seq", SWAP)


def norm_forward(values, gain, shift):
    center = values - jnp.mean(values, axis=-1, keepdims=True)
    variance = jnp.mean(center * center, axis=-1, keepdims=True)
    inverse = lax.rsqrt(variance + EPS)
    normed = center * inverse
    return (normed * gain + shift, normed, inverse)


def norm_backward(incoming, normed, inverse, gain):
    scaled = incoming * gain
    inner = (
        scaled
        - jnp.mean(scaled, axis=-1, keepdims=True)
        - normed * jnp.mean(scaled * normed, axis=-1, keepdims=True)
    )
    return (inner * inverse, jnp.sum(incoming * normed, axis=0), jnp.sum(incoming, axis=0))


def halves_of(value, axis, which):
    size = value.shape[axis] // 2
    return (
        lax.dynamic_slice_in_dim(value, which * size, size, axis),
        lax.dynamic_slice_in_dim(value, (1 - which) * size, size, axis),
    )


def in_order(own, other, axis, which):
    first = which == 0
    return jnp.concatenate([jnp.where(first, own, other), jnp.where(first, other, own)], axis=axis)


def gather_group(value):
    if lax.axis_size("tensor") == 4:
        beside = core(value)
        far = across(value)
        return (jnp.concatenate([value, beside]), jnp.concatenate([far, core(far)]))
    rows = lax.all_gather(value, "tensor", axis=0, tiled=True)
    return tuple(jnp.split(rows, 2))


def scatter_group(far, near):
    if lax.axis_size("tensor") == 4:
        away = far()
        size = away.shape[0] // 2
        sent = across(low(wide(away[:size]) + wide(core(away[size:]))))
        here = near()
        return wide(here[:size]) + wide(core(here[size:])) + wide(sent)
    away = far()
    here = near()
    return wide(lax.psum_scatter(jnp.concatenate([here, away]), "tensor", scatter_dimension=0, tiled=True))


def gather_slot(value):
    if lax.axis_size("tensor") == 4:
        half = value.shape[0] // 2
        beside = core(value)
        far = across(value)
        past = over(value)
        both = jnp.concatenate([over(far[:half]), across(past[half:])])
        return [jnp.concatenate([piece, other]) for piece, other in
                ((value, beside), (far, core(far)), (past, core(past)), (both, core(both)))]
    own = lax.all_gather(value, "tensor", axis=0, tiled=True)
    return jnp.split(own, 2) + jnp.split(over(own), 2)


def scatter_slot(parts):
    if lax.axis_size("tensor") == 4:
        def chip(part):
            rows = part()
            size = rows.shape[0] // 2
            return wide(rows[:size]) + wide(core(rows[size:]))

        both = low(chip(parts[3]))
        half = both.shape[0] // 2
        both_far = across(both[:half])
        both_past = over(both[half:])
        far = chip(parts[1])
        far_first = across(low(far[:half]))
        past = chip(parts[2])
        past_last = over(low(past[half:]))
        far_last = across(low(far[half:] + wide(both_past)))
        past_first = over(low(past[:half] + wide(both_far)))
        here = chip(parts[0])
        return here + wide(jnp.concatenate([far_first, far_last])) + wide(jnp.concatenate([past_first, past_last]))
    own = lax.psum_scatter(jnp.concatenate([parts[0](), parts[1]()]), "tensor", scatter_dimension=0, tiled=True)
    other = lax.psum_scatter(jnp.concatenate([parts[2](), parts[3]()]), "tensor", scatter_dimension=0, tiled=True)
    return wide(own) + wide(over(other))


def on_line(value, pairs):
    return lax.ppermute(value, "dp", pairs)


def vector_sum(group, pair):
    if lax.axis_size("tensor") == 4 and lax.axis_size("dp") == 4:
        group = group + core(group)
        group = group + across(group)
        rows = jnp.concatenate([group, pair])
        rows = rows + over(rows)
        rows = rows + lax.ppermute(rows, "dp", CORE)
        rows = rows + lax.ppermute(rows, "dp", ACROSS)
        return rows[: group.shape[0]], rows[group.shape[0] :]
    return lax.psum(group, ("dp", "seq", "tensor")), lax.psum(pair, ("dp", "seq"))


def tie(values, after, name):
    count = len(values)
    return pl.pallas_call(
        lambda *refs: None,
        out_shape=[jax.ShapeDtypeStruct(v.shape, v.dtype) for v in values],
        in_specs=[pl.BlockSpec(memory_space=pl.ANY)] * (count + len(after)),
        out_specs=[pl.BlockSpec(memory_space=pl.ANY)] * count,
        input_output_aliases={i: i for i in range(count)},
        compiler_params=pltpu.CompilerParams(vmem_limit_bytes=1 << 16),
        cost_estimate=cost(0),
        name="tie_%d" % name,
    )(*values, *after)


class Order:
    def __init__(self):
        self.after, self.label = [], 999

    def enter(self, *values):
        out = tie(list(values), self.after, self.label)
        self.after = [out[0]]
        return out if len(out) > 1 else out[0]

    def here(self):
        self.token = self.enter(self.token)
        return self.token

    def done(self, *values):
        self.after.extend(values)


def act_gradient(where, pieces, weight, tile=256):
    size, model = pieces[0].shape
    part = weight.shape[0] // 2
    count = len(pieces)
    steps = part // tile

    def kernel(where_ref, *refs):
        weight_ref, out, rows_out = refs[count:]
        block = jnp.concatenate([ref[...] for ref in refs[:count]], axis=0)
        out[...] = dot_nt(block, weight_ref[...]).astype(jnp.bfloat16)

        @pl.when(pl.program_id(0) == 0)
        def _():
            rows_out[...] = block

    return fused(
        "act_gradient", kernel, where, (steps,),
        [(p, p.shape, lambda n, w: (0, 0)) for p in pieces] + [(weight, (tile, model), lambda n, w: (w[0] * steps + n, 0))],
        [
            ((count * size, part), jnp.bfloat16, (count * size, tile), lambda n, w: (0, n)),
            ((count * size, model), jnp.bfloat16, (count * size, model), lambda n, w: (0, 0)),
        ],
    )


def feed_forward(where, pieces, weight, bias, grads, chunk, tile=512):
    size, model = pieces[0].shape
    part = weight.shape[1] // 2
    steps = part // tile
    half = 2 * size

    def kernel(where_ref, first, second, weight_ref, bias_ref, grads_ref, act_ref, up_ref, rows_ref, sums_ref):
        rows = jnp.concatenate([first[...], second[...]], axis=0)
        pre = dot_nn(rows, weight_ref[...]) + wide(bias_ref[...])
        cdf = 0.5 * (1.0 + lax.erf(pre * (0.5**0.5)))
        act_ref[...] = (pre * cdf).astype(jnp.bfloat16)
        slope = cdf + pre * (jnp.exp(-0.5 * pre * pre) * 0.3989422804014327)
        low_grad = (wide(grads_ref[...]) * slope).astype(jnp.bfloat16)
        up_ref[...] = low_grad
        sums_ref[...] = jnp.broadcast_to(jnp.sum(wide(low_grad), axis=0, keepdims=True), sums_ref.shape)

        @pl.when(pl.program_id(0) == 0)
        def _():
            rows_ref[...] = rows

    return fused(
        "feed_forward", kernel, where, (steps,),
        [(p, p.shape, lambda n, w: (0, 0)) for p in pieces]
        + [
            (weight, (model, tile), lambda n, w: (0, w[0] * steps + n)),
            (bias.reshape(1, -1), (1, tile), lambda n, w: (0, w[0] * steps + n)),
            (grads, (half, tile), lambda n, w: (chunk, n)),
        ],
        [
            ((half, part), jnp.bfloat16, (half, tile), lambda n, w: (0, n)),
            ((half, part), jnp.bfloat16, (half, tile), lambda n, w: (0, n)),
            ((half, model), jnp.bfloat16, (half, model), lambda n, w: (0, 0)),
            ((8, part), jnp.float32, (8, tile), lambda n, w: (0, n)),
        ],
    )


def blank(shape):
    return pl.pallas_call(
        lambda out: None,
        out_shape=jax.ShapeDtypeStruct(shape, jnp.float32),
        out_specs=pl.BlockSpec(memory_space=pl.ANY),
        compiler_params=pltpu.CompilerParams(vmem_limit_bytes=1 << 16),
        cost_estimate=cost(0),
        name="blank",
    )()


DOTS = {"nn": dot_nn, "nt": dot_nt, "tn": dot_tn}


def fused(name, kernel, where, grid, operands, outs):
    return pl.pallas_call(
        kernel,
        grid_spec=pltpu.PrefetchScalarGridSpec(
            num_scalar_prefetch=1,
            grid=grid,
            in_specs=[pl.BlockSpec(block, index) for _, block, index in operands],
            out_specs=[pl.BlockSpec(block, index) for _, _, block, index in outs],
        ),
        out_shape=[jax.ShapeDtypeStruct(shape, kind) for shape, kind, _, _ in outs],
        compiler_params=pltpu.CompilerParams(vmem_limit_bytes=MATMUL_LIMIT),
        cost_estimate=cost(0),
        name=name,
    )(where, *[array for array, _, _ in operands])


def matmul(name, kind, where, grid, pairs, outs, axis=0):
    count = len(pairs)

    def kernel(where_ref, *refs):
        total = None
        for left, right in zip(refs[:count], refs[count : 2 * count]):
            part = DOTS[kind](left[...], right[...])
            total = part if total is None else total + part
        start = 0
        for out in refs[2 * count :]:
            size = out.shape[axis]
            piece = total[start : start + size] if axis == 0 else total[:, start : start + size]
            out[...] = piece.astype(jnp.bfloat16)
            start += size

    operands = [left for left, _ in pairs] + [right for _, right in pairs]
    return fused(name, kernel, where, grid, operands, [(shape, jnp.bfloat16, block, index) for shape, block, index in outs])


def plain_local(
    hidden_in, norm1_gain, norm1_bias, query_weight, query_bias, key_weight, value_weight, value_bias, out_weight,
    out_bias, norm2_gain, norm2_bias, up_weight, up_bias, down_weight, down_bias, seg_lengths, parents, out_grad,
):
    local_rows, model = hidden_in.shape
    tensor_count = lax.axis_size("tensor")
    group = local_rows * tensor_count
    whole = 2 * group
    columns = query_weight.shape[1]
    width = columns // 2
    heads = width // HD
    units = up_weight.shape[1]
    seq = lax.axis_index("seq")
    tensor = lax.axis_index("tensor")
    block = 256
    f32 = jnp.float32
    gain_one, gain_two = wide(norm1_gain), wide(norm2_gain)

    inputs = wide(hidden_in)
    first, normed_one, inverse_one = norm_forward(inputs, gain_one, wide(norm1_bias))
    chunks_one = gather_slot(low(first))

    qkv_weight = jnp.concatenate([halves_of(w, 1, seq)[0] for w in (query_weight, key_weight, value_weight)], axis=1)
    qkv_bias = jnp.concatenate(
        [halves_of(query_bias, 0, seq)[0], jnp.zeros((width,), jnp.bfloat16), halves_of(value_bias, 0, seq)[0]]
    )
    out_rel = jnp.concatenate(halves_of(out_weight, 0, seq))
    up_rel = jnp.concatenate(halves_of(up_weight, 1, seq), axis=1)
    up_bias_rel = wide(jnp.concatenate(halves_of(up_bias, 0, seq)))
    down_rel = jnp.concatenate(halves_of(down_weight, 0, seq))

    blocks = jnp.arange(whole // block, dtype=jnp.int32)
    if tensor_count == 4:
        place = blocks ^ (seq * 4 + tensor)
    else:
        side = group // block
        place = ((blocks // side) ^ seq) * side + blocks % side
    fq, fk, slope_rows, key_lists, query_lists = tree_features(
        seg_lengths[0], parents[0], tensor * (columns // HD) + seq * heads, heads, block, whole
    )

    qkv = jnp.concatenate(
        [(jnp.dot(rows, qkv_weight, preferred_element_type=f32) + wide(qkv_bias)).astype(jnp.bfloat16) for rows in chunks_one]
    )
    grad_near, grad_far = gather_group(out_grad)
    side = whole // block // 2
    mixed_other, logs_other = attention_forward(jnp.int32(side), side, place, key_lists, qkv, fq, fk, slope_rows, block)
    mixed_own, logs_own = attention_forward(jnp.int32(0), side, place, key_lists, qkv, fq, fk, slope_rows, block)
    heads_out = jnp.concatenate([mixed_own, over(mixed_other)], axis=1)
    half = group // 2

    def product(left, right):
        return lambda: jnp.dot(left, right, preferred_element_type=f32).astype(jnp.bfloat16)

    def product_nt(left, right):
        return lambda: dot_nt(left, right).astype(jnp.bfloat16)

    def low_dot(left, right):
        return dot_tn(left, right).astype(jnp.bfloat16)

    branch = scatter_group(product(heads_out[half:], out_rel), product(heads_out[:half], out_rel)) + wide(out_bias)
    act_grad_near = low(dot_nt(grad_near, down_rel))
    middle = inputs + branch
    second, normed_two, inverse_two = norm_forward(middle, gain_two, wide(norm2_bias))
    two_near, two_far = gather_group(low(second))
    act_grad_far = low(dot_nt(grad_far, down_rel))
    activated, up_grad = [], []
    for rows, grads in ((two_near, act_grad_near), (two_far, act_grad_far)):
        pre = jnp.dot(rows, up_rel, preferred_element_type=f32) + up_bias_rel
        cdf = 0.5 * (1.0 + lax.erf(pre * (0.5 ** 0.5)))
        activated.append((pre * cdf).astype(jnp.bfloat16))
        slope = cdf + pre * (jnp.exp(-0.5 * pre * pre) * 0.3989422804014327)
        up_grad.append((wide(grads) * slope).astype(jnp.bfloat16))
    act_all = jnp.concatenate(activated)
    up_grad_all = jnp.concatenate(up_grad)
    rows_two = jnp.concatenate([two_near, two_far])
    grad_rows = jnp.concatenate([grad_near, grad_far])
    rows_one = jnp.concatenate(chunks_one)
    part = units // 2
    cotangent = wide(out_grad)

    def down_parts(index):
        cols = slice(index * (model // 2), (index + 1) * (model // 2))
        return low_dot(act_all[:, :part], grad_rows[:, cols]), low_dot(act_all[:, part:], grad_rows[:, cols])

    quarter = model // 4

    def up_parts(index):
        rows = rows_two[:, index * quarter : (index + 1) * quarter]
        return jnp.stack([low_dot(rows, up_grad_all[:, :part]), low_dot(rows, up_grad_all[:, part:])])

    def ffn_sum():
        return scatter_group(product(act_all[half:], down_rel), product(act_all[:half], down_rel)) + wide(down_bias)

    def norm_two(second_grad):
        middle_part, gain_grad, bias_grad = norm_backward(second_grad, normed_two, inverse_two, gain_two)
        return cotangent + middle_part, gain_grad, bias_grad

    def heads_grads(rows):
        return dot_nt(rows, out_rel).astype(jnp.bfloat16)

    def attention_grads(arrived, near_grads):
        return attention_backward(
            place, query_lists, qkv, jnp.concatenate([near_grads, arrived]), (mixed_own, mixed_other),
            fq, fk, slope_rows, (logs_own, logs_other), block,
        )

    def first_grads(grads):
        return scatter_slot([product_nt(grads[i * half : (i + 1) * half], qkv_weight) for i in range(4)])

    def qkv_part(grads, index):
        return low_dot(rows_one, grads[:, index * width : (index + 1) * width])

    second_grad = scatter_group(product_nt(up_grad[1], up_rel), product_nt(up_grad[0], up_rel))
    middle_grad, grad_norm2_gain, grad_norm2_bias = norm_two(second_grad)
    branch_grad = low(middle_grad)
    branch_near, branch_far = gather_group(branch_grad)
    ffn_out = ffn_sum()
    grad_up_bias = jnp.sum(wide(up_grad_all), axis=0)
    heads_grad = jnp.concatenate([heads_grads(branch_near), heads_grads(branch_far)])
    grads = attention_grads(over(heads_grad[:, width:]), heads_grad[:, :width])
    branch_rows = jnp.concatenate([branch_near, branch_far])
    first_grad = first_grads(grads)
    sums = [[*down_parts(0)], [*down_parts(1)], *[[up[0], up[1]] for up in map(up_parts, range(4))]]
    sums.append([low_dot(heads_out[:, :width], branch_rows), low_dot(heads_out[:, width:], branch_rows)])
    axes = [0, 0, 1, 1, 1, 1, 0, 1, 1, 1]
    for i in range(3):
        sums.append([qkv_part(grads, i), jnp.zeros((model, width), jnp.bfloat16)])
    sums = [lax.psum(in_order(own, other, axis, seq), ("dp", "seq")) for (own, other), axis in zip(sums, axes)]

    layer_out = (middle + ffn_out).astype(jnp.bfloat16)
    grad_down_bias = jnp.sum(cotangent, axis=0)
    grad_out_bias = jnp.sum(wide(branch_grad), axis=0)
    bias_sum = jnp.sum(wide(grads), axis=0)
    input_part, grad_norm1_gain, grad_norm1_bias = norm_backward(first_grad, normed_one, inverse_one, gain_one)
    grad_in = (middle_grad + input_part).astype(jnp.bfloat16)

    nothing = jnp.zeros((width,), f32)
    query_bias_row = in_order(bias_sum[:width], nothing, 0, seq)
    value_bias_row = in_order(bias_sum[2 * width :], nothing, 0, seq)
    up_bias_row = in_order(grad_up_bias[:part], grad_up_bias[part:], 0, seq)
    pairs = jnp.concatenate([query_bias_row, value_bias_row, up_bias_row])
    group_rows, pair_rows = vector_sum(
        jnp.stack([grad_norm1_gain, grad_norm1_bias, grad_out_bias, grad_norm2_gain, grad_norm2_bias, grad_down_bias]),
        jnp.pad(pairs, (0, -pairs.shape[0] % model)).reshape(-1, model),
    )
    pair_rows = pair_rows.reshape(-1)

    down = wide(jnp.concatenate(sums[:2], axis=1))
    up = wide(jnp.concatenate(sums[2:6], axis=0))
    out = wide(sums[6])
    qkv_out = [wide(v) for v in sums[7:]]

    return (
        layer_out,
        grad_in,
        group_rows[0],
        group_rows[1],
        qkv_out[0],
        pair_rows[:columns],
        qkv_out[1],
        qkv_out[2],
        pair_rows[columns : 2 * columns],
        out,
        group_rows[2],
        group_rows[3],
        group_rows[4],
        up,
        pair_rows[2 * columns : 2 * columns + units],
        down,
        group_rows[5],
    )


(
    D0, D1, U0, U1, Q0, Q1, Q2, S0, S1, S2, S3, SB, SE, SL, G0, G1, G2, G3, GB, GE, GL, F0, F1, F2, F3, FB, FE, FL, S, G, BN, BF,
    ATT, O, FN, V, d0, d1, u0, u1, q0, q1, q2, o, v,
) = range(45)
D_STEPS, U_STEPS, Q_STEPS = (D0, D1), (U0, U1), (Q0, Q1, Q2)
S_STEPS, G_STEPS, F_STEPS = [S0, S1, S2, S3, SB, SE, SL], [G0, G1, G2, G3, GB, GE, GL], [F0, F1, F2, F3, FB, FE, FL]
D_HOPS, U_HOPS, Q_HOPS, O_HOPS, V_HOPS = (d0, d1), (u0, u1), (q0, q1, q2), o, v
ORDER = (
    S3, U1, SB, S1, S2, SE, SL, D0, S0, u1, S, D1, BN, BF, d0, u1, O, ATT, d0, d1, o, F3, u1, FB, U0, F1, F2, o,
    d0, d1, FE, FL, u1, u0, G3, F0, o, d0, d1, GB, FN, G1, G2, u0, Q0, GE, GL, G0, o, d1, Q1, q0, G, u0, Q2, V,
    q0, q1, v, o, q2, q0, q1, v, u0, q2, q1, v, v, q0, q2, q1, v, q2,
)


def line_steps(mine):
    arrived = yield [on_line(mine, INWARD)], [mine]
    inner = low(wide(mine) + wide(arrived))
    arrived = yield [on_line(inner, MIDDLE)], [inner]
    total = low(wide(inner) + wide(arrived))
    arrived = yield [on_line(total, OUTWARD)], [total]
    line = lax.axis_index("dp")
    total = low(jnp.where((line == 0) | (line == 3), arrived, total))
    arrived = yield [over(total)], [total]
    return total, arrived


def pair_steps(own, other):
    arrived = yield [over(other)], [other, own]
    return (yield from line_steps(low(wide(own) + wide(arrived))))


def vector_steps(group, pair):
    arrived = yield [core(group)], [group]
    group = group + arrived
    arrived = yield [across(group)], [group]
    rows = jnp.concatenate([group + arrived, pair])
    arrived = yield [over(rows)], [rows]
    rows = rows + arrived
    arrived = yield [on_line(rows, CORE)], [rows]
    rows = rows + arrived
    arrived = yield [on_line(rows, ACROSS)], [rows]
    rows = rows + arrived
    return rows[: group.shape[0]], rows[group.shape[0] :]


class Sums:
    def __init__(self, order):
        self.order, self.steps, self.pending, self.results = order, {}, {}, {}

    def start(self, name, steps):
        self.steps[name] = steps
        self.pending[name], sent = next(steps)
        self.order.done(*sent)

    def wait(self, name):
        arrived = self.order.enter(*self.pending[name])
        try:
            self.pending[name], sent = self.steps[name].send(arrived)
            self.order.done(*sent)
        except StopIteration as stop:
            self.results[name] = stop.value


def quick_local(
    hidden_in, norm1_gain, norm1_bias, query_weight, query_bias, key_weight, value_weight, value_bias, out_weight,
    out_bias, norm2_gain, norm2_bias, up_weight, up_bias, down_weight, down_bias, seg_lengths, parents, out_grad,
):
    size, model = hidden_in.shape
    half, group, whole = 2 * size, 4 * size, 8 * size
    columns = query_weight.shape[1]
    width = columns // 2
    heads = width // HD
    units = up_weight.shape[1]
    part = units // 2
    seq, tensor = lax.axis_index("seq"), lax.axis_index("tensor")
    block = size
    f32, bf16 = jnp.float32, jnp.bfloat16
    gain_one, gain_two = wide(norm1_gain), wide(norm2_gain)

    def product(left, right):
        return jnp.dot(left, right, preferred_element_type=f32).astype(bf16)

    def product_nt(left, right):
        return dot_nt(left, right).astype(bf16)

    def whole_block(value):
        return (value, value.shape, lambda n, w: (0, 0))

    order = Order()
    inputs = wide(hidden_in)
    first, normed_one, inverse_one = norm_forward(inputs, gain_one, wide(norm1_bias))
    first = low(first)
    far, past = across(first), over(first)
    order.done(first)
    lengths, parent_ids = order.enter(seg_lengths, parents)
    qkv_weight = jnp.concatenate([halves_of(w, 1, seq)[0] for w in (query_weight, key_weight, value_weight)], axis=1)
    qkv_bias = jnp.concatenate(
        [halves_of(query_bias, 0, seq)[0], jnp.zeros((width,), bf16), halves_of(value_bias, 0, seq)[0]]
    )

    def projected(rows):
        return (jnp.dot(rows, qkv_weight, preferred_element_type=f32) + wide(qkv_bias)).astype(bf16)

    blocks = jnp.arange(whole // block, dtype=jnp.int32)
    place = blocks ^ (seq * 4 + tensor)
    fq, fk, slope_rows, key_lists, query_lists = tree_features(
        lengths[0], parent_ids[0], tensor * (columns // HD) + seq * heads, heads, block, whole
    )
    chunks_one = [jnp.concatenate([first, core(first)])]
    qkv_parts = [projected(chunks_one[0])]
    out_rel = jnp.concatenate(halves_of(out_weight, 0, seq))
    order.done(qkv_parts[0], fk, fq, out_rel)
    far, past = order.enter(far, past)
    both = [over(low(far[: size // 2])), across(low(past[size // 2 :]))]
    for piece in (far, past):
        chunks_one.append(jnp.concatenate([piece, core(piece)]))
        qkv_parts.append(projected(chunks_one[-1]))
        order.done(qkv_parts[-1])
    both = jnp.concatenate(order.enter(*both))
    chunks_one.append(jnp.concatenate([both, core(both)]))
    qkv_parts.append(projected(chunks_one[-1]))
    qkv = jnp.concatenate(qkv_parts)

    order.done(qkv)
    grad_piece = order.enter(out_grad)
    grad_far, grad_past = across(grad_piece), over(grad_piece)
    side = whole // block // 2

    def attend(first_block, count, place_now):
        mixed, logs = attention_forward(jnp.int32(first_block), count, place_now, key_lists, qkv, fq, fk, slope_rows, block)
        order.done(mixed)
        return mixed, logs

    mixed_other, logs_other = attend(side, side, place)
    far_part = attend(side // 2, side - side // 2, order.enter(place))
    mixed_past = over(mixed_other)
    place_now, grad_far, grad_past = order.enter(place, grad_far, grad_past)
    grad_both = [over(low(grad_far[: size // 2])), across(low(grad_past[size // 2 :]))]
    near_part = attend(0, side // 2, place_now)
    mixed_own, logs_own = (jnp.concatenate(pair) for pair in zip(near_part, far_part))
    mixed_past, *grad_both = order.enter(mixed_past, *grad_both)
    heads_out = jnp.concatenate([mixed_own, mixed_past], axis=1)
    branch_far = product(heads_out[half:], out_rel)
    branch_sent = low(wide(branch_far[:size]) + wide(core(branch_far[size:])))
    branch_back = across(branch_sent)
    branch_near = product(heads_out[:half], out_rel)
    order.done(branch_near, branch_sent)

    where = seq.reshape(1)
    grad_far = order.enter(grad_far)
    pieces = [grad_piece, core(grad_piece), grad_far, core(grad_far)]
    act_grad, grad_rows = ([v] for v in act_gradient(where, pieces, down_weight))
    order.done(act_grad[0])
    branch_back = order.enter(branch_back)
    branch = wide(branch_near[:size]) + wide(core(branch_near[size:])) + wide(branch_back)
    middle = inputs + branch + wide(out_bias)
    second, normed_two, inverse_two = norm_forward(middle, gain_two, wide(norm2_bias))
    second = low(second)
    second_core, second_far, second_past = core(second), across(second), over(second)
    order.done(second)
    act, up_grad, rows_two, up_sums = [], [], [], []

    def feed(pieces, chunk):
        out = feed_forward(where, pieces, up_weight, up_bias, act_grad[chunk // 2], chunk % 2)
        for held, value in zip((act, up_grad, rows_two, up_sums), out):
            held.append(value)
        order.done(out[0])

    second_core = order.enter(second_core)
    feed((second, second_core), 0)
    grad_both = jnp.concatenate(grad_both)
    pieces = [grad_past, core(grad_past), grad_both, core(grad_both)]
    for held, value in zip((act_grad, grad_rows), act_gradient(where, pieces, down_weight)):
        held.append(value)
    order.done(act_grad[1])
    second_far, second_past = order.enter(second_far, second_past)
    second_both = [over(low(second_far[: size // 2])), across(low(second_past[size // 2 :]))]
    feed((second_far, core(second_far)), 1)
    feed((second_past, core(second_past)), 2)
    second_both = jnp.concatenate(order.enter(*second_both))
    feed((second_both, core(second_both)), 3)
    cotangent = wide(out_grad)

    sums = Sums(order)
    order.token = where
    state = {}
    order.done(*act, *up_grad)

    parts = 2
    cols = model // parts

    def start_down(index):
        pairs = [
            (
                (act[c], (half, part // 2), lambda m, w: (0, m)),
                (grad_rows[c // 2], (half, cols), lambda m, w, c=c: (c % 2, index)),
            )
            for c in range(4)
        ]
        out = ((part, cols), (part // 2, cols), lambda m, w: (m, 0))
        sums.start(D_HOPS[index], line_steps(*matmul("down_part", "tn", order.here(), (2,), pairs, [out])))

    def start_up(index):
        pairs = [
            (
                (rows_two[c], (half, cols // 2), lambda m, w: (0, 2 * index + m)),
                (up_grad[c], (half, part), lambda m, w: (0, 0)),
            )
            for c in range(4)
        ]
        out = ((cols, part), (cols // 2, part), lambda m, w: (m, 0))
        sums.start(U_HOPS[index], line_steps(*matmul("up_part", "tn", order.here(), (2,), pairs, [out])))

    def scatter_steps(name, kind, source, right, tile):
        def rows(chunk):
            own, other = matmul(
                name, kind, order.here(), (model // tile,), [(source(chunk), right)],
                [((size, model), (size, tile), lambda n, w: (0, n))] * 2,
            )
            state[name, chunk] = own, core(other)
            order.done(own)

        def total(chunk):
            own, other = state[name, chunk]
            return wide(own) + wide(other)

        def send(key, transfer, value):
            sent = low(value)
            state[name, key] = transfer(sent)
            order.done(sent)

        def both():
            send("both", across, total(3))

        def far():
            send("far", across, total(1))

        def past():
            send("past", over, total(2) + wide(order.enter(state[name, "both"])))

        def own_rows():
            far, past = order.enter(state[name, "far"], state[name, "past"])
            return total(0) + wide(far) + wide(past)

        return [partial(rows, i) for i in range(4)] + [both, far, past], own_rows

    tile = 512

    def second_norm():
        incoming = second_rows()
        inner, gain_grad, bias_grad = norm_backward(incoming, normed_two, inverse_two, gain_two)
        middle_grad = cotangent + inner
        branch_grad = low(middle_grad)
        state["middle_grad"], state["norm2"] = middle_grad, (gain_grad, bias_grad)
        state["dy"] = [branch_grad, core(branch_grad)]
        state["dy_back"] = across(branch_grad)
        order.done(branch_grad)

    def heads_rows(pieces):
        rows = jnp.concatenate(pieces)
        return matmul(
            "heads_gradient", "nt", order.here(), (1,),
            [(whole_block(rows), whole_block(out_rel))],
            [((half, width), (half, width), lambda n, w: (0, 0))] * 2, 1,
        )

    def heads_near():
        state["do_near"] = heads_rows(state["dy"])
        order.done(state["do_near"][0])

    def heads_far():
        back = order.enter(state["dy_back"])
        state["dy"] += [back, core(back)]
        far = heads_rows(state["dy"][2:])
        state["do_own"], sent = (low(jnp.concatenate(pair)) for pair in zip(state["do_near"], far))
        state["do_past"] = over(sent)
        order.done(state["do_own"], sent)

    def attention():
        rows_one = jnp.concatenate(order.enter(*chunks_one))
        state["rows_one"] = rows_one
        order.done(rows_one)
        rows = jnp.concatenate([state["do_own"], order.enter(state["do_past"])])
        state["grads"] = attention_backward(
            place, query_lists, qkv, rows, (mixed_own, mixed_other), fq, fk, slope_rows, (logs_own, logs_other), block
        )
        order.done(state["grads"])

    def layer_end():
        state["layer_out"] = (middle + ffn_rows() + wide(down_bias)).astype(bf16)
        order.done(state["layer_out"])

    def start_out():
        rows = jnp.concatenate(state["dy"])
        here = order.here()
        halves = [
            matmul(
                "out_part", "tn", here, (2,),
                [(whole_block(v), (rows, (group, model // 2), lambda n, w: (0, n)))],
                [((width, model), (width, model // 2), lambda n, w: (0, n))],
            )[0]
            for v in (mixed_own, mixed_past)
        ]
        sums.start(O_HOPS, pair_steps(*halves))

    def first_norm():
        incoming = first_rows()
        inner, gain_grad, bias_grad = norm_backward(incoming, normed_one, inverse_one, gain_one)
        state["grad_in"] = (state["middle_grad"] + inner).astype(bf16)
        state["norm1"] = gain_grad, bias_grad
        order.done(state["grad_in"])

    def start_qkv(index):
        grads = state["grads"]
        size_of = 3 * width // projection_parts
        (value,) = matmul(
            "projection_part", "tn", order.here(), (4,),
            [((state["rows_one"], (whole, model // 4), lambda m, w: (0, m)), (grads, (whole, size_of), lambda m, w: (0, index)))],
            [((model, size_of), (model // 4, size_of), lambda m, w: (m, 0))],
        )
        sums.start(Q_HOPS[index], line_steps(value))

    projection_parts = sum(step in ORDER for step in Q_STEPS)
    second_steps, second_rows = scatter_steps(
        "second_gradient", "nt", lambda c: whole_block(up_grad[c]), (up_weight, (tile, part), lambda n, w: (n, w[0])), tile
    )
    ffn_steps, ffn_rows = scatter_steps(
        "feed_back", "nn", lambda c: whole_block(act[c]), (down_weight, (part, tile), lambda n, w: (w[0], n)), tile
    )
    first_steps, first_rows = scatter_steps(
        "first_gradient", "nt", lambda c: (state["grads"], (half, 3 * width), lambda n, w: (c, 0)), (qkv_weight, (2 * tile, 3 * width), lambda n, w: (n, 0)), 2 * tile
    )
    def start_vectors():
        bias_sum = jnp.sum(wide(state["grads"]), axis=0)
        nothing = jnp.zeros((width,), f32)
        pairs = jnp.concatenate(
            [
                in_order(bias_sum[:width], nothing, 0, seq),
                in_order(bias_sum[2 * width :], nothing, 0, seq),
                in_order(sum(s[0] for s in up_sums), jnp.zeros((part,), f32), 0, seq),
            ]
        )
        grad_out_bias = jnp.sum(wide(state["dy"][0]), axis=0)
        grad_down_bias = jnp.sum(cotangent, axis=0)
        group_rows = jnp.stack([*state["norm1"], grad_out_bias, *state["norm2"], grad_down_bias])
        sums.start(V_HOPS, vector_steps(group_rows, jnp.pad(pairs, (0, -pairs.shape[0] % model)).reshape(-1, model)))

    steps = dict(zip(S_STEPS + G_STEPS + F_STEPS, second_steps + ffn_steps + first_steps))
    steps |= {S: second_norm, G: layer_end, BN: heads_near, BF: heads_far, ATT: attention, O: start_out, FN: first_norm, V: start_vectors}
    for i in range(3):
        steps[Q_STEPS[i]] = partial(start_qkv, i)
    for i in range(parts):
        steps[D_STEPS[i]], steps[U_STEPS[i]] = partial(start_down, i), partial(start_up, i)
    for step in ORDER:
        order.label = step
        if step in steps:
            steps[step]()
        else:
            sums.wait(step)

    group_rows, pair_rows = sums.results[V_HOPS]
    pair_rows = pair_rows.reshape(-1)

    def put(out, value, row, column):
        return lax.dynamic_update_slice(out, wide(value), (row, column))

    up, down = blank((model, units)), blank((units, model))
    for i in range(parts):
        own, other = sums.results[U_HOPS[i]]
        up = put(put(up, own, i * cols, seq * part), other, i * cols, (1 - seq) * part)
        own, other = sums.results[D_HOPS[i]]
        down = put(put(down, own, seq * part, i * cols), other, (1 - seq) * part, i * cols)
    out = blank((columns, model))
    own, other = sums.results[O_HOPS]
    out = put(put(out, own, seq * width, 0), other, (1 - seq) * width, 0)
    own, other = (
        jnp.concatenate([sums.results[Q_HOPS[i]][j] for i in range(projection_parts)], axis=1) for j in range(2)
    )
    projections = []
    for i in range(3):
        cols = slice(i * width, (i + 1) * width)
        projection = put(blank((model, columns)), own[:, cols], 0, seq * width)
        projections.append(put(projection, other[:, cols], 0, (1 - seq) * width))
    return (
        state["layer_out"],
        state["grad_in"],
        group_rows[0],
        group_rows[1],
        projections[0],
        pair_rows[:columns],
        projections[1],
        projections[2],
        pair_rows[columns : 2 * columns],
        out,
        group_rows[2],
        group_rows[3],
        group_rows[4],
        up,
        pair_rows[2 * columns : 2 * columns + units],
        down,
        group_rows[5],
    )


def local(*args):
    quick = lax.axis_size("tensor") == 4 and lax.axis_size("dp") == 4 and args[0].shape[0] == 256
    return quick_local(*args) if quick else plain_local(*args)


def solution(mesh):
    placed = (
        P(("dp", "seq", "tensor"), None),
        P(),
        P(),
        P(None, "tensor"),
        P("tensor"),
        P(None, "tensor"),
        P(None, "tensor"),
        P("tensor"),
        P("tensor", None),
        P(),
        P(),
        P(),
        P(None, "tensor"),
        P("tensor"),
        P("tensor", None),
        P(),
        P("dp", None),
        P("dp", None),
        P(("dp", "seq", "tensor"), None),
    )
    return jax.shard_map(
        local,
        mesh=mesh,
        in_specs=placed,
        out_specs=(
            P(("dp", "seq", "tensor"), None),
            P(("dp", "seq", "tensor"), None),
            P(),
            P(),
            P(None, "tensor"),
            P("tensor"),
            P(None, "tensor"),
            P(None, "tensor"),
            P("tensor"),
            P("tensor", None),
            P(),
            P(),
            P(),
            P(None, "tensor"),
            P("tensor"),
            P("tensor", None),
            P(),
        ),
        check_vma=False,
    )
```

```python
from functools import partial

import jax
import jax.numpy as jnp
from jax import lax
from jax.experimental import pallas as pl
from jax.experimental.pallas import tpu as pltpu
from jax.sharding import PartitionSpec as P

HEADS = 32
EPS = 1e-05
HD = 64
LANES = 128
BIG = 2.0 ** 100
SLOPE_COL = 16
LSE_COL = 24
VMEM_LIMIT = 36 * 1024 * 1024
MATMUL_LIMIT = 26 * 1024 * 1024


def dot_nt(left, right):
    return lax.dot_general(left, right, (((1,), (1,)), ((), ())), preferred_element_type=jnp.float32)


def dot_tn(left, right):
    return lax.dot_general(left, right, (((0,), (0,)), ((), ())), preferred_element_type=jnp.float32)


def dot_nn(left, right):
    return lax.dot_general(left, right, (((1,), (0,)), ((), ())), preferred_element_type=jnp.float32)


def three_parts(value):
    high = value.astype(jnp.bfloat16).astype(jnp.float32)
    rest = value - high
    middle = rest.astype(jnp.bfloat16).astype(jnp.float32)
    return high, middle, rest - middle


def tree_features(lengths, parent_ids, first_head, heads, block, whole):
    nseg = lengths.shape[0]
    seg_ids = jnp.arange(nseg, dtype=jnp.int32)
    ends = jnp.cumsum(lengths, dtype=jnp.int32)
    starts = ends - lengths
    parents = jnp.where(seg_ids > 0, parent_ids, 0)
    own = seg_ids[:, None] == seg_ids[None, :]
    ancestor = own | (parents[:, None] == seg_ids[None, :]) | (seg_ids[None, :] == 0)
    above = (ancestor & ~own).astype(jnp.int32)
    path_start = jnp.sum(above * lengths[None, :], axis=1, dtype=jnp.int32)
    token = jnp.arange(whole, dtype=jnp.int32)[:, None]
    hot = (token >= starts[None, :]) & (token < ends[None, :])
    depth = token + jnp.sum(jnp.where(hot, (path_start - starts)[None, :], 0), axis=1, keepdims=True)
    reach = jnp.sum(jnp.where(hot[:, None, :] & ancestor[None, :, :], 1, 0), axis=2)
    lane = jnp.arange(LANES, dtype=jnp.int32)[None, :]
    pad = ((0, 0), (0, LANES - nseg))
    query_side = jnp.pad(hot.astype(jnp.float32), pad)
    key_side = jnp.pad(jnp.where(reach > 0, 0.0, -BIG), pad)
    digit = lane - SLOPE_COL
    coarse = (depth // 256) * 256
    fine = depth - coarse
    in_slope = (digit >= 0) & (digit < 6)
    key_side = jnp.where(in_slope, jnp.where(digit % 2 == 0, coarse, fine).astype(jnp.float32), key_side)
    key_side = jnp.where((lane >= LSE_COL) & (lane < LSE_COL + 3), 1.0, key_side)
    head_ids = (first_head + jnp.arange(heads, dtype=jnp.int32)).astype(jnp.float32)
    slopes = jnp.exp2(-8.0 * (head_ids + 1.0) / 32)
    parts = jnp.stack(three_parts(slopes), axis=1)
    slope_rows = jnp.pad(jnp.repeat(parts, 2, axis=1), ((0, 0), (SLOPE_COL, LANES - SLOPE_COL - 6)))
    count = whole // block
    held = jnp.max(hot.reshape(count, block, nseg).astype(jnp.float32), axis=1)
    reached = jnp.max(reach.reshape(count, block, nseg).astype(jnp.float32), axis=1)
    ids = jnp.arange(count, dtype=jnp.int32)
    active = (jnp.sum(held[:, None, :] * reached[None, :, :], axis=2) > 0.5) & (ids[None, :] < ids[:, None])

    def packed(flags):
        rank = jnp.cumsum(flags.astype(jnp.int32), axis=1) - 1
        slot = flags[:, :, None] & (rank[:, :, None] == ids[None, None, :])
        listed = jnp.sum(jnp.where(slot, ids[None, :, None], 0), axis=1, dtype=jnp.int32)
        total = jnp.sum(flags.astype(jnp.int32), axis=1, keepdims=True, dtype=jnp.int32)
        return jnp.concatenate([total, listed], axis=1)

    return (
        query_side.astype(jnp.bfloat16),
        key_side.astype(jnp.bfloat16),
        slope_rows.astype(jnp.bfloat16),
        packed(active),
        packed(active.T),
    )


def _masks(block):
    lane = lax.broadcasted_iota(jnp.int32, (block, LANES), 1)
    return [lane < HD, lane >= HD], lane


def forward_kernel(first_block, place, lists, qkv, fq, fk, srow, o, lse, qa, vt, top, acc, *, block, pairs):
    count = qkv.shape[0] // block
    width = pairs * LANES
    heads = 2 * pairs
    halves, lane = _masks(block)
    zero = jnp.zeros((block, LANES), jnp.bfloat16)
    ones = jnp.ones((16, block), jnp.bfloat16)
    row = lax.broadcasted_iota(jnp.int32, (block, block), 0)
    col = lax.broadcasted_iota(jnp.int32, (block, block), 1)
    diagonal = row <= col
    side_blocks = count // 2

    def spot(index):
        return pl.ds(pl.multiple_of(place[index] * block, block), block)

    def canon(index):
        return pl.ds(pl.multiple_of(index * block, block), block)

    def turn(j, _):
        for pair in range(pairs):
            cols = slice(pair * LANES, (pair + 1) * LANES)
            turned = qkv[spot(j), 2 * width + pair * LANES : 2 * width + (pair + 1) * LANES].astype(jnp.float32).T.astype(jnp.bfloat16)
            for side in range(2):
                vt[j, 2 * pair + side] = jnp.concatenate([turned[side * HD : (side + 1) * HD], ones], axis=0)
        return 0

    lax.fori_loop(0, count, turn, 0)

    def step(j, first):
        key_features = fk[canon(j), :]
        keys = [
            jnp.concatenate([qkv[spot(j), width + pair * LANES : width + (pair + 1) * LANES], key_features], axis=1) for pair in range(pairs)
        ]
        scores = [dot_nt(keys[h // 2], qa[h]) for h in range(heads)]
        if first:
            scores = [jnp.where(diagonal, score, -BIG) for score in scores]
        bests = [jnp.max(score, axis=0, keepdims=True) for score in scores]
        if not first:
            olds = [top[h : h + 1, :] for h in range(heads)]
            bests = [jnp.maximum(old, best) for old, best in zip(olds, bests)]
            scales = [jnp.exp(old - best) for old, best in zip(olds, bests)]
        weights = [jnp.exp(score - best).astype(jnp.bfloat16) for score, best in zip(scores, bests)]
        mixed = [dot_nn(vt[j, h], weights[h]) for h in range(heads)]
        for h in range(heads):
            acc[h] = mixed[h] if first else acc[h] * scales[h] + mixed[h]
            top[h : h + 1, :] = bests[h]

    def rows(n, _):
        i = place[first_block[0] + n]
        query_features = fq[canon(i), :]
        for pair in range(pairs):
            cols = slice(pair * LANES, (pair + 1) * LANES)
            queries = qkv[spot(i), cols] * jnp.bfloat16(HD ** -0.5)
            for side in range(2):
                h = 2 * pair + side
                qa[h] = jnp.concatenate(
                    [jnp.where(halves[side], queries, zero), query_features + srow[h : h + 1, :]], axis=1
                )
        step(i, True)

        def other(m, _):
            step(lists[i, m + 1], False)
            return 0

        lax.fori_loop(0, lists[i, 0], other, 0)
        logs = []
        for pair in range(pairs):
            cols = slice(pair * LANES, (pair + 1) * LANES)
            mixed = []
            for h in (2 * pair, 2 * pair + 1):
                total = acc[h, HD : HD + 1, :]
                mixed.append(acc[h, :HD, :] / total)
                logs.append(top[h : h + 1, :] + jnp.log(total))
            o[canon(n), cols] = jnp.concatenate(mixed, axis=0).T.astype(o.dtype)
        logs.append(jnp.zeros((LANES - heads, block), jnp.float32))
        lse[canon(n), :] = jnp.concatenate(logs, axis=0).T
        return 0

    lax.fori_loop(0, o.shape[0] // block, rows, 0)


def backward_kernel(
    place, lists, qkv, do, o_own, o_other, fq, fk, srow, lse_own, lse_other, dqkv, qa, da, dqa, dka, dva, *, block, pairs
):
    count = qkv.shape[0] // block
    width = pairs * LANES
    heads = 2 * pairs
    halves, lane = _masks(block)
    zero = jnp.zeros((block, LANES), jnp.bfloat16)
    row = lax.broadcasted_iota(jnp.int32, (block, block), 0)
    col = lax.broadcasted_iota(jnp.int32, (block, block), 1)
    diagonal = row <= col
    ones = jnp.where(lane < 3, 1.0, 0.0).astype(jnp.bfloat16)
    side_blocks = count // 2

    def spot(index):
        return pl.ds(pl.multiple_of(place[index] * block, block), block)

    def canon(index):
        return pl.ds(pl.multiple_of(index * block, block), block)

    def spread(value, first):
        high, middle, low = three_parts(value)
        spread_out = jnp.where(lane == first, high, 0.0)
        spread_out = jnp.where(lane == first + 1, middle, spread_out)
        return jnp.where(lane == first + 2, low, spread_out).astype(jnp.bfloat16)

    def prepare(i, _):
        query_features = fq[canon(i), :]
        own = place[i] < side_blocks
        mixed_rows = canon(place[i] % side_blocks)
        logs = jnp.where(own, lse_own[mixed_rows, :], lse_other[mixed_rows, :])
        for pair in range(pairs):
            cols = slice(pair * LANES, (pair + 1) * LANES)
            queries = qkv[spot(i), cols] * jnp.bfloat16(HD ** -0.5)
            grads = do[spot(i), cols]
            mixed = jnp.where(own, o_own[mixed_rows, cols], o_other[mixed_rows, cols])
            product = grads.astype(jnp.float32) * mixed.astype(jnp.float32)
            for side in range(2):
                h = 2 * pair + side
                delta = jnp.sum(jnp.where(halves[side], product, 0.0), axis=1, keepdims=True)
                log_total = jnp.sum(jnp.where(lane == h, logs, 0.0), axis=1, keepdims=True)
                features = query_features + srow[h : h + 1, :] + spread(-log_total, LSE_COL)
                qa[h, canon(i), :] = jnp.concatenate([jnp.where(halves[side], queries, zero), features], axis=1)
                da[h, canon(i), :] = jnp.concatenate([jnp.where(halves[side], grads, zero), spread(-delta, 0)], axis=1)
        dqa[i] = jnp.zeros((pairs * LANES, block), jnp.float32)
        return 0

    lax.fori_loop(0, count, prepare, 0)

    def columns(j, _):
        key_features = fk[canon(j), :]
        key_blocks = [qkv[spot(j), width + pair * LANES : width + (pair + 1) * LANES] for pair in range(pairs)]
        keys = [jnp.concatenate([key_block, key_features], axis=1) for key_block in key_blocks]
        values = [
            jnp.concatenate([qkv[spot(j), 2 * width + pair * LANES : 2 * width + (pair + 1) * LANES], ones], axis=1) for pair in range(pairs)
        ]
        turned = [key_block.astype(jnp.float32).T.astype(jnp.bfloat16) for key_block in key_blocks]

        def step(i, first):
            query_rows = [qa[h, canon(i), :] for h in range(heads)]
            grad_rows = [da[h, canon(i), :] for h in range(heads)]
            scores = [dot_nt(keys[h // 2], query_rows[h]) for h in range(heads)]
            slopes = [dot_nt(values[h // 2], grad_rows[h]) for h in range(heads)]
            if first:
                scores = [jnp.where(diagonal, score, -BIG) for score in scores]
            probs = [jnp.exp(score) for score in scores]
            changes = [(prob * slope).astype(jnp.bfloat16) for prob, slope in zip(probs, slopes)]
            probs = [prob.astype(jnp.bfloat16) for prob in probs]
            for pair in range(pairs):
                cols = slice(pair * LANES, (pair + 1) * LANES)
                a, b = 2 * pair, 2 * pair + 1
                value_part = dot_nn(probs[a], grad_rows[a][:, :LANES]) + dot_nn(probs[b], grad_rows[b][:, :LANES])
                key_part = dot_nn(changes[a], query_rows[a][:, :LANES]) + dot_nn(changes[b], query_rows[b][:, :LANES])
                if first:
                    dva[:, cols] = value_part
                    dka[:, cols] = key_part
                else:
                    dva[:, cols] += value_part
                    dka[:, cols] += key_part
                for side in range(2):
                    h = 2 * pair + side
                    part = slice(h * HD, (h + 1) * HD)
                    dqa[i, part, :] += dot_nn(turned[pair][side * HD : (side + 1) * HD], changes[h])

        step(j, True)

        def other(n, _):
            step(lists[j, n + 1], False)
            return 0

        lax.fori_loop(0, lists[j, 0], other, 0)
        dqkv[spot(j), width : 2 * width] = dka[...].astype(dqkv.dtype)
        dqkv[spot(j), 2 * width :] = dva[...].astype(dqkv.dtype)
        return 0

    lax.fori_loop(0, count, columns, 0)

    def finish(i, _):
        dqkv[spot(i), :width] = (dqa[i] * HD ** -0.5).T.astype(dqkv.dtype)
        return 0

    lax.fori_loop(0, count, finish, 0)


def cost(microseconds):
    return pl.CostEstimate(flops=int(microseconds * 1.15e9), bytes_accessed=0, transcendentals=0)


def _attention_call(name, kernel, scalars, arrays, outs, scratch, microseconds):
    vmem = pl.BlockSpec(memory_space=pltpu.VMEM)
    return pl.pallas_call(
        kernel,
        out_shape=outs,
        in_specs=[pl.BlockSpec(memory_space=pltpu.SMEM)] * len(scalars) + [vmem] * len(arrays),
        out_specs=[vmem] * len(outs),
        scratch_shapes=scratch,
        compiler_params=pltpu.CompilerParams(vmem_limit_bytes=VMEM_LIMIT),
        cost_estimate=cost(microseconds),
        name=name,
    )(*scalars, *arrays)


def attention_forward(first_block, count, place, lists, qkv, fq, fk, srow, block):
    whole, width = qkv.shape[0], qkv.shape[1] // 3
    pairs = width // LANES
    return _attention_call(
        "attention_forward",
        partial(forward_kernel, block=block, pairs=pairs),
        (first_block.reshape(1), place, lists),
        (qkv, fq, fk, srow),
        [jax.ShapeDtypeStruct((count * block, width), jnp.bfloat16), jax.ShapeDtypeStruct((count * block, LANES), jnp.float32)],
        [
            pltpu.VMEM((2 * pairs, block, 2 * LANES), jnp.bfloat16),
            pltpu.VMEM((whole // block, 2 * pairs, HD + 16, block), jnp.bfloat16),
            pltpu.VMEM((8, block), jnp.float32),
            pltpu.VMEM((2 * pairs, HD + 16, block), jnp.float32),
        ],
        0,
    )


def attention_backward(place, lists, qkv, do, o, fq, fk, srow, lse, block):
    whole, width = do.shape
    pairs = width // LANES
    return _attention_call(
        "attention_backward",
        partial(backward_kernel, block=block, pairs=pairs),
        (place, lists),
        (qkv, do, *o, fq, fk, srow, *lse),
        [jax.ShapeDtypeStruct((whole, 3 * width), jnp.bfloat16)],
        [
            pltpu.VMEM((2 * pairs, whole, 2 * LANES), jnp.bfloat16),
            pltpu.VMEM((2 * pairs, whole, 2 * LANES), jnp.bfloat16),
            pltpu.VMEM((whole // block, width, block), jnp.float32),
            pltpu.VMEM((block, width), jnp.float32),
            pltpu.VMEM((block, width), jnp.float32),
        ],
        0,
    )[0]


CORE = [(0, 1), (1, 0), (2, 3), (3, 2)]
ACROSS = [(0, 2), (2, 0), (1, 3), (3, 1)]
SWAP = [(0, 1), (1, 0)]
INWARD = [(0, 1), (3, 2)]
MIDDLE = [(1, 2), (2, 1)]
OUTWARD = [(1, 0), (2, 3)]


def low(value):
    return lax.optimization_barrier(value.astype(jnp.bfloat16))


def wide(value):
    return value.astype(jnp.float32)


def core(value):
    return lax.ppermute(value, "tensor", CORE)


def across(value):
    return lax.ppermute(value, "tensor", ACROSS)


def over(value):
    return lax.ppermute(value, "seq", SWAP)


def norm_forward(values, gain, shift):
    center = values - jnp.mean(values, axis=-1, keepdims=True)
    variance = jnp.mean(center * center, axis=-1, keepdims=True)
    inverse = lax.rsqrt(variance + EPS)
    normed = center * inverse
    return (normed * gain + shift, normed, inverse)


def norm_backward(incoming, normed, inverse, gain):
    scaled = incoming * gain
    inner = (
        scaled
        - jnp.mean(scaled, axis=-1, keepdims=True)
        - normed * jnp.mean(scaled * normed, axis=-1, keepdims=True)
    )
    return (inner * inverse, jnp.sum(incoming * normed, axis=0), jnp.sum(incoming, axis=0))


def halves_of(value, axis, which):
    size = value.shape[axis] // 2
    return (
        lax.dynamic_slice_in_dim(value, which * size, size, axis),
        lax.dynamic_slice_in_dim(value, (1 - which) * size, size, axis),
    )


def in_order(own, other, axis, which):
    first = which == 0
    return jnp.concatenate([jnp.where(first, own, other), jnp.where(first, other, own)], axis=axis)


def gather_group(value):
    if lax.axis_size("tensor") == 4:
        beside = core(value)
        far = across(value)
        return (jnp.concatenate([value, beside]), jnp.concatenate([far, core(far)]))
    rows = lax.all_gather(value, "tensor", axis=0, tiled=True)
    return tuple(jnp.split(rows, 2))


def scatter_group(far, near):
    if lax.axis_size("tensor") == 4:
        away = far()
        size = away.shape[0] // 2
        sent = across(low(wide(away[:size]) + wide(core(away[size:]))))
        here = near()
        return wide(here[:size]) + wide(core(here[size:])) + wide(sent)
    away = far()
    here = near()
    return wide(lax.psum_scatter(jnp.concatenate([here, away]), "tensor", scatter_dimension=0, tiled=True))


def gather_slot(value):
    if lax.axis_size("tensor") == 4:
        half = value.shape[0] // 2
        beside = core(value)
        far = across(value)
        past = over(value)
        both = jnp.concatenate([over(far[:half]), across(past[half:])])
        return [jnp.concatenate([piece, other]) for piece, other in
                ((value, beside), (far, core(far)), (past, core(past)), (both, core(both)))]
    own = lax.all_gather(value, "tensor", axis=0, tiled=True)
    return jnp.split(own, 2) + jnp.split(over(own), 2)


def scatter_slot(parts):
    if lax.axis_size("tensor") == 4:
        def chip(part):
            rows = part()
            size = rows.shape[0] // 2
            return wide(rows[:size]) + wide(core(rows[size:]))

        both = low(chip(parts[3]))
        half = both.shape[0] // 2
        both_far = across(both[:half])
        both_past = over(both[half:])
        far = chip(parts[1])
        far_first = across(low(far[:half]))
        past = chip(parts[2])
        past_last = over(low(past[half:]))
        far_last = across(low(far[half:] + wide(both_past)))
        past_first = over(low(past[:half] + wide(both_far)))
        here = chip(parts[0])
        return here + wide(jnp.concatenate([far_first, far_last])) + wide(jnp.concatenate([past_first, past_last]))
    own = lax.psum_scatter(jnp.concatenate([parts[0](), parts[1]()]), "tensor", scatter_dimension=0, tiled=True)
    other = lax.psum_scatter(jnp.concatenate([parts[2](), parts[3]()]), "tensor", scatter_dimension=0, tiled=True)
    return wide(own) + wide(over(other))


def on_line(value, pairs):
    return lax.ppermute(value, "dp", pairs)


def vector_sum(group, pair):
    if lax.axis_size("tensor") == 4 and lax.axis_size("dp") == 4:
        group = group + core(group)
        group = group + across(group)
        rows = jnp.concatenate([group, pair])
        rows = rows + over(rows)
        rows = rows + lax.ppermute(rows, "dp", CORE)
        rows = rows + lax.ppermute(rows, "dp", ACROSS)
        return rows[: group.shape[0]], rows[group.shape[0] :]
    return lax.psum(group, ("dp", "seq", "tensor")), lax.psum(pair, ("dp", "seq"))


def tie(values, after, name):
    count = len(values)
    return pl.pallas_call(
        lambda *refs: None,
        out_shape=[jax.ShapeDtypeStruct(v.shape, v.dtype) for v in values],
        in_specs=[pl.BlockSpec(memory_space=pl.ANY)] * (count + len(after)),
        out_specs=[pl.BlockSpec(memory_space=pl.ANY)] * count,
        input_output_aliases={i: i for i in range(count)},
        compiler_params=pltpu.CompilerParams(vmem_limit_bytes=1 << 16),
        cost_estimate=cost(0),
        name="tie_%d" % name,
    )(*values, *after)


class Order:
    def __init__(self):
        self.after, self.label = [], 999

    def enter(self, *values):
        out = tie(list(values), self.after, self.label)
        self.after = [out[0]]
        return out if len(out) > 1 else out[0]

    def here(self):
        self.token = self.enter(self.token)
        return self.token

    def done(self, *values):
        self.after.extend(values)


def act_gradient(where, pieces, weight, tile=256):
    size, model = pieces[0].shape
    part = weight.shape[0] // 2
    count = len(pieces)
    steps = part // tile

    def kernel(where_ref, *refs):
        weight_ref, out, rows_out = refs[count:]
        block = jnp.concatenate([ref[...] for ref in refs[:count]], axis=0)
        out[...] = dot_nt(block, weight_ref[...]).astype(jnp.bfloat16)

        @pl.when(pl.program_id(0) == 0)
        def _():
            rows_out[...] = block

    return fused(
        "act_gradient", kernel, where, (steps,),
        [(p, p.shape, lambda n, w: (0, 0)) for p in pieces] + [(weight, (tile, model), lambda n, w: (w[0] * steps + n, 0))],
        [
            ((count * size, part), jnp.bfloat16, (count * size, tile), lambda n, w: (0, n)),
            ((count * size, model), jnp.bfloat16, (count * size, model), lambda n, w: (0, 0)),
        ],
    )


def feed_forward(where, pieces, weight, bias, grads, chunk, tile=512):
    size, model = pieces[0].shape
    part = weight.shape[1] // 2
    steps = part // tile
    half = 2 * size

    def kernel(where_ref, first, second, weight_ref, bias_ref, grads_ref, act_ref, up_ref, rows_ref, sums_ref):
        rows = jnp.concatenate([first[...], second[...]], axis=0)
        pre = dot_nn(rows, weight_ref[...]) + wide(bias_ref[...])
        cdf = 0.5 * (1.0 + lax.erf(pre * (0.5**0.5)))
        act_ref[...] = (pre * cdf).astype(jnp.bfloat16)
        slope = cdf + pre * (jnp.exp(-0.5 * pre * pre) * 0.3989422804014327)
        low_grad = (wide(grads_ref[...]) * slope).astype(jnp.bfloat16)
        up_ref[...] = low_grad
        sums_ref[...] = jnp.broadcast_to(jnp.sum(wide(low_grad), axis=0, keepdims=True), sums_ref.shape)

        @pl.when(pl.program_id(0) == 0)
        def _():
            rows_ref[...] = rows

    return fused(
        "feed_forward", kernel, where, (steps,),
        [(p, p.shape, lambda n, w: (0, 0)) for p in pieces]
        + [
            (weight, (model, tile), lambda n, w: (0, w[0] * steps + n)),
            (bias.reshape(1, -1), (1, tile), lambda n, w: (0, w[0] * steps + n)),
            (grads, (half, tile), lambda n, w: (chunk, n)),
        ],
        [
            ((half, part), jnp.bfloat16, (half, tile), lambda n, w: (0, n)),
            ((half, part), jnp.bfloat16, (half, tile), lambda n, w: (0, n)),
            ((half, model), jnp.bfloat16, (half, model), lambda n, w: (0, 0)),
            ((8, part), jnp.float32, (8, tile), lambda n, w: (0, n)),
        ],
    )


def blank(shape):
    return pl.pallas_call(
        lambda out: None,
        out_shape=jax.ShapeDtypeStruct(shape, jnp.float32),
        out_specs=pl.BlockSpec(memory_space=pl.ANY),
        compiler_params=pltpu.CompilerParams(vmem_limit_bytes=1 << 16),
        cost_estimate=cost(0),
        name="blank",
    )()


DOTS = {"nn": dot_nn, "nt": dot_nt, "tn": dot_tn}


def fused(name, kernel, where, grid, operands, outs):
    return pl.pallas_call(
        kernel,
        grid_spec=pltpu.PrefetchScalarGridSpec(
            num_scalar_prefetch=1,
            grid=grid,
            in_specs=[pl.BlockSpec(block, index) for _, block, index in operands],
            out_specs=[pl.BlockSpec(block, index) for _, _, block, index in outs],
        ),
        out_shape=[jax.ShapeDtypeStruct(shape, kind) for shape, kind, _, _ in outs],
        compiler_params=pltpu.CompilerParams(vmem_limit_bytes=MATMUL_LIMIT),
        cost_estimate=cost(0),
        name=name,
    )(where, *[array for array, _, _ in operands])


def matmul(name, kind, where, grid, pairs, outs, axis=0):
    count = len(pairs)

    def kernel(where_ref, *refs):
        total = None
        for left, right in zip(refs[:count], refs[count : 2 * count]):
            part = DOTS[kind](left[...], right[...])
            total = part if total is None else total + part
        start = 0
        for out in refs[2 * count :]:
            size = out.shape[axis]
            piece = total[start : start + size] if axis == 0 else total[:, start : start + size]
            out[...] = piece.astype(jnp.bfloat16)
            start += size

    operands = [left for left, _ in pairs] + [right for _, right in pairs]
    return fused(name, kernel, where, grid, operands, [(shape, jnp.bfloat16, block, index) for shape, block, index in outs])


def plain_local(
    hidden_in, norm1_gain, norm1_bias, query_weight, query_bias, key_weight, value_weight, value_bias, out_weight,
    out_bias, norm2_gain, norm2_bias, up_weight, up_bias, down_weight, down_bias, seg_lengths, parents, out_grad,
):
    local_rows, model = hidden_in.shape
    tensor_count = lax.axis_size("tensor")
    group = local_rows * tensor_count
    whole = 2 * group
    columns = query_weight.shape[1]
    width = columns // 2
    heads = width // HD
    units = up_weight.shape[1]
    seq = lax.axis_index("seq")
    tensor = lax.axis_index("tensor")
    block = 256
    f32 = jnp.float32
    gain_one, gain_two = wide(norm1_gain), wide(norm2_gain)

    inputs = wide(hidden_in)
    first, normed_one, inverse_one = norm_forward(inputs, gain_one, wide(norm1_bias))
    chunks_one = gather_slot(low(first))

    qkv_weight = jnp.concatenate([halves_of(w, 1, seq)[0] for w in (query_weight, key_weight, value_weight)], axis=1)
    qkv_bias = jnp.concatenate(
        [halves_of(query_bias, 0, seq)[0], jnp.zeros((width,), jnp.bfloat16), halves_of(value_bias, 0, seq)[0]]
    )
    out_rel = jnp.concatenate(halves_of(out_weight, 0, seq))
    up_rel = jnp.concatenate(halves_of(up_weight, 1, seq), axis=1)
    up_bias_rel = wide(jnp.concatenate(halves_of(up_bias, 0, seq)))
    down_rel = jnp.concatenate(halves_of(down_weight, 0, seq))

    blocks = jnp.arange(whole // block, dtype=jnp.int32)
    if tensor_count == 4:
        place = blocks ^ (seq * 4 + tensor)
    else:
        side = group // block
        place = ((blocks // side) ^ seq) * side + blocks % side
    fq, fk, slope_rows, key_lists, query_lists = tree_features(
        seg_lengths[0], parents[0], tensor * (columns // HD) + seq * heads, heads, block, whole
    )

    qkv = jnp.concatenate(
        [(jnp.dot(rows, qkv_weight, preferred_element_type=f32) + wide(qkv_bias)).astype(jnp.bfloat16) for rows in chunks_one]
    )
    grad_near, grad_far = gather_group(out_grad)
    side = whole // block // 2
    mixed_other, logs_other = attention_forward(jnp.int32(side), side, place, key_lists, qkv, fq, fk, slope_rows, block)
    mixed_own, logs_own = attention_forward(jnp.int32(0), side, place, key_lists, qkv, fq, fk, slope_rows, block)
    heads_out = jnp.concatenate([mixed_own, over(mixed_other)], axis=1)
    half = group // 2

    def product(left, right):
        return lambda: jnp.dot(left, right, preferred_element_type=f32).astype(jnp.bfloat16)

    def product_nt(left, right):
        return lambda: dot_nt(left, right).astype(jnp.bfloat16)

    def low_dot(left, right):
        return dot_tn(left, right).astype(jnp.bfloat16)

    branch = scatter_group(product(heads_out[half:], out_rel), product(heads_out[:half], out_rel)) + wide(out_bias)
    act_grad_near = low(dot_nt(grad_near, down_rel))
    middle = inputs + branch
    second, normed_two, inverse_two = norm_forward(middle, gain_two, wide(norm2_bias))
    two_near, two_far = gather_group(low(second))
    act_grad_far = low(dot_nt(grad_far, down_rel))
    activated, up_grad = [], []
    for rows, grads in ((two_near, act_grad_near), (two_far, act_grad_far)):
        pre = jnp.dot(rows, up_rel, preferred_element_type=f32) + up_bias_rel
        cdf = 0.5 * (1.0 + lax.erf(pre * (0.5 ** 0.5)))
        activated.append((pre * cdf).astype(jnp.bfloat16))
        slope = cdf + pre * (jnp.exp(-0.5 * pre * pre) * 0.3989422804014327)
        up_grad.append((wide(grads) * slope).astype(jnp.bfloat16))
    act_all = jnp.concatenate(activated)
    up_grad_all = jnp.concatenate(up_grad)
    rows_two = jnp.concatenate([two_near, two_far])
    grad_rows = jnp.concatenate([grad_near, grad_far])
    rows_one = jnp.concatenate(chunks_one)
    part = units // 2
    cotangent = wide(out_grad)

    def down_parts(index):
        cols = slice(index * (model // 2), (index + 1) * (model // 2))
        return low_dot(act_all[:, :part], grad_rows[:, cols]), low_dot(act_all[:, part:], grad_rows[:, cols])

    quarter = model // 4

    def up_parts(index):
        rows = rows_two[:, index * quarter : (index + 1) * quarter]
        return jnp.stack([low_dot(rows, up_grad_all[:, :part]), low_dot(rows, up_grad_all[:, part:])])

    def ffn_sum():
        return scatter_group(product(act_all[half:], down_rel), product(act_all[:half], down_rel)) + wide(down_bias)

    def norm_two(second_grad):
        middle_part, gain_grad, bias_grad = norm_backward(second_grad, normed_two, inverse_two, gain_two)
        return cotangent + middle_part, gain_grad, bias_grad

    def heads_grads(rows):
        return dot_nt(rows, out_rel).astype(jnp.bfloat16)

    def attention_grads(arrived, near_grads):
        return attention_backward(
            place, query_lists, qkv, jnp.concatenate([near_grads, arrived]), (mixed_own, mixed_other),
            fq, fk, slope_rows, (logs_own, logs_other), block,
        )

    def first_grads(grads):
        return scatter_slot([product_nt(grads[i * half : (i + 1) * half], qkv_weight) for i in range(4)])

    def qkv_part(grads, index):
        return low_dot(rows_one, grads[:, index * width : (index + 1) * width])

    second_grad = scatter_group(product_nt(up_grad[1], up_rel), product_nt(up_grad[0], up_rel))
    middle_grad, grad_norm2_gain, grad_norm2_bias = norm_two(second_grad)
    branch_grad = low(middle_grad)
    branch_near, branch_far = gather_group(branch_grad)
    ffn_out = ffn_sum()
    grad_up_bias = jnp.sum(wide(up_grad_all), axis=0)
    heads_grad = jnp.concatenate([heads_grads(branch_near), heads_grads(branch_far)])
    grads = attention_grads(over(heads_grad[:, width:]), heads_grad[:, :width])
    branch_rows = jnp.concatenate([branch_near, branch_far])
    first_grad = first_grads(grads)
    sums = [[*down_parts(0)], [*down_parts(1)], *[[up[0], up[1]] for up in map(up_parts, range(4))]]
    sums.append([low_dot(heads_out[:, :width], branch_rows), low_dot(heads_out[:, width:], branch_rows)])
    axes = [0, 0, 1, 1, 1, 1, 0, 1, 1, 1]
    for i in range(3):
        sums.append([qkv_part(grads, i), jnp.zeros((model, width), jnp.bfloat16)])
    sums = [lax.psum(in_order(own, other, axis, seq), ("dp", "seq")) for (own, other), axis in zip(sums, axes)]

    layer_out = (middle + ffn_out).astype(jnp.bfloat16)
    grad_down_bias = jnp.sum(cotangent, axis=0)
    grad_out_bias = jnp.sum(wide(branch_grad), axis=0)
    bias_sum = jnp.sum(wide(grads), axis=0)
    input_part, grad_norm1_gain, grad_norm1_bias = norm_backward(first_grad, normed_one, inverse_one, gain_one)
    grad_in = (middle_grad + input_part).astype(jnp.bfloat16)

    nothing = jnp.zeros((width,), f32)
    query_bias_row = in_order(bias_sum[:width], nothing, 0, seq)
    value_bias_row = in_order(bias_sum[2 * width :], nothing, 0, seq)
    up_bias_row = in_order(grad_up_bias[:part], grad_up_bias[part:], 0, seq)
    pairs = jnp.concatenate([query_bias_row, value_bias_row, up_bias_row])
    group_rows, pair_rows = vector_sum(
        jnp.stack([grad_norm1_gain, grad_norm1_bias, grad_out_bias, grad_norm2_gain, grad_norm2_bias, grad_down_bias]),
        jnp.pad(pairs, (0, -pairs.shape[0] % model)).reshape(-1, model),
    )
    pair_rows = pair_rows.reshape(-1)

    down = wide(jnp.concatenate(sums[:2], axis=1))
    up = wide(jnp.concatenate(sums[2:6], axis=0))
    out = wide(sums[6])
    qkv_out = [wide(v) for v in sums[7:]]

    return (
        layer_out,
        grad_in,
        group_rows[0],
        group_rows[1],
        qkv_out[0],
        pair_rows[:columns],
        qkv_out[1],
        qkv_out[2],
        pair_rows[columns : 2 * columns],
        out,
        group_rows[2],
        group_rows[3],
        group_rows[4],
        up,
        pair_rows[2 * columns : 2 * columns + units],
        down,
        group_rows[5],
    )


(
    D0, D1, U0, U1, Q0, Q1, Q2, S0, S1, S2, S3, SB, SE, SL, G0, G1, G2, G3, GB, GE, GL, F0, F1, F2, F3, FB, FE, FL, S, G, BN, BF,
    ATT, O, FN, V, d0, d1, u0, u1, q0, q1, q2, o, v,
) = range(45)
D_STEPS, U_STEPS, Q_STEPS = (D0, D1), (U0, U1), (Q0, Q1, Q2)
S_STEPS, G_STEPS, F_STEPS = [S0, S1, S2, S3, SB, SE, SL], [G0, G1, G2, G3, GB, GE, GL], [F0, F1, F2, F3, FB, FE, FL]
D_HOPS, U_HOPS, Q_HOPS, O_HOPS, V_HOPS = (d0, d1), (u0, u1), (q0, q1, q2), o, v
ORDER = (
    S3, U1, SB, S1, S2, SE, SL, D0, S0, u1, S, D1, BN, BF, d0, u1, O, ATT, d1, o, d0, u1, U0, o, d1, d0, u1, u0,
    o, d1, Q0, d0, F3, u0, FB, F1, o, F2, q0, FE, d1, FL, Q2, F0, u0, o, Q1, q0, FN, q2, q0, q1, q2, V, u0, v,
    q1, q2, G3, v, q0, GB, G1, G2, q1, q2, GE, GL, v, G0, v, q1, v, G,
)


def line_steps(mine):
    arrived = yield [on_line(mine, INWARD)], [mine]
    inner = low(wide(mine) + wide(arrived))
    arrived = yield [on_line(inner, MIDDLE)], [inner]
    total = low(wide(inner) + wide(arrived))
    arrived = yield [on_line(total, OUTWARD)], [total]
    line = lax.axis_index("dp")
    total = low(jnp.where((line == 0) | (line == 3), arrived, total))
    arrived = yield [over(total)], [total]
    return total, arrived


def pair_steps(own, other):
    arrived = yield [over(other)], [other, own]
    return (yield from line_steps(low(wide(own) + wide(arrived))))


def vector_steps(group, pair):
    arrived = yield [core(group)], [group]
    group = group + arrived
    arrived = yield [across(group)], [group]
    rows = jnp.concatenate([group + arrived, pair])
    arrived = yield [over(rows)], [rows]
    rows = rows + arrived
    arrived = yield [on_line(rows, CORE)], [rows]
    rows = rows + arrived
    arrived = yield [on_line(rows, ACROSS)], [rows]
    rows = rows + arrived
    return rows[: group.shape[0]], rows[group.shape[0] :]


class Sums:
    def __init__(self, order):
        self.order, self.steps, self.pending, self.results = order, {}, {}, {}

    def start(self, name, steps):
        self.steps[name] = steps
        self.pending[name], sent = next(steps)
        self.order.done(*sent)

    def wait(self, name):
        arrived = self.order.enter(*self.pending[name])
        try:
            self.pending[name], sent = self.steps[name].send(arrived)
            self.order.done(*sent)
        except StopIteration as stop:
            self.results[name] = stop.value


def quick_local(
    hidden_in, norm1_gain, norm1_bias, query_weight, query_bias, key_weight, value_weight, value_bias, out_weight,
    out_bias, norm2_gain, norm2_bias, up_weight, up_bias, down_weight, down_bias, seg_lengths, parents, out_grad,
):
    size, model = hidden_in.shape
    half, group, whole = 2 * size, 4 * size, 8 * size
    columns = query_weight.shape[1]
    width = columns // 2
    heads = width // HD
    units = up_weight.shape[1]
    part = units // 2
    seq, tensor = lax.axis_index("seq"), lax.axis_index("tensor")
    block = size
    f32, bf16 = jnp.float32, jnp.bfloat16
    gain_one, gain_two = wide(norm1_gain), wide(norm2_gain)

    def product(left, right):
        return jnp.dot(left, right, preferred_element_type=f32).astype(bf16)

    def product_nt(left, right):
        return dot_nt(left, right).astype(bf16)

    def whole_block(value):
        return (value, value.shape, lambda n, w: (0, 0))

    order = Order()
    inputs = wide(hidden_in)
    first, normed_one, inverse_one = norm_forward(inputs, gain_one, wide(norm1_bias))
    first = low(first)
    far, past = across(first), over(first)
    order.done(first)
    lengths, parent_ids = order.enter(seg_lengths, parents)
    qkv_weight = jnp.concatenate([halves_of(w, 1, seq)[0] for w in (query_weight, key_weight, value_weight)], axis=1)
    qkv_bias = jnp.concatenate(
        [halves_of(query_bias, 0, seq)[0], jnp.zeros((width,), bf16), halves_of(value_bias, 0, seq)[0]]
    )

    def projected(rows):
        return (jnp.dot(rows, qkv_weight, preferred_element_type=f32) + wide(qkv_bias)).astype(bf16)

    blocks = jnp.arange(whole // block, dtype=jnp.int32)
    place = blocks ^ (seq * 4 + tensor)
    fq, fk, slope_rows, key_lists, query_lists = tree_features(
        lengths[0], parent_ids[0], tensor * (columns // HD) + seq * heads, heads, block, whole
    )
    chunks_one = [jnp.concatenate([first, core(first)])]
    qkv_parts = [projected(chunks_one[0])]
    out_rel = jnp.concatenate(halves_of(out_weight, 0, seq))
    order.done(qkv_parts[0], fk, fq, out_rel)
    far, past = order.enter(far, past)
    both = [over(low(far[: size // 2])), across(low(past[size // 2 :]))]
    for piece in (far, past):
        chunks_one.append(jnp.concatenate([piece, core(piece)]))
        qkv_parts.append(projected(chunks_one[-1]))
        order.done(qkv_parts[-1])
    both = jnp.concatenate(order.enter(*both))
    chunks_one.append(jnp.concatenate([both, core(both)]))
    qkv_parts.append(projected(chunks_one[-1]))
    qkv = jnp.concatenate(qkv_parts)

    order.done(qkv)
    grad_piece = order.enter(out_grad)
    grad_far, grad_past = across(grad_piece), over(grad_piece)
    side = whole // block // 2

    def attend(first_block, count, place_now):
        mixed, logs = attention_forward(jnp.int32(first_block), count, place_now, key_lists, qkv, fq, fk, slope_rows, block)
        order.done(mixed)
        return mixed, logs

    mixed_other, logs_other = attend(side, side, place)
    far_part = attend(side // 2, side - side // 2, order.enter(place))
    mixed_past = over(mixed_other)
    place_now, grad_far, grad_past = order.enter(place, grad_far, grad_past)
    grad_both = [over(low(grad_far[: size // 2])), across(low(grad_past[size // 2 :]))]
    near_part = attend(0, side // 2, place_now)
    mixed_own, logs_own = (jnp.concatenate(pair) for pair in zip(near_part, far_part))
    mixed_past, *grad_both = order.enter(mixed_past, *grad_both)
    heads_out = jnp.concatenate([mixed_own, mixed_past], axis=1)
    branch_far = product(heads_out[half:], out_rel)
    branch_sent = low(wide(branch_far[:size]) + wide(core(branch_far[size:])))
    branch_back = across(branch_sent)
    branch_near = product(heads_out[:half], out_rel)
    order.done(branch_near, branch_sent)

    where = seq.reshape(1)
    grad_far = order.enter(grad_far)
    pieces = [grad_piece, core(grad_piece), grad_far, core(grad_far)]
    act_grad, grad_rows = ([v] for v in act_gradient(where, pieces, down_weight))
    order.done(act_grad[0])
    branch_back = order.enter(branch_back)
    branch = wide(branch_near[:size]) + wide(core(branch_near[size:])) + wide(branch_back)
    middle = inputs + branch + wide(out_bias)
    second, normed_two, inverse_two = norm_forward(middle, gain_two, wide(norm2_bias))
    second = low(second)
    second_core, second_far, second_past = core(second), across(second), over(second)
    order.done(second)
    act, up_grad, rows_two, up_sums = [], [], [], []

    def feed(pieces, chunk):
        out = feed_forward(where, pieces, up_weight, up_bias, act_grad[chunk // 2], chunk % 2)
        for held, value in zip((act, up_grad, rows_two, up_sums), out):
            held.append(value)
        order.done(out[0])

    second_core = order.enter(second_core)
    feed((second, second_core), 0)
    grad_both = jnp.concatenate(grad_both)
    pieces = [grad_past, core(grad_past), grad_both, core(grad_both)]
    for held, value in zip((act_grad, grad_rows), act_gradient(where, pieces, down_weight)):
        held.append(value)
    order.done(act_grad[1])
    second_far, second_past = order.enter(second_far, second_past)
    second_both = [over(low(second_far[: size // 2])), across(low(second_past[size // 2 :]))]
    feed((second_far, core(second_far)), 1)
    feed((second_past, core(second_past)), 2)
    second_both = jnp.concatenate(order.enter(*second_both))
    feed((second_both, core(second_both)), 3)
    cotangent = wide(out_grad)

    sums = Sums(order)
    order.token = where
    state = {}
    order.done(*act, *up_grad)

    parts = 2
    cols = model // parts

    def start_down(index):
        pairs = [
            (
                (act[c], (half, part // 2), lambda m, w: (0, m)),
                (grad_rows[c // 2], (half, cols), lambda m, w, c=c: (c % 2, index)),
            )
            for c in range(4)
        ]
        out = ((part, cols), (part // 2, cols), lambda m, w: (m, 0))
        sums.start(D_HOPS[index], line_steps(*matmul("down_part", "tn", order.here(), (2,), pairs, [out])))

    def start_up(index):
        pairs = [
            (
                (rows_two[c], (half, cols // 2), lambda m, w: (0, 2 * index + m)),
                (up_grad[c], (half, part), lambda m, w: (0, 0)),
            )
            for c in range(4)
        ]
        out = ((cols, part), (cols // 2, part), lambda m, w: (m, 0))
        sums.start(U_HOPS[index], line_steps(*matmul("up_part", "tn", order.here(), (2,), pairs, [out])))

    def scatter_steps(name, kind, source, right, tile):
        def rows(chunk):
            own, other = matmul(
                name, kind, order.here(), (model // tile,), [(source(chunk), right)],
                [((size, model), (size, tile), lambda n, w: (0, n))] * 2,
            )
            state[name, chunk] = own, core(other)
            order.done(own)

        def total(chunk):
            own, other = state[name, chunk]
            return wide(own) + wide(other)

        def send(key, transfer, value):
            sent = low(value)
            state[name, key] = transfer(sent)
            order.done(sent)

        def both():
            send("both", across, total(3))

        def far():
            send("far", across, total(1))

        def past():
            send("past", over, total(2) + wide(order.enter(state[name, "both"])))

        def own_rows():
            far, past = order.enter(state[name, "far"], state[name, "past"])
            return total(0) + wide(far) + wide(past)

        return [partial(rows, i) for i in range(4)] + [both, far, past], own_rows

    tile = 512

    def second_norm():
        incoming = second_rows()
        inner, gain_grad, bias_grad = norm_backward(incoming, normed_two, inverse_two, gain_two)
        middle_grad = cotangent + inner
        branch_grad = low(middle_grad)
        state["middle_grad"], state["norm2"] = middle_grad, (gain_grad, bias_grad)
        state["dy"] = [branch_grad, core(branch_grad)]
        state["dy_back"] = across(branch_grad)
        order.done(branch_grad)

    def heads_rows(pieces):
        rows = jnp.concatenate(pieces)
        return matmul(
            "heads_gradient", "nt", order.here(), (1,),
            [(whole_block(rows), whole_block(out_rel))],
            [((half, width), (half, width), lambda n, w: (0, 0))] * 2, 1,
        )

    def heads_near():
        state["do_near"] = heads_rows(state["dy"])
        order.done(state["do_near"][0])

    def heads_far():
        back = order.enter(state["dy_back"])
        state["dy"] += [back, core(back)]
        far = heads_rows(state["dy"][2:])
        state["do_own"], sent = (low(jnp.concatenate(pair)) for pair in zip(state["do_near"], far))
        state["do_past"] = over(sent)
        order.done(state["do_own"], sent)

    def attention():
        rows_one = jnp.concatenate(order.enter(*chunks_one))
        state["rows_one"] = rows_one
        order.done(rows_one)
        rows = jnp.concatenate([state["do_own"], order.enter(state["do_past"])])
        state["grads"] = attention_backward(
            place, query_lists, qkv, rows, (mixed_own, mixed_other), fq, fk, slope_rows, (logs_own, logs_other), block
        )
        order.done(state["grads"])

    def layer_end():
        state["layer_out"] = (middle + ffn_rows() + wide(down_bias)).astype(bf16)
        order.done(state["layer_out"])

    def start_out():
        rows = jnp.concatenate(state["dy"])
        here = order.here()
        halves = [
            matmul(
                "out_part", "tn", here, (2,),
                [(whole_block(v), (rows, (group, model // 2), lambda n, w: (0, n)))],
                [((width, model), (width, model // 2), lambda n, w: (0, n))],
            )[0]
            for v in (mixed_own, mixed_past)
        ]
        sums.start(O_HOPS, pair_steps(*halves))

    def first_norm():
        incoming = first_rows()
        inner, gain_grad, bias_grad = norm_backward(incoming, normed_one, inverse_one, gain_one)
        state["grad_in"] = (state["middle_grad"] + inner).astype(bf16)
        state["norm1"] = gain_grad, bias_grad
        order.done(state["grad_in"])

    def start_qkv(index):
        grads = state["grads"]
        size_of = 3 * width // projection_parts
        (value,) = matmul(
            "projection_part", "tn", order.here(), (4,),
            [((state["rows_one"], (whole, model // 4), lambda m, w: (0, m)), (grads, (whole, size_of), lambda m, w: (0, index)))],
            [((model, size_of), (model // 4, size_of), lambda m, w: (m, 0))],
        )
        sums.start(Q_HOPS[index], line_steps(value))

    projection_parts = sum(step in ORDER for step in Q_STEPS)
    second_steps, second_rows = scatter_steps(
        "second_gradient", "nt", lambda c: whole_block(up_grad[c]), (up_weight, (tile, part), lambda n, w: (n, w[0])), tile
    )
    ffn_steps, ffn_rows = scatter_steps(
        "feed_back", "nn", lambda c: whole_block(act[c]), (down_weight, (part, tile), lambda n, w: (w[0], n)), tile
    )
    first_steps, first_rows = scatter_steps(
        "first_gradient", "nt", lambda c: (state["grads"], (half, 3 * width), lambda n, w: (c, 0)), (qkv_weight, (2 * tile, 3 * width), lambda n, w: (n, 0)), 2 * tile
    )
    def start_vectors():
        bias_sum = jnp.sum(wide(state["grads"]), axis=0)
        nothing = jnp.zeros((width,), f32)
        pairs = jnp.concatenate(
            [
                in_order(bias_sum[:width], nothing, 0, seq),
                in_order(bias_sum[2 * width :], nothing, 0, seq),
                in_order(sum(s[0] for s in up_sums), jnp.zeros((part,), f32), 0, seq),
            ]
        )
        grad_out_bias = jnp.sum(wide(state["dy"][0]), axis=0)
        grad_down_bias = jnp.sum(cotangent, axis=0)
        group_rows = jnp.stack([*state["norm1"], grad_out_bias, *state["norm2"], grad_down_bias])
        sums.start(V_HOPS, vector_steps(group_rows, jnp.pad(pairs, (0, -pairs.shape[0] % model)).reshape(-1, model)))

    steps = dict(zip(S_STEPS + G_STEPS + F_STEPS, second_steps + ffn_steps + first_steps))
    steps |= {S: second_norm, G: layer_end, BN: heads_near, BF: heads_far, ATT: attention, O: start_out, FN: first_norm, V: start_vectors}
    for i in range(3):
        steps[Q_STEPS[i]] = partial(start_qkv, i)
    for i in range(parts):
        steps[D_STEPS[i]], steps[U_STEPS[i]] = partial(start_down, i), partial(start_up, i)
    for step in ORDER:
        order.label = step
        if step in steps:
            steps[step]()
        else:
            sums.wait(step)

    group_rows, pair_rows = sums.results[V_HOPS]
    pair_rows = pair_rows.reshape(-1)

    def put(out, value, row, column):
        return lax.dynamic_update_slice(out, wide(value), (row, column))

    up, down = blank((model, units)), blank((units, model))
    for i in range(parts):
        own, other = sums.results[U_HOPS[i]]
        up = put(put(up, own, i * cols, seq * part), other, i * cols, (1 - seq) * part)
        own, other = sums.results[D_HOPS[i]]
        down = put(put(down, own, seq * part, i * cols), other, (1 - seq) * part, i * cols)
    out = blank((columns, model))
    own, other = sums.results[O_HOPS]
    out = put(put(out, own, seq * width, 0), other, (1 - seq) * width, 0)
    own, other = (
        jnp.concatenate([sums.results[Q_HOPS[i]][j] for i in range(projection_parts)], axis=1) for j in range(2)
    )
    projections = []
    for i in range(3):
        cols = slice(i * width, (i + 1) * width)
        projection = put(blank((model, columns)), own[:, cols], 0, seq * width)
        projections.append(put(projection, other[:, cols], 0, (1 - seq) * width))
    return (
        state["layer_out"],
        state["grad_in"],
        group_rows[0],
        group_rows[1],
        projections[0],
        pair_rows[:columns],
        projections[1],
        projections[2],
        pair_rows[columns : 2 * columns],
        out,
        group_rows[2],
        group_rows[3],
        group_rows[4],
        up,
        pair_rows[2 * columns : 2 * columns + units],
        down,
        group_rows[5],
    )


def local(*args):
    quick = lax.axis_size("tensor") == 4 and lax.axis_size("dp") == 4 and args[0].shape[0] == 256
    return quick_local(*args) if quick else plain_local(*args)


def solution(mesh):
    placed = (
        P(("dp", "seq", "tensor"), None),
        P(),
        P(),
        P(None, "tensor"),
        P("tensor"),
        P(None, "tensor"),
        P(None, "tensor"),
        P("tensor"),
        P("tensor", None),
        P(),
        P(),
        P(),
        P(None, "tensor"),
        P("tensor"),
        P("tensor", None),
        P(),
        P("dp", None),
        P("dp", None),
        P(("dp", "seq", "tensor"), None),
    )
    return jax.shard_map(
        local,
        mesh=mesh,
        in_specs=placed,
        out_specs=(
            P(("dp", "seq", "tensor"), None),
            P(("dp", "seq", "tensor"), None),
            P(),
            P(),
            P(None, "tensor"),
            P("tensor"),
            P(None, "tensor"),
            P(None, "tensor"),
            P("tensor"),
            P("tensor", None),
            P(),
            P(),
            P(),
            P(None, "tensor"),
            P("tensor"),
            P("tensor", None),
            P(),
        ),
        check_vma=False,
    )
```

```python
from functools import partial

import jax
import jax.numpy as jnp
from jax import lax
from jax.experimental import pallas as pl
from jax.experimental.pallas import tpu as pltpu
from jax.sharding import PartitionSpec as P

HEADS = 32
EPS = 1e-05
HD = 64
LANES = 128
BIG = 2.0 ** 100
SLOPE_COL = 16
LSE_COL = 24
VMEM_LIMIT = 36 * 1024 * 1024
MATMUL_LIMIT = 26 * 1024 * 1024


def dot_nt(left, right):
    return lax.dot_general(left, right, (((1,), (1,)), ((), ())), preferred_element_type=jnp.float32)


def dot_tn(left, right):
    return lax.dot_general(left, right, (((0,), (0,)), ((), ())), preferred_element_type=jnp.float32)


def dot_nn(left, right):
    return lax.dot_general(left, right, (((1,), (0,)), ((), ())), preferred_element_type=jnp.float32)


def three_parts(value):
    high = value.astype(jnp.bfloat16).astype(jnp.float32)
    rest = value - high
    middle = rest.astype(jnp.bfloat16).astype(jnp.float32)
    return high, middle, rest - middle


def tree_features(lengths, parent_ids, first_head, heads, block, whole):
    nseg = lengths.shape[0]
    seg_ids = jnp.arange(nseg, dtype=jnp.int32)
    ends = jnp.cumsum(lengths, dtype=jnp.int32)
    starts = ends - lengths
    parents = jnp.where(seg_ids > 0, parent_ids, 0)
    own = seg_ids[:, None] == seg_ids[None, :]
    ancestor = own | (parents[:, None] == seg_ids[None, :]) | (seg_ids[None, :] == 0)
    above = (ancestor & ~own).astype(jnp.int32)
    path_start = jnp.sum(above * lengths[None, :], axis=1, dtype=jnp.int32)
    token = jnp.arange(whole, dtype=jnp.int32)[:, None]
    hot = (token >= starts[None, :]) & (token < ends[None, :])
    depth = token + jnp.sum(jnp.where(hot, (path_start - starts)[None, :], 0), axis=1, keepdims=True)
    reach = jnp.sum(jnp.where(hot[:, None, :] & ancestor[None, :, :], 1, 0), axis=2)
    lane = jnp.arange(LANES, dtype=jnp.int32)[None, :]
    pad = ((0, 0), (0, LANES - nseg))
    query_side = jnp.pad(hot.astype(jnp.float32), pad)
    key_side = jnp.pad(jnp.where(reach > 0, 0.0, -BIG), pad)
    digit = lane - SLOPE_COL
    coarse = (depth // 256) * 256
    fine = depth - coarse
    in_slope = (digit >= 0) & (digit < 6)
    key_side = jnp.where(in_slope, jnp.where(digit % 2 == 0, coarse, fine).astype(jnp.float32), key_side)
    key_side = jnp.where((lane >= LSE_COL) & (lane < LSE_COL + 3), 1.0, key_side)
    head_ids = (first_head + jnp.arange(heads, dtype=jnp.int32)).astype(jnp.float32)
    slopes = jnp.exp2(-8.0 * (head_ids + 1.0) / 32)
    parts = jnp.stack(three_parts(slopes), axis=1)
    slope_rows = jnp.pad(jnp.repeat(parts, 2, axis=1), ((0, 0), (SLOPE_COL, LANES - SLOPE_COL - 6)))
    count = whole // block
    held = jnp.max(hot.reshape(count, block, nseg).astype(jnp.float32), axis=1)
    reached = jnp.max(reach.reshape(count, block, nseg).astype(jnp.float32), axis=1)
    ids = jnp.arange(count, dtype=jnp.int32)
    active = (jnp.sum(held[:, None, :] * reached[None, :, :], axis=2) > 0.5) & (ids[None, :] < ids[:, None])

    def packed(flags):
        rank = jnp.cumsum(flags.astype(jnp.int32), axis=1) - 1
        slot = flags[:, :, None] & (rank[:, :, None] == ids[None, None, :])
        listed = jnp.sum(jnp.where(slot, ids[None, :, None], 0), axis=1, dtype=jnp.int32)
        total = jnp.sum(flags.astype(jnp.int32), axis=1, keepdims=True, dtype=jnp.int32)
        return jnp.concatenate([total, listed], axis=1)

    return (
        query_side.astype(jnp.bfloat16),
        key_side.astype(jnp.bfloat16),
        slope_rows.astype(jnp.bfloat16),
        packed(active),
        packed(active.T),
    )


def _masks(block):
    lane = lax.broadcasted_iota(jnp.int32, (block, LANES), 1)
    return [lane < HD, lane >= HD], lane


def forward_kernel(first_block, place, lists, qkv, fq, fk, srow, o, lse, qa, vt, top, acc, *, block, pairs):
    count = qkv.shape[0] // block
    width = pairs * LANES
    heads = 2 * pairs
    halves, lane = _masks(block)
    zero = jnp.zeros((block, LANES), jnp.bfloat16)
    ones = jnp.ones((16, block), jnp.bfloat16)
    row = lax.broadcasted_iota(jnp.int32, (block, block), 0)
    col = lax.broadcasted_iota(jnp.int32, (block, block), 1)
    diagonal = row <= col
    side_blocks = count // 2

    def spot(index):
        return pl.ds(pl.multiple_of(place[index] * block, block), block)

    def canon(index):
        return pl.ds(pl.multiple_of(index * block, block), block)

    def turn(j, _):
        for pair in range(pairs):
            cols = slice(pair * LANES, (pair + 1) * LANES)
            turned = qkv[spot(j), 2 * width + pair * LANES : 2 * width + (pair + 1) * LANES].astype(jnp.float32).T.astype(jnp.bfloat16)
            for side in range(2):
                vt[j, 2 * pair + side] = jnp.concatenate([turned[side * HD : (side + 1) * HD], ones], axis=0)
        return 0

    lax.fori_loop(0, count, turn, 0)

    def step(j, first):
        key_features = fk[canon(j), :]
        keys = [
            jnp.concatenate([qkv[spot(j), width + pair * LANES : width + (pair + 1) * LANES], key_features], axis=1) for pair in range(pairs)
        ]
        scores = [dot_nt(keys[h // 2], qa[h]) for h in range(heads)]
        if first:
            scores = [jnp.where(diagonal, score, -BIG) for score in scores]
        bests = [jnp.max(score, axis=0, keepdims=True) for score in scores]
        if not first:
            olds = [top[h : h + 1, :] for h in range(heads)]
            bests = [jnp.maximum(old, best) for old, best in zip(olds, bests)]
            scales = [jnp.exp(old - best) for old, best in zip(olds, bests)]
        weights = [jnp.exp(score - best).astype(jnp.bfloat16) for score, best in zip(scores, bests)]
        mixed = [dot_nn(vt[j, h], weights[h]) for h in range(heads)]
        for h in range(heads):
            acc[h] = mixed[h] if first else acc[h] * scales[h] + mixed[h]
            top[h : h + 1, :] = bests[h]

    def rows(n, _):
        i = place[first_block[0] + n]
        query_features = fq[canon(i), :]
        for pair in range(pairs):
            cols = slice(pair * LANES, (pair + 1) * LANES)
            queries = qkv[spot(i), cols] * jnp.bfloat16(HD ** -0.5)
            for side in range(2):
                h = 2 * pair + side
                qa[h] = jnp.concatenate(
                    [jnp.where(halves[side], queries, zero), query_features + srow[h : h + 1, :]], axis=1
                )
        step(i, True)

        def other(m, _):
            step(lists[i, m + 1], False)
            return 0

        lax.fori_loop(0, lists[i, 0], other, 0)
        logs = []
        for pair in range(pairs):
            cols = slice(pair * LANES, (pair + 1) * LANES)
            mixed = []
            for h in (2 * pair, 2 * pair + 1):
                total = acc[h, HD : HD + 1, :]
                mixed.append(acc[h, :HD, :] / total)
                logs.append(top[h : h + 1, :] + jnp.log(total))
            o[canon(n), cols] = jnp.concatenate(mixed, axis=0).T.astype(o.dtype)
        logs.append(jnp.zeros((LANES - heads, block), jnp.float32))
        lse[canon(n), :] = jnp.concatenate(logs, axis=0).T
        return 0

    lax.fori_loop(0, o.shape[0] // block, rows, 0)


def backward_kernel(
    place, lists, qkv, do, o_own, o_other, fq, fk, srow, lse_own, lse_other, dqkv, qa, da, dqa, dka, dva, *, block, pairs
):
    count = qkv.shape[0] // block
    width = pairs * LANES
    heads = 2 * pairs
    halves, lane = _masks(block)
    zero = jnp.zeros((block, LANES), jnp.bfloat16)
    row = lax.broadcasted_iota(jnp.int32, (block, block), 0)
    col = lax.broadcasted_iota(jnp.int32, (block, block), 1)
    diagonal = row <= col
    ones = jnp.where(lane < 3, 1.0, 0.0).astype(jnp.bfloat16)
    side_blocks = count // 2

    def spot(index):
        return pl.ds(pl.multiple_of(place[index] * block, block), block)

    def canon(index):
        return pl.ds(pl.multiple_of(index * block, block), block)

    def spread(value, first):
        high, middle, low = three_parts(value)
        spread_out = jnp.where(lane == first, high, 0.0)
        spread_out = jnp.where(lane == first + 1, middle, spread_out)
        return jnp.where(lane == first + 2, low, spread_out).astype(jnp.bfloat16)

    def prepare(i, _):
        query_features = fq[canon(i), :]
        own = place[i] < side_blocks
        mixed_rows = canon(place[i] % side_blocks)
        logs = jnp.where(own, lse_own[mixed_rows, :], lse_other[mixed_rows, :])
        for pair in range(pairs):
            cols = slice(pair * LANES, (pair + 1) * LANES)
            queries = qkv[spot(i), cols] * jnp.bfloat16(HD ** -0.5)
            grads = do[spot(i), cols]
            mixed = jnp.where(own, o_own[mixed_rows, cols], o_other[mixed_rows, cols])
            product = grads.astype(jnp.float32) * mixed.astype(jnp.float32)
            for side in range(2):
                h = 2 * pair + side
                delta = jnp.sum(jnp.where(halves[side], product, 0.0), axis=1, keepdims=True)
                log_total = jnp.sum(jnp.where(lane == h, logs, 0.0), axis=1, keepdims=True)
                features = query_features + srow[h : h + 1, :] + spread(-log_total, LSE_COL)
                qa[h, canon(i), :] = jnp.concatenate([jnp.where(halves[side], queries, zero), features], axis=1)
                da[h, canon(i), :] = jnp.concatenate([jnp.where(halves[side], grads, zero), spread(-delta, 0)], axis=1)
        dqa[i] = jnp.zeros((pairs * LANES, block), jnp.float32)
        return 0

    lax.fori_loop(0, count, prepare, 0)

    def columns(j, _):
        key_features = fk[canon(j), :]
        key_blocks = [qkv[spot(j), width + pair * LANES : width + (pair + 1) * LANES] for pair in range(pairs)]
        keys = [jnp.concatenate([key_block, key_features], axis=1) for key_block in key_blocks]
        values = [
            jnp.concatenate([qkv[spot(j), 2 * width + pair * LANES : 2 * width + (pair + 1) * LANES], ones], axis=1) for pair in range(pairs)
        ]
        turned = [key_block.astype(jnp.float32).T.astype(jnp.bfloat16) for key_block in key_blocks]

        def step(i, first):
            query_rows = [qa[h, canon(i), :] for h in range(heads)]
            grad_rows = [da[h, canon(i), :] for h in range(heads)]
            scores = [dot_nt(keys[h // 2], query_rows[h]) for h in range(heads)]
            slopes = [dot_nt(values[h // 2], grad_rows[h]) for h in range(heads)]
            if first:
                scores = [jnp.where(diagonal, score, -BIG) for score in scores]
            probs = [jnp.exp(score) for score in scores]
            changes = [(prob * slope).astype(jnp.bfloat16) for prob, slope in zip(probs, slopes)]
            probs = [prob.astype(jnp.bfloat16) for prob in probs]
            for pair in range(pairs):
                cols = slice(pair * LANES, (pair + 1) * LANES)
                a, b = 2 * pair, 2 * pair + 1
                value_part = dot_nn(probs[a], grad_rows[a][:, :LANES]) + dot_nn(probs[b], grad_rows[b][:, :LANES])
                key_part = dot_nn(changes[a], query_rows[a][:, :LANES]) + dot_nn(changes[b], query_rows[b][:, :LANES])
                if first:
                    dva[:, cols] = value_part
                    dka[:, cols] = key_part
                else:
                    dva[:, cols] += value_part
                    dka[:, cols] += key_part
                for side in range(2):
                    h = 2 * pair + side
                    part = slice(h * HD, (h + 1) * HD)
                    dqa[i, part, :] += dot_nn(turned[pair][side * HD : (side + 1) * HD], changes[h])

        step(j, True)

        def other(n, _):
            step(lists[j, n + 1], False)
            return 0

        lax.fori_loop(0, lists[j, 0], other, 0)
        dqkv[spot(j), width : 2 * width] = dka[...].astype(dqkv.dtype)
        dqkv[spot(j), 2 * width :] = dva[...].astype(dqkv.dtype)
        return 0

    lax.fori_loop(0, count, columns, 0)

    def finish(i, _):
        dqkv[spot(i), :width] = (dqa[i] * HD ** -0.5).T.astype(dqkv.dtype)
        return 0

    lax.fori_loop(0, count, finish, 0)


def cost(microseconds):
    return pl.CostEstimate(flops=int(microseconds * 1.15e9), bytes_accessed=0, transcendentals=0)


def _attention_call(name, kernel, scalars, arrays, outs, scratch, microseconds):
    vmem = pl.BlockSpec(memory_space=pltpu.VMEM)
    return pl.pallas_call(
        kernel,
        out_shape=outs,
        in_specs=[pl.BlockSpec(memory_space=pltpu.SMEM)] * len(scalars) + [vmem] * len(arrays),
        out_specs=[vmem] * len(outs),
        scratch_shapes=scratch,
        compiler_params=pltpu.CompilerParams(vmem_limit_bytes=VMEM_LIMIT),
        cost_estimate=cost(microseconds),
        name=name,
    )(*scalars, *arrays)


def attention_forward(first_block, count, place, lists, qkv, fq, fk, srow, block):
    whole, width = qkv.shape[0], qkv.shape[1] // 3
    pairs = width // LANES
    return _attention_call(
        "attention_forward",
        partial(forward_kernel, block=block, pairs=pairs),
        (first_block.reshape(1), place, lists),
        (qkv, fq, fk, srow),
        [jax.ShapeDtypeStruct((count * block, width), jnp.bfloat16), jax.ShapeDtypeStruct((count * block, LANES), jnp.float32)],
        [
            pltpu.VMEM((2 * pairs, block, 2 * LANES), jnp.bfloat16),
            pltpu.VMEM((whole // block, 2 * pairs, HD + 16, block), jnp.bfloat16),
            pltpu.VMEM((8, block), jnp.float32),
            pltpu.VMEM((2 * pairs, HD + 16, block), jnp.float32),
        ],
        0,
    )


def attention_backward(place, lists, qkv, do, o, fq, fk, srow, lse, block):
    whole, width = do.shape
    pairs = width // LANES
    return _attention_call(
        "attention_backward",
        partial(backward_kernel, block=block, pairs=pairs),
        (place, lists),
        (qkv, do, *o, fq, fk, srow, *lse),
        [jax.ShapeDtypeStruct((whole, 3 * width), jnp.bfloat16)],
        [
            pltpu.VMEM((2 * pairs, whole, 2 * LANES), jnp.bfloat16),
            pltpu.VMEM((2 * pairs, whole, 2 * LANES), jnp.bfloat16),
            pltpu.VMEM((whole // block, width, block), jnp.float32),
            pltpu.VMEM((block, width), jnp.float32),
            pltpu.VMEM((block, width), jnp.float32),
        ],
        0,
    )[0]


CORE = [(0, 1), (1, 0), (2, 3), (3, 2)]
ACROSS = [(0, 2), (2, 0), (1, 3), (3, 1)]
SWAP = [(0, 1), (1, 0)]
INWARD = [(0, 1), (3, 2)]
MIDDLE = [(1, 2), (2, 1)]
OUTWARD = [(1, 0), (2, 3)]


def low(value):
    return lax.optimization_barrier(value.astype(jnp.bfloat16))


def wide(value):
    return value.astype(jnp.float32)


def core(value):
    return lax.ppermute(value, "tensor", CORE)


def across(value):
    return lax.ppermute(value, "tensor", ACROSS)


def over(value):
    return lax.ppermute(value, "seq", SWAP)


def norm_forward(values, gain, shift):
    center = values - jnp.mean(values, axis=-1, keepdims=True)
    variance = jnp.mean(center * center, axis=-1, keepdims=True)
    inverse = lax.rsqrt(variance + EPS)
    normed = center * inverse
    return (normed * gain + shift, normed, inverse)


def norm_backward(incoming, normed, inverse, gain):
    scaled = incoming * gain
    inner = (
        scaled
        - jnp.mean(scaled, axis=-1, keepdims=True)
        - normed * jnp.mean(scaled * normed, axis=-1, keepdims=True)
    )
    return (inner * inverse, jnp.sum(incoming * normed, axis=0), jnp.sum(incoming, axis=0))


def halves_of(value, axis, which):
    size = value.shape[axis] // 2
    return (
        lax.dynamic_slice_in_dim(value, which * size, size, axis),
        lax.dynamic_slice_in_dim(value, (1 - which) * size, size, axis),
    )


def in_order(own, other, axis, which):
    first = which == 0
    return jnp.concatenate([jnp.where(first, own, other), jnp.where(first, other, own)], axis=axis)


def gather_group(value):
    if lax.axis_size("tensor") == 4:
        beside = core(value)
        far = across(value)
        return (jnp.concatenate([value, beside]), jnp.concatenate([far, core(far)]))
    rows = lax.all_gather(value, "tensor", axis=0, tiled=True)
    return tuple(jnp.split(rows, 2))


def scatter_group(far, near):
    if lax.axis_size("tensor") == 4:
        away = far()
        size = away.shape[0] // 2
        sent = across(low(wide(away[:size]) + wide(core(away[size:]))))
        here = near()
        return wide(here[:size]) + wide(core(here[size:])) + wide(sent)
    away = far()
    here = near()
    return wide(lax.psum_scatter(jnp.concatenate([here, away]), "tensor", scatter_dimension=0, tiled=True))


def gather_slot(value):
    if lax.axis_size("tensor") == 4:
        half = value.shape[0] // 2
        beside = core(value)
        far = across(value)
        past = over(value)
        both = jnp.concatenate([over(far[:half]), across(past[half:])])
        return [jnp.concatenate([piece, other]) for piece, other in
                ((value, beside), (far, core(far)), (past, core(past)), (both, core(both)))]
    own = lax.all_gather(value, "tensor", axis=0, tiled=True)
    return jnp.split(own, 2) + jnp.split(over(own), 2)


def scatter_slot(parts):
    if lax.axis_size("tensor") == 4:
        def chip(part):
            rows = part()
            size = rows.shape[0] // 2
            return wide(rows[:size]) + wide(core(rows[size:]))

        both = low(chip(parts[3]))
        half = both.shape[0] // 2
        both_far = across(both[:half])
        both_past = over(both[half:])
        far = chip(parts[1])
        far_first = across(low(far[:half]))
        past = chip(parts[2])
        past_last = over(low(past[half:]))
        far_last = across(low(far[half:] + wide(both_past)))
        past_first = over(low(past[:half] + wide(both_far)))
        here = chip(parts[0])
        return here + wide(jnp.concatenate([far_first, far_last])) + wide(jnp.concatenate([past_first, past_last]))
    own = lax.psum_scatter(jnp.concatenate([parts[0](), parts[1]()]), "tensor", scatter_dimension=0, tiled=True)
    other = lax.psum_scatter(jnp.concatenate([parts[2](), parts[3]()]), "tensor", scatter_dimension=0, tiled=True)
    return wide(own) + wide(over(other))


def on_line(value, pairs):
    return lax.ppermute(value, "dp", pairs)


def vector_sum(group, pair):
    if lax.axis_size("tensor") == 4 and lax.axis_size("dp") == 4:
        group = group + core(group)
        group = group + across(group)
        rows = jnp.concatenate([group, pair])
        rows = rows + over(rows)
        rows = rows + lax.ppermute(rows, "dp", CORE)
        rows = rows + lax.ppermute(rows, "dp", ACROSS)
        return rows[: group.shape[0]], rows[group.shape[0] :]
    return lax.psum(group, ("dp", "seq", "tensor")), lax.psum(pair, ("dp", "seq"))


def tie(values, after, name):
    count = len(values)
    return pl.pallas_call(
        lambda *refs: None,
        out_shape=[jax.ShapeDtypeStruct(v.shape, v.dtype) for v in values],
        in_specs=[pl.BlockSpec(memory_space=pl.ANY)] * (count + len(after)),
        out_specs=[pl.BlockSpec(memory_space=pl.ANY)] * count,
        input_output_aliases={i: i for i in range(count)},
        compiler_params=pltpu.CompilerParams(vmem_limit_bytes=1 << 16),
        cost_estimate=cost(0),
        name="tie_%d" % name,
    )(*values, *after)


class Order:
    def __init__(self):
        self.after, self.label = [], 999

    def enter(self, *values):
        out = tie(list(values), self.after, self.label)
        self.after = [out[0]]
        return out if len(out) > 1 else out[0]

    def here(self):
        self.token = self.enter(self.token)
        return self.token

    def done(self, *values):
        self.after.extend(values)


def act_gradient(where, pieces, weight, tile=256):
    size, model = pieces[0].shape
    part = weight.shape[0] // 2
    count = len(pieces)
    steps = part // tile

    def kernel(where_ref, *refs):
        weight_ref, out, rows_out = refs[count:]
        block = jnp.concatenate([ref[...] for ref in refs[:count]], axis=0)
        out[...] = dot_nt(block, weight_ref[...]).astype(jnp.bfloat16)

        @pl.when(pl.program_id(0) == 0)
        def _():
            rows_out[...] = block

    return fused(
        "act_gradient", kernel, where, (steps,),
        [(p, p.shape, lambda n, w: (0, 0)) for p in pieces] + [(weight, (tile, model), lambda n, w: (w[0] * steps + n, 0))],
        [
            ((count * size, part), jnp.bfloat16, (count * size, tile), lambda n, w: (0, n)),
            ((count * size, model), jnp.bfloat16, (count * size, model), lambda n, w: (0, 0)),
        ],
    )


def feed_forward(where, pieces, weight, bias, grads, chunk, tile=512):
    size, model = pieces[0].shape
    part = weight.shape[1] // 2
    steps = part // tile
    half = 2 * size

    def kernel(where_ref, first, second, weight_ref, bias_ref, grads_ref, act_ref, up_ref, rows_ref, sums_ref):
        rows = jnp.concatenate([first[...], second[...]], axis=0)
        pre = dot_nn(rows, weight_ref[...]) + wide(bias_ref[...])
        cdf = 0.5 * (1.0 + lax.erf(pre * (0.5**0.5)))
        act_ref[...] = (pre * cdf).astype(jnp.bfloat16)
        slope = cdf + pre * (jnp.exp(-0.5 * pre * pre) * 0.3989422804014327)
        low_grad = (wide(grads_ref[...]) * slope).astype(jnp.bfloat16)
        up_ref[...] = low_grad
        sums_ref[...] = jnp.broadcast_to(jnp.sum(wide(low_grad), axis=0, keepdims=True), sums_ref.shape)

        @pl.when(pl.program_id(0) == 0)
        def _():
            rows_ref[...] = rows

    return fused(
        "feed_forward", kernel, where, (steps,),
        [(p, p.shape, lambda n, w: (0, 0)) for p in pieces]
        + [
            (weight, (model, tile), lambda n, w: (0, w[0] * steps + n)),
            (bias.reshape(1, -1), (1, tile), lambda n, w: (0, w[0] * steps + n)),
            (grads, (half, tile), lambda n, w: (chunk, n)),
        ],
        [
            ((half, part), jnp.bfloat16, (half, tile), lambda n, w: (0, n)),
            ((half, part), jnp.bfloat16, (half, tile), lambda n, w: (0, n)),
            ((half, model), jnp.bfloat16, (half, model), lambda n, w: (0, 0)),
            ((8, part), jnp.float32, (8, tile), lambda n, w: (0, n)),
        ],
    )


def blank(shape):
    return pl.pallas_call(
        lambda out: None,
        out_shape=jax.ShapeDtypeStruct(shape, jnp.float32),
        out_specs=pl.BlockSpec(memory_space=pl.ANY),
        compiler_params=pltpu.CompilerParams(vmem_limit_bytes=1 << 16),
        cost_estimate=cost(0),
        name="blank",
    )()


DOTS = {"nn": dot_nn, "nt": dot_nt, "tn": dot_tn}


def fused(name, kernel, where, grid, operands, outs):
    return pl.pallas_call(
        kernel,
        grid_spec=pltpu.PrefetchScalarGridSpec(
            num_scalar_prefetch=1,
            grid=grid,
            in_specs=[pl.BlockSpec(block, index) for _, block, index in operands],
            out_specs=[pl.BlockSpec(block, index) for _, _, block, index in outs],
        ),
        out_shape=[jax.ShapeDtypeStruct(shape, kind) for shape, kind, _, _ in outs],
        compiler_params=pltpu.CompilerParams(vmem_limit_bytes=MATMUL_LIMIT),
        cost_estimate=cost(0),
        name=name,
    )(where, *[array for array, _, _ in operands])


def matmul(name, kind, where, grid, pairs, outs, axis=0):
    count = len(pairs)

    def kernel(where_ref, *refs):
        total = None
        for left, right in zip(refs[:count], refs[count : 2 * count]):
            part = DOTS[kind](left[...], right[...])
            total = part if total is None else total + part
        start = 0
        for out in refs[2 * count :]:
            size = out.shape[axis]
            piece = total[start : start + size] if axis == 0 else total[:, start : start + size]
            out[...] = piece.astype(jnp.bfloat16)
            start += size

    operands = [left for left, _ in pairs] + [right for _, right in pairs]
    return fused(name, kernel, where, grid, operands, [(shape, jnp.bfloat16, block, index) for shape, block, index in outs])


def plain_local(
    hidden_in, norm1_gain, norm1_bias, query_weight, query_bias, key_weight, value_weight, value_bias, out_weight,
    out_bias, norm2_gain, norm2_bias, up_weight, up_bias, down_weight, down_bias, seg_lengths, parents, out_grad,
):
    local_rows, model = hidden_in.shape
    tensor_count = lax.axis_size("tensor")
    group = local_rows * tensor_count
    whole = 2 * group
    columns = query_weight.shape[1]
    width = columns // 2
    heads = width // HD
    units = up_weight.shape[1]
    seq = lax.axis_index("seq")
    tensor = lax.axis_index("tensor")
    block = 256
    f32 = jnp.float32
    gain_one, gain_two = wide(norm1_gain), wide(norm2_gain)

    inputs = wide(hidden_in)
    first, normed_one, inverse_one = norm_forward(inputs, gain_one, wide(norm1_bias))
    chunks_one = gather_slot(low(first))

    qkv_weight = jnp.concatenate([halves_of(w, 1, seq)[0] for w in (query_weight, key_weight, value_weight)], axis=1)
    qkv_bias = jnp.concatenate(
        [halves_of(query_bias, 0, seq)[0], jnp.zeros((width,), jnp.bfloat16), halves_of(value_bias, 0, seq)[0]]
    )
    out_rel = jnp.concatenate(halves_of(out_weight, 0, seq))
    up_rel = jnp.concatenate(halves_of(up_weight, 1, seq), axis=1)
    up_bias_rel = wide(jnp.concatenate(halves_of(up_bias, 0, seq)))
    down_rel = jnp.concatenate(halves_of(down_weight, 0, seq))

    blocks = jnp.arange(whole // block, dtype=jnp.int32)
    if tensor_count == 4:
        place = blocks ^ (seq * 4 + tensor)
    else:
        side = group // block
        place = ((blocks // side) ^ seq) * side + blocks % side
    fq, fk, slope_rows, key_lists, query_lists = tree_features(
        seg_lengths[0], parents[0], tensor * (columns // HD) + seq * heads, heads, block, whole
    )

    qkv = jnp.concatenate(
        [(jnp.dot(rows, qkv_weight, preferred_element_type=f32) + wide(qkv_bias)).astype(jnp.bfloat16) for rows in chunks_one]
    )
    grad_near, grad_far = gather_group(out_grad)
    side = whole // block // 2
    mixed_other, logs_other = attention_forward(jnp.int32(side), side, place, key_lists, qkv, fq, fk, slope_rows, block)
    mixed_own, logs_own = attention_forward(jnp.int32(0), side, place, key_lists, qkv, fq, fk, slope_rows, block)
    heads_out = jnp.concatenate([mixed_own, over(mixed_other)], axis=1)
    half = group // 2

    def product(left, right):
        return lambda: jnp.dot(left, right, preferred_element_type=f32).astype(jnp.bfloat16)

    def product_nt(left, right):
        return lambda: dot_nt(left, right).astype(jnp.bfloat16)

    def low_dot(left, right):
        return dot_tn(left, right).astype(jnp.bfloat16)

    branch = scatter_group(product(heads_out[half:], out_rel), product(heads_out[:half], out_rel)) + wide(out_bias)
    act_grad_near = low(dot_nt(grad_near, down_rel))
    middle = inputs + branch
    second, normed_two, inverse_two = norm_forward(middle, gain_two, wide(norm2_bias))
    two_near, two_far = gather_group(low(second))
    act_grad_far = low(dot_nt(grad_far, down_rel))
    activated, up_grad = [], []
    for rows, grads in ((two_near, act_grad_near), (two_far, act_grad_far)):
        pre = jnp.dot(rows, up_rel, preferred_element_type=f32) + up_bias_rel
        cdf = 0.5 * (1.0 + lax.erf(pre * (0.5 ** 0.5)))
        activated.append((pre * cdf).astype(jnp.bfloat16))
        slope = cdf + pre * (jnp.exp(-0.5 * pre * pre) * 0.3989422804014327)
        up_grad.append((wide(grads) * slope).astype(jnp.bfloat16))
    act_all = jnp.concatenate(activated)
    up_grad_all = jnp.concatenate(up_grad)
    rows_two = jnp.concatenate([two_near, two_far])
    grad_rows = jnp.concatenate([grad_near, grad_far])
    rows_one = jnp.concatenate(chunks_one)
    part = units // 2
    cotangent = wide(out_grad)

    def down_parts(index):
        cols = slice(index * (model // 2), (index + 1) * (model // 2))
        return low_dot(act_all[:, :part], grad_rows[:, cols]), low_dot(act_all[:, part:], grad_rows[:, cols])

    quarter = model // 4

    def up_parts(index):
        rows = rows_two[:, index * quarter : (index + 1) * quarter]
        return jnp.stack([low_dot(rows, up_grad_all[:, :part]), low_dot(rows, up_grad_all[:, part:])])

    def ffn_sum():
        return scatter_group(product(act_all[half:], down_rel), product(act_all[:half], down_rel)) + wide(down_bias)

    def norm_two(second_grad):
        middle_part, gain_grad, bias_grad = norm_backward(second_grad, normed_two, inverse_two, gain_two)
        return cotangent + middle_part, gain_grad, bias_grad

    def heads_grads(rows):
        return dot_nt(rows, out_rel).astype(jnp.bfloat16)

    def attention_grads(arrived, near_grads):
        return attention_backward(
            place, query_lists, qkv, jnp.concatenate([near_grads, arrived]), (mixed_own, mixed_other),
            fq, fk, slope_rows, (logs_own, logs_other), block,
        )

    def first_grads(grads):
        return scatter_slot([product_nt(grads[i * half : (i + 1) * half], qkv_weight) for i in range(4)])

    def qkv_part(grads, index):
        return low_dot(rows_one, grads[:, index * width : (index + 1) * width])

    second_grad = scatter_group(product_nt(up_grad[1], up_rel), product_nt(up_grad[0], up_rel))
    middle_grad, grad_norm2_gain, grad_norm2_bias = norm_two(second_grad)
    branch_grad = low(middle_grad)
    branch_near, branch_far = gather_group(branch_grad)
    ffn_out = ffn_sum()
    grad_up_bias = jnp.sum(wide(up_grad_all), axis=0)
    heads_grad = jnp.concatenate([heads_grads(branch_near), heads_grads(branch_far)])
    grads = attention_grads(over(heads_grad[:, width:]), heads_grad[:, :width])
    branch_rows = jnp.concatenate([branch_near, branch_far])
    first_grad = first_grads(grads)
    sums = [[*down_parts(0)], [*down_parts(1)], *[[up[0], up[1]] for up in map(up_parts, range(4))]]
    sums.append([low_dot(heads_out[:, :width], branch_rows), low_dot(heads_out[:, width:], branch_rows)])
    axes = [0, 0, 1, 1, 1, 1, 0, 1, 1, 1]
    for i in range(3):
        sums.append([qkv_part(grads, i), jnp.zeros((model, width), jnp.bfloat16)])
    sums = [lax.psum(in_order(own, other, axis, seq), ("dp", "seq")) for (own, other), axis in zip(sums, axes)]

    layer_out = (middle + ffn_out).astype(jnp.bfloat16)
    grad_down_bias = jnp.sum(cotangent, axis=0)
    grad_out_bias = jnp.sum(wide(branch_grad), axis=0)
    bias_sum = jnp.sum(wide(grads), axis=0)
    input_part, grad_norm1_gain, grad_norm1_bias = norm_backward(first_grad, normed_one, inverse_one, gain_one)
    grad_in = (middle_grad + input_part).astype(jnp.bfloat16)

    nothing = jnp.zeros((width,), f32)
    query_bias_row = in_order(bias_sum[:width], nothing, 0, seq)
    value_bias_row = in_order(bias_sum[2 * width :], nothing, 0, seq)
    up_bias_row = in_order(grad_up_bias[:part], grad_up_bias[part:], 0, seq)
    pairs = jnp.concatenate([query_bias_row, value_bias_row, up_bias_row])
    group_rows, pair_rows = vector_sum(
        jnp.stack([grad_norm1_gain, grad_norm1_bias, grad_out_bias, grad_norm2_gain, grad_norm2_bias, grad_down_bias]),
        jnp.pad(pairs, (0, -pairs.shape[0] % model)).reshape(-1, model),
    )
    pair_rows = pair_rows.reshape(-1)

    down = wide(jnp.concatenate(sums[:2], axis=1))
    up = wide(jnp.concatenate(sums[2:6], axis=0))
    out = wide(sums[6])
    qkv_out = [wide(v) for v in sums[7:]]

    return (
        layer_out,
        grad_in,
        group_rows[0],
        group_rows[1],
        qkv_out[0],
        pair_rows[:columns],
        qkv_out[1],
        qkv_out[2],
        pair_rows[columns : 2 * columns],
        out,
        group_rows[2],
        group_rows[3],
        group_rows[4],
        up,
        pair_rows[2 * columns : 2 * columns + units],
        down,
        group_rows[5],
    )


(
    D0, D1, U0, U1, Q0, Q1, Q2, S0, S1, S2, S3, SB, SE, SL, G0, G1, G2, G3, GB, GE, GL, F0, F1, F2, F3, FB, FE, FL, S, G, BN, BF,
    ATT, O, FN, V, d0, d1, u0, u1, q0, q1, q2, o, v,
) = range(45)
D_STEPS, U_STEPS, Q_STEPS = (D0, D1), (U0, U1), (Q0, Q1, Q2)
S_STEPS, G_STEPS, F_STEPS = [S0, S1, S2, S3, SB, SE, SL], [G0, G1, G2, G3, GB, GE, GL], [F0, F1, F2, F3, FB, FE, FL]
D_HOPS, U_HOPS, Q_HOPS, O_HOPS, V_HOPS = (d0, d1), (u0, u1), (q0, q1, q2), o, v
ORDER = (
    S3, U1, SB, S1, S2, SE, SL, D0, S0, u1, S, D1, BN, BF, d0, u1, O, ATT, o, d1, d0, u1, U0, o, d1, d0, u1, u0,
    o, d1, Q2, F3, d0, u0, FB, o, F1, F2, q2, d1, FE, FL, Q0, u0, o, F0, q2, Q1, q0, FN, q1, q0, q2, G3, u0, V,
    q1, q0, v, GB, q2, G1, v, G2, q1, GE, q0, GL, v, G0, q1, v, v, G,
)


def line_steps(mine):
    arrived = yield [on_line(mine, INWARD)], [mine]
    inner = low(wide(mine) + wide(arrived))
    arrived = yield [on_line(inner, MIDDLE)], [inner]
    total = low(wide(inner) + wide(arrived))
    arrived = yield [on_line(total, OUTWARD)], [total]
    line = lax.axis_index("dp")
    total = low(jnp.where((line == 0) | (line == 3), arrived, total))
    arrived = yield [over(total)], [total]
    return total, arrived


def pair_steps(own, other):
    arrived = yield [over(other)], [other, own]
    return (yield from line_steps(low(wide(own) + wide(arrived))))


def vector_steps(group, pair):
    arrived = yield [core(group)], [group]
    group = group + arrived
    arrived = yield [across(group)], [group]
    rows = jnp.concatenate([group + arrived, pair])
    arrived = yield [over(rows)], [rows]
    rows = rows + arrived
    arrived = yield [on_line(rows, CORE)], [rows]
    rows = rows + arrived
    arrived = yield [on_line(rows, ACROSS)], [rows]
    rows = rows + arrived
    return rows[: group.shape[0]], rows[group.shape[0] :]


class Sums:
    def __init__(self, order):
        self.order, self.steps, self.pending, self.results = order, {}, {}, {}

    def start(self, name, steps):
        self.steps[name] = steps
        self.pending[name], sent = next(steps)
        self.order.done(*sent)

    def wait(self, name):
        arrived = self.order.enter(*self.pending[name])
        try:
            self.pending[name], sent = self.steps[name].send(arrived)
            self.order.done(*sent)
        except StopIteration as stop:
            self.results[name] = stop.value


def quick_local(
    hidden_in, norm1_gain, norm1_bias, query_weight, query_bias, key_weight, value_weight, value_bias, out_weight,
    out_bias, norm2_gain, norm2_bias, up_weight, up_bias, down_weight, down_bias, seg_lengths, parents, out_grad,
):
    size, model = hidden_in.shape
    half, group, whole = 2 * size, 4 * size, 8 * size
    columns = query_weight.shape[1]
    width = columns // 2
    heads = width // HD
    units = up_weight.shape[1]
    part = units // 2
    seq, tensor = lax.axis_index("seq"), lax.axis_index("tensor")
    block = size
    f32, bf16 = jnp.float32, jnp.bfloat16
    gain_one, gain_two = wide(norm1_gain), wide(norm2_gain)

    def product(left, right):
        return jnp.dot(left, right, preferred_element_type=f32).astype(bf16)

    def product_nt(left, right):
        return dot_nt(left, right).astype(bf16)

    def whole_block(value):
        return (value, value.shape, lambda n, w: (0, 0))

    order = Order()
    inputs = wide(hidden_in)
    first, normed_one, inverse_one = norm_forward(inputs, gain_one, wide(norm1_bias))
    first = low(first)
    far, past = across(first), over(first)
    order.done(first)
    lengths, parent_ids = order.enter(seg_lengths, parents)
    qkv_weight = jnp.concatenate([halves_of(w, 1, seq)[0] for w in (query_weight, key_weight, value_weight)], axis=1)
    qkv_bias = jnp.concatenate(
        [halves_of(query_bias, 0, seq)[0], jnp.zeros((width,), bf16), halves_of(value_bias, 0, seq)[0]]
    )

    def projected(rows):
        return (jnp.dot(rows, qkv_weight, preferred_element_type=f32) + wide(qkv_bias)).astype(bf16)

    blocks = jnp.arange(whole // block, dtype=jnp.int32)
    place = blocks ^ (seq * 4 + tensor)
    fq, fk, slope_rows, key_lists, query_lists = tree_features(
        lengths[0], parent_ids[0], tensor * (columns // HD) + seq * heads, heads, block, whole
    )
    chunks_one = [jnp.concatenate([first, core(first)])]
    qkv_parts = [projected(chunks_one[0])]
    out_rel = jnp.concatenate(halves_of(out_weight, 0, seq))
    order.done(qkv_parts[0], fk, fq, out_rel)
    far, past = order.enter(far, past)
    both = [over(low(far[: size // 2])), across(low(past[size // 2 :]))]
    for piece in (far, past):
        chunks_one.append(jnp.concatenate([piece, core(piece)]))
        qkv_parts.append(projected(chunks_one[-1]))
        order.done(qkv_parts[-1])
    both = jnp.concatenate(order.enter(*both))
    chunks_one.append(jnp.concatenate([both, core(both)]))
    qkv_parts.append(projected(chunks_one[-1]))
    qkv = jnp.concatenate(qkv_parts)

    order.done(qkv)
    grad_piece = order.enter(out_grad)
    grad_far, grad_past = across(grad_piece), over(grad_piece)
    side = whole // block // 2

    def attend(first_block, count, place_now):
        mixed, logs = attention_forward(jnp.int32(first_block), count, place_now, key_lists, qkv, fq, fk, slope_rows, block)
        order.done(mixed)
        return mixed, logs

    mixed_other, logs_other = attend(side, side, place)
    far_part = attend(side // 2, side - side // 2, order.enter(place))
    mixed_past = over(mixed_other)
    place_now, grad_far, grad_past = order.enter(place, grad_far, grad_past)
    grad_both = [over(low(grad_far[: size // 2])), across(low(grad_past[size // 2 :]))]
    near_part = attend(0, side // 2, place_now)
    mixed_own, logs_own = (jnp.concatenate(pair) for pair in zip(near_part, far_part))
    mixed_past, *grad_both = order.enter(mixed_past, *grad_both)
    heads_out = jnp.concatenate([mixed_own, mixed_past], axis=1)
    branch_far = product(heads_out[half:], out_rel)
    branch_sent = low(wide(branch_far[:size]) + wide(core(branch_far[size:])))
    branch_back = across(branch_sent)
    branch_near = product(heads_out[:half], out_rel)
    order.done(branch_near, branch_sent)

    where = seq.reshape(1)
    grad_far = order.enter(grad_far)
    pieces = [grad_piece, core(grad_piece), grad_far, core(grad_far)]
    act_grad, grad_rows = ([v] for v in act_gradient(where, pieces, down_weight))
    order.done(act_grad[0])
    branch_back = order.enter(branch_back)
    branch = wide(branch_near[:size]) + wide(core(branch_near[size:])) + wide(branch_back)
    middle = inputs + branch + wide(out_bias)
    second, normed_two, inverse_two = norm_forward(middle, gain_two, wide(norm2_bias))
    second = low(second)
    second_core, second_far, second_past = core(second), across(second), over(second)
    order.done(second)
    act, up_grad, rows_two, up_sums = [], [], [], []

    def feed(pieces, chunk):
        out = feed_forward(where, pieces, up_weight, up_bias, act_grad[chunk // 2], chunk % 2)
        for held, value in zip((act, up_grad, rows_two, up_sums), out):
            held.append(value)
        order.done(out[0])

    second_core = order.enter(second_core)
    feed((second, second_core), 0)
    grad_both = jnp.concatenate(grad_both)
    pieces = [grad_past, core(grad_past), grad_both, core(grad_both)]
    for held, value in zip((act_grad, grad_rows), act_gradient(where, pieces, down_weight)):
        held.append(value)
    order.done(act_grad[1])
    second_far, second_past = order.enter(second_far, second_past)
    second_both = [over(low(second_far[: size // 2])), across(low(second_past[size // 2 :]))]
    feed((second_far, core(second_far)), 1)
    feed((second_past, core(second_past)), 2)
    second_both = jnp.concatenate(order.enter(*second_both))
    feed((second_both, core(second_both)), 3)
    cotangent = wide(out_grad)

    sums = Sums(order)
    order.token = where
    state = {}
    order.done(*act, *up_grad)

    parts = 2
    cols = model // parts

    def start_down(index):
        pairs = [
            (
                (act[c], (half, part // 2), lambda m, w: (0, m)),
                (grad_rows[c // 2], (half, cols), lambda m, w, c=c: (c % 2, index)),
            )
            for c in range(4)
        ]
        out = ((part, cols), (part // 2, cols), lambda m, w: (m, 0))
        sums.start(D_HOPS[index], line_steps(*matmul("down_part", "tn", order.here(), (2,), pairs, [out])))

    def start_up(index):
        pairs = [
            (
                (rows_two[c], (half, cols // 2), lambda m, w: (0, 2 * index + m)),
                (up_grad[c], (half, part), lambda m, w: (0, 0)),
            )
            for c in range(4)
        ]
        out = ((cols, part), (cols // 2, part), lambda m, w: (m, 0))
        sums.start(U_HOPS[index], line_steps(*matmul("up_part", "tn", order.here(), (2,), pairs, [out])))

    def scatter_steps(name, kind, source, right, tile):
        def rows(chunk):
            own, other = matmul(
                name, kind, order.here(), (model // tile,), [(source(chunk), right)],
                [((size, model), (size, tile), lambda n, w: (0, n))] * 2,
            )
            state[name, chunk] = own, core(other)
            order.done(own)

        def total(chunk):
            own, other = state[name, chunk]
            return wide(own) + wide(other)

        def send(key, transfer, value):
            sent = low(value)
            state[name, key] = transfer(sent)
            order.done(sent)

        def both():
            send("both", across, total(3))

        def far():
            send("far", across, total(1))

        def past():
            send("past", over, total(2) + wide(order.enter(state[name, "both"])))

        def own_rows():
            far, past = order.enter(state[name, "far"], state[name, "past"])
            return total(0) + wide(far) + wide(past)

        return [partial(rows, i) for i in range(4)] + [both, far, past], own_rows

    tile = 512

    def second_norm():
        incoming = second_rows()
        inner, gain_grad, bias_grad = norm_backward(incoming, normed_two, inverse_two, gain_two)
        middle_grad = cotangent + inner
        branch_grad = low(middle_grad)
        state["middle_grad"], state["norm2"] = middle_grad, (gain_grad, bias_grad)
        state["dy"] = [branch_grad, core(branch_grad)]
        state["dy_back"] = across(branch_grad)
        order.done(branch_grad)

    def heads_rows(pieces):
        rows = jnp.concatenate(pieces)
        return matmul(
            "heads_gradient", "nt", order.here(), (1,),
            [(whole_block(rows), whole_block(out_rel))],
            [((half, width), (half, width), lambda n, w: (0, 0))] * 2, 1,
        )

    def heads_near():
        state["do_near"] = heads_rows(state["dy"])
        order.done(state["do_near"][0])

    def heads_far():
        back = order.enter(state["dy_back"])
        state["dy"] += [back, core(back)]
        far = heads_rows(state["dy"][2:])
        state["do_own"], sent = (low(jnp.concatenate(pair)) for pair in zip(state["do_near"], far))
        state["do_past"] = over(sent)
        order.done(state["do_own"], sent)

    def attention():
        rows_one = jnp.concatenate(order.enter(*chunks_one))
        state["rows_one"] = rows_one
        order.done(rows_one)
        rows = jnp.concatenate([state["do_own"], order.enter(state["do_past"])])
        state["grads"] = attention_backward(
            place, query_lists, qkv, rows, (mixed_own, mixed_other), fq, fk, slope_rows, (logs_own, logs_other), block
        )
        order.done(state["grads"])

    def layer_end():
        state["layer_out"] = (middle + ffn_rows() + wide(down_bias)).astype(bf16)
        order.done(state["layer_out"])

    def start_out():
        rows = jnp.concatenate(state["dy"])
        here = order.here()
        halves = [
            matmul(
                "out_part", "tn", here, (2,),
                [(whole_block(v), (rows, (group, model // 2), lambda n, w: (0, n)))],
                [((width, model), (width, model // 2), lambda n, w: (0, n))],
            )[0]
            for v in (mixed_own, mixed_past)
        ]
        sums.start(O_HOPS, pair_steps(*halves))

    def first_norm():
        incoming = first_rows()
        inner, gain_grad, bias_grad = norm_backward(incoming, normed_one, inverse_one, gain_one)
        state["grad_in"] = (state["middle_grad"] + inner).astype(bf16)
        state["norm1"] = gain_grad, bias_grad
        order.done(state["grad_in"])

    def start_qkv(index):
        grads = state["grads"]
        size_of = 3 * width // projection_parts
        (value,) = matmul(
            "projection_part", "tn", order.here(), (4,),
            [((state["rows_one"], (whole, model // 4), lambda m, w: (0, m)), (grads, (whole, size_of), lambda m, w: (0, index)))],
            [((model, size_of), (model // 4, size_of), lambda m, w: (m, 0))],
        )
        sums.start(Q_HOPS[index], line_steps(value))

    projection_parts = sum(step in ORDER for step in Q_STEPS)
    second_steps, second_rows = scatter_steps(
        "second_gradient", "nt", lambda c: whole_block(up_grad[c]), (up_weight, (tile, part), lambda n, w: (n, w[0])), tile
    )
    ffn_steps, ffn_rows = scatter_steps(
        "feed_back", "nn", lambda c: whole_block(act[c]), (down_weight, (part, tile), lambda n, w: (w[0], n)), tile
    )
    first_steps, first_rows = scatter_steps(
        "first_gradient", "nt", lambda c: (state["grads"], (half, 3 * width), lambda n, w: (c, 0)), (qkv_weight, (2 * tile, 3 * width), lambda n, w: (n, 0)), 2 * tile
    )
    def start_vectors():
        bias_sum = jnp.sum(wide(state["grads"]), axis=0)
        nothing = jnp.zeros((width,), f32)
        pairs = jnp.concatenate(
            [
                in_order(bias_sum[:width], nothing, 0, seq),
                in_order(bias_sum[2 * width :], nothing, 0, seq),
                in_order(sum(s[0] for s in up_sums), jnp.zeros((part,), f32), 0, seq),
            ]
        )
        grad_out_bias = jnp.sum(wide(state["dy"][0]), axis=0)
        grad_down_bias = jnp.sum(cotangent, axis=0)
        group_rows = jnp.stack([*state["norm1"], grad_out_bias, *state["norm2"], grad_down_bias])
        sums.start(V_HOPS, vector_steps(group_rows, jnp.pad(pairs, (0, -pairs.shape[0] % model)).reshape(-1, model)))

    steps = dict(zip(S_STEPS + G_STEPS + F_STEPS, second_steps + ffn_steps + first_steps))
    steps |= {S: second_norm, G: layer_end, BN: heads_near, BF: heads_far, ATT: attention, O: start_out, FN: first_norm, V: start_vectors}
    for i in range(3):
        steps[Q_STEPS[i]] = partial(start_qkv, i)
    for i in range(parts):
        steps[D_STEPS[i]], steps[U_STEPS[i]] = partial(start_down, i), partial(start_up, i)
    for step in ORDER:
        order.label = step
        if step in steps:
            steps[step]()
        else:
            sums.wait(step)

    group_rows, pair_rows = sums.results[V_HOPS]
    pair_rows = pair_rows.reshape(-1)

    def put(out, value, row, column):
        return lax.dynamic_update_slice(out, wide(value), (row, column))

    up, down = blank((model, units)), blank((units, model))
    for i in range(parts):
        own, other = sums.results[U_HOPS[i]]
        up = put(put(up, own, i * cols, seq * part), other, i * cols, (1 - seq) * part)
        own, other = sums.results[D_HOPS[i]]
        down = put(put(down, own, seq * part, i * cols), other, (1 - seq) * part, i * cols)
    out = blank((columns, model))
    own, other = sums.results[O_HOPS]
    out = put(put(out, own, seq * width, 0), other, (1 - seq) * width, 0)
    own, other = (
        jnp.concatenate([sums.results[Q_HOPS[i]][j] for i in range(projection_parts)], axis=1) for j in range(2)
    )
    projections = []
    for i in range(3):
        cols = slice(i * width, (i + 1) * width)
        projection = put(blank((model, columns)), own[:, cols], 0, seq * width)
        projections.append(put(projection, other[:, cols], 0, (1 - seq) * width))
    return (
        state["layer_out"],
        state["grad_in"],
        group_rows[0],
        group_rows[1],
        projections[0],
        pair_rows[:columns],
        projections[1],
        projections[2],
        pair_rows[columns : 2 * columns],
        out,
        group_rows[2],
        group_rows[3],
        group_rows[4],
        up,
        pair_rows[2 * columns : 2 * columns + units],
        down,
        group_rows[5],
    )


def local(*args):
    quick = lax.axis_size("tensor") == 4 and lax.axis_size("dp") == 4 and args[0].shape[0] == 256
    return quick_local(*args) if quick else plain_local(*args)


def solution(mesh):
    placed = (
        P(("dp", "seq", "tensor"), None),
        P(),
        P(),
        P(None, "tensor"),
        P("tensor"),
        P(None, "tensor"),
        P(None, "tensor"),
        P("tensor"),
        P("tensor", None),
        P(),
        P(),
        P(),
        P(None, "tensor"),
        P("tensor"),
        P("tensor", None),
        P(),
        P("dp", None),
        P("dp", None),
        P(("dp", "seq", "tensor"), None),
    )
    return jax.shard_map(
        local,
        mesh=mesh,
        in_specs=placed,
        out_specs=(
            P(("dp", "seq", "tensor"), None),
            P(("dp", "seq", "tensor"), None),
            P(),
            P(),
            P(None, "tensor"),
            P("tensor"),
            P(None, "tensor"),
            P(None, "tensor"),
            P("tensor"),
            P("tensor", None),
            P(),
            P(),
            P(),
            P(None, "tensor"),
            P("tensor"),
            P("tensor", None),
            P(),
        ),
        check_vma=False,
    )
```
